256 devices in a mesh: gx: 32 (over z, y), gy: 8 (over x, core).
Axes of the slice: x: 4, y: 4, z: 8, core: 2. Of those that a mesh axis runs over, the one named last changes fastest.
Arguments:
- right_side: float32 [512, 512, 512], P('gx', 'gy'), may hold values from -8 to 8
- guess: float32 [512, 512, 512], P('gx', 'gy'), may hold values from -4 to 4
- diagonal: float32 [512, 512, 512], P('gx', 'gy'), may hold values from 0.02 to 0.5
Outputs:
- solution_field: float32 [512, 512, 512], P('gx', 'gy')
- residual: float32 [512, 512, 512], P('gx', 'gy')
The draws below stay inside these ranges and needn't reach their ends.
All inputs are finite; a program needn't handle non-finite values.
Results may differ from the reference program's by a relative error of at most 0.00065.
Values sent between devices are 32-bit elements; how exact they have to be, the bound alone decides.
No kernel may reach another device: no remote copies, remote signals or barrier semaphores. Data moves between devices by JAX's collectives and lax.ppermute only.
A program may use at most 128 MiB of HBM per device.

```python
import math
import jax
import jax.numpy as jnp
from jax import lax

NZ = 512
STEPS = 4
NX = 512
NY = 512


def level_of(rng, extent, cuts, smallest, largest):
    def one(position, parts):
        draws = jax.random.uniform(jax.random.fold_in(jax.random.fold_in(rng, 6), position), (parts,), jnp.float32, smallest / len(cuts), largest / len(cuts))
        return jnp.repeat(jnp.exp(draws), extent[position] // parts).reshape((-1,) + (1,) * (len(extent) - position - 1))

    gain = one(*cuts[0])
    for cut in cuts[1:]:
        gain = gain * one(*cut)
    return gain


def normal_values(own_key, dims, deviation, reach, cuts=(), held_as=jnp.bfloat16):
    drawn = jax.random.normal(own_key, dims, jnp.float32) * deviation
    if len(cuts) > 0:
        drawn = level_of(own_key, dims, cuts, -0.22, 0.18) * drawn
    return jnp.clip(drawn, min=-reach, max=reach).astype(held_as)


def setup_inputs(seed: int = 0) -> dict:
    splits = jax.random.split(jax.random.key(seed), 4)
    return {
        "right_side": normal_values(splits[0], (NX, NY, NZ), 1.0, 8.0, ((0, 32), (1, 8)), jnp.float32),
        "guess": normal_values(splits[1], (NX, NY, NZ), 0.5, 4.0, ((0, 32), (1, 8)), jnp.float32),
        "diagonal": jnp.clip(jnp.exp(math.log(0.5) - 3.218876 * jax.random.uniform(splits[2], (NX, NY, NZ), jnp.float32) ** level_of(splits[2], (NX, NY, NZ), ((0, 32), (1, 8)), -0.2, 0.2)), 0.02, 0.5),
    }


center_shift = 6.25
half_range = 6.25


def operate(field, diagonal):
    padded = jnp.pad(field, 1)
    beside = padded[2:, 1:-1, 1:-1] + padded[:-2, 1:-1, 1:-1]
    beside = beside + padded[1:-1, 2:, 1:-1] + padded[1:-1, :-2, 1:-1]
    beside = beside + padded[1:-1, 1:-1, 2:] + padded[1:-1, 1:-1, :-2]
    return (6.0 + diagonal) * field - beside


def change_matrix(depth):
    rows = []
    for i in range(depth + 1):
        line = []
        for k in range(depth + 1):
            value = 0.0
            if k == 0:
                value = center_shift if i == 0 else (half_range if i == 1 else 0.0)
            elif k < depth:
                if i == k:
                    value = center_shift
                elif i == k - 1 or i == k + 1:
                    value = half_range / 2.0
            line.append(value)
        rows.append(line)
    return jnp.array(rows, dtype=jnp.float32)


def quad(left, matrix, right):
    return jnp.sum(left * jnp.dot(matrix, right, precision=lax.Precision.HIGHEST))


def coefficient_steps(gram, depth):
    change = change_matrix(depth)
    unit = jnp.zeros((depth + 1,), jnp.float32).at[0].set(1.0)
    xc = jnp.zeros((depth + 1,), jnp.float32)
    rc = unit
    pc = unit
    for step in range(depth):
        rr = quad(rc, gram, rc)
        moved = jnp.dot(change, pc, precision=lax.Precision.HIGHEST)
        alpha = rr / quad(pc, gram, moved)
        xc = xc + alpha * pc
        rc = rc - alpha * moved
        beta = quad(rc, gram, rc) / rr
        pc = rc + beta * pc
    return xc, rc


def reference(right_side, guess, diagonal):
    first = right_side - operate(guess, diagonal)
    basis = [first]
    for k in range(STEPS):
        applied = operate(basis[k], diagonal)
        if k == 0:
            nextone = (applied - center_shift * basis[k]) / half_range
        else:
            nextone = 2.0 * (applied - center_shift * basis[k]) / half_range - basis[k - 1]
        basis.append(nextone)
    stacked = jnp.stack(basis).reshape(STEPS + 1, -1)
    gram = jnp.dot(stacked, stacked.T, precision=lax.Precision.HIGHEST)
    xc, rc = coefficient_steps(gram, STEPS)
    solution_field = guess
    residual = jnp.zeros_like(guess)
    for k in range(STEPS + 1):
        solution_field = solution_field + xc[k] * basis[k]
        residual = residual + rc[k] * basis[k]
    return solution_field, residual
```

```python
import functools

import jax
import jax.numpy as jnp
from jax import lax
from jax.experimental import pallas as pl
from jax.experimental.pallas import tpu as pltpu
from jax.sharding import PartitionSpec as P

STEPS = 4
SUB, LANE = 8, 128
center_shift = 6.25
half_range = 6.25
VMEM_LIMIT = 40 * 1024 * 1024

vmem = pl.BlockSpec(memory_space=pltpu.VMEM)


def f32(*shape):
    return jax.ShapeDtypeStruct(shape, jnp.float32)


def call(body, outs, *args, alias=None, flops=0):
    size = sum(a.size * 4 for a in args) + sum(o.size * 4 for o in outs)
    return pl.pallas_call(
        body,
        out_shape=outs,
        in_specs=[vmem] * len(args),
        out_specs=[vmem] * len(outs),
        input_output_aliases=alias or {},
        compiler_params=pltpu.CompilerParams(vmem_limit_bytes=VMEM_LIMIT),
        cost_estimate=pl.CostEstimate(
            flops=flops, bytes_accessed=size, transcendentals=0
        ),
    )(*args)


def faces_body(t_ref, xlow, xhigh, ylow, yhigh):
    nx, ny, _ = t_ref.shape
    xlow[...] = t_ref[0:1]
    xhigh[...] = t_ref[nx - 1 : nx]
    for i in range(nx):
        ylow[i : i + 1, :] = t_ref[i, 0:1, :]
        yhigh[i : i + 1, :] = t_ref[i, ny - 1 : ny, :]


def face_shapes(t):
    nx, ny, nz = t.shape
    return [f32(1, ny, nz), f32(1, ny, nz), f32(nx, nz), f32(nx, nz)]


def tiles(shape):
    return shape[1] // SUB, shape[2] // LANE


def layer(t_ref, i, below, above, emit, carry):
    rows, cols = tiles(t_ref.shape)
    sub = lax.broadcasted_iota(jnp.int32, (SUB, LANE), 0)
    lane = lax.broadcasted_iota(jnp.int32, (SUB, LANE), 1)
    first_sub, last_sub = sub == 0, sub == SUB - 1
    first_lane, last_lane = lane == 0, lane == LANE - 1

    def load(j, c, di=0):
        return t_ref[i + di, pl.ds(j * SUB, SUB), pl.ds(c * LANE, LANE)]

    zero = jnp.zeros((SUB, LANE), jnp.float32)
    now = [load(0, c) for c in range(cols)]
    fromlow = [zero] * cols
    for j in range(rows):
        after = [load(j + 1, c) for c in range(cols)] if j + 1 < rows else None
        right = [pltpu.roll(v, 1, 1) for v in now]
        left = [pltpu.roll(v, LANE - 1, 1) for v in now]
        down = [pltpu.roll(v, 1, 0) for v in now]
        for c in range(cols):
            up = pltpu.roll(now[c], SUB - 1, 0)
            nextup = pltpu.roll(after[c], SUB - 1, 0) if after is not None else zero
            s = jnp.where(first_sub, fromlow[c], down[c])
            s = s + jnp.where(last_sub, nextup, up)
            s = s + jnp.where(first_lane, right[c - 1] if c > 0 else zero, right[c])
            s = s + jnp.where(last_lane, left[c + 1] if c + 1 < cols else zero, left[c])
            if below:
                s = s + load(j, c, -1)
            if above:
                s = s + load(j, c, 1)
            carry = emit(i, j, c, now[c], s, carry)
        fromlow = down
        now = after
    return carry


def sweep(t_ref, emit, carry):
    nx = t_ref.shape[0]
    carry = layer(t_ref, 0, False, True, emit, carry)
    carry = lax.fori_loop(
        1, nx - 1, lambda i, a: layer(t_ref, i, True, True, emit, a), carry
    )
    return layer(t_ref, nx - 1, True, False, emit, carry)


def at(j, c):
    return pl.ds(j * SUB, SUB), pl.ds(c * LANE, LANE)


def first_body(guess, right_side, diagonal, out):
    def emit(i, j, c, mid, beside, carry):
        d = diagonal[(i, *at(j, c))]
        applied = (6.0 + d) * mid - beside
        out[(i, *at(j, c))] = right_side[(i, *at(j, c))] - applied
        return carry

    sweep(guess, emit, 0)


def next_body(index, last, *refs):
    if index == 0:
        current, diagonal, out, sums = refs
    else:
        current, previous, diagonal, out, sums = refs
    scale = 1.0 / half_range if index == 0 else 2.0 / half_range
    zero = jnp.zeros((SUB, LANE), jnp.float32)
    count = sums.shape[0]

    def emit(i, j, c, mid, beside, carry):
        place = (i, *at(j, c))
        d = diagonal[place]
        value = scale * ((d + (6.0 - center_shift)) * mid - beside)
        added = [mid * mid]
        if index > 0:
            before = previous[place]
            value = value - before
            added.append(mid * before)
        if last:
            added += [mid * value, value * value]
        out[place] = value
        return tuple(a + b for a, b in zip(carry, added))

    total = sweep(current, emit, (zero,) * count)
    for n in range(count):
        sums[n] = total[n]


def fix_rows(scales, t_ref, xlow, xhigh, ylow, yhigh, visit):
    nx = t_ref.shape[0]
    rows, cols = tiles(t_ref.shape)
    sub = lax.broadcasted_iota(jnp.int32, (SUB, LANE), 0)
    sxl, sxh, syl, syh = scales

    def one(i, inner):
        for j in range(rows):
            edge_j = j == 0 or j == rows - 1
            if inner and not edge_j:
                continue
            for c in range(cols):
                place = (i, *at(j, c))
                old = t_ref[place]
                new = old
                if not inner and i == 0:
                    new = new + sxl * xlow[(0, *at(j, c))]
                if not inner and i == nx - 1:
                    new = new + sxh * xhigh[(0, *at(j, c))]
                if j == 0:
                    line = ylow[pl.ds(i, 1), pl.ds(c * LANE, LANE)]
                    new = new + jnp.where(sub == 0, syl * line, 0.0)
                if j == rows - 1:
                    line = yhigh[pl.ds(i, 1), pl.ds(c * LANE, LANE)]
                    new = new + jnp.where(sub == SUB - 1, syh * line, 0.0)
                visit(i, j, c, place, old, new)

    for i in range(nx):
        one(i, 0 < i < nx - 1)


def edge_scales(scale_ref):
    return tuple(scale_ref[n] for n in range(4))


def fix_body(scale_ref, t_in, xlow, xhigh, ylow, yhigh, t, fx0, fx1, fy0, fy1):
    nx = t_in.shape[0]
    rows, _ = tiles(t_in.shape)

    def visit(i, j, c, place, old, new):
        t[place] = new
        lanes = pl.ds(c * LANE, LANE)
        if i == 0:
            fx0[(0, *at(j, c))] = new
        if i == nx - 1:
            fx1[(0, *at(j, c))] = new
        if j == 0:
            fy0[pl.ds(i, 1), lanes] = new[0:1, :]
        if j == rows - 1:
            fy1[pl.ds(i, 1), lanes] = new[SUB - 1 : SUB, :]

    fix_rows(edge_scales(scale_ref), t_in, xlow, xhigh, ylow, yhigh, visit)


def close_body(scale_ref, t_in, before, xlow, xhigh, ylow, yhigh, s0, s1, s2, s3, t, out):
    acc = [s3[2], s3[3]]

    def visit(i, j, c, place, old, new):
        t[place] = new
        acc[0] = acc[0] + before[place] * (new - old)
        acc[1] = acc[1] + (new * new - old * old)

    fix_rows(edge_scales(scale_ref), t_in, xlow, xhigh, ylow, yhigh, visit)
    parts = [s0[0], s1[1], s1[0], s2[1], s2[0], s3[1], s3[0], acc[0], acc[1]]
    lane = lax.broadcasted_iota(jnp.int32, (SUB, LANE), 1)
    packed = jnp.zeros((SUB, LANE), jnp.float32)
    for n, part in enumerate(parts):
        total = jnp.sum(part, axis=1, keepdims=True)
        packed = jnp.where(lane == n, total, packed)
    packed = jnp.sum(packed, axis=0, keepdims=True)
    out[...] = jnp.broadcast_to(packed, out.shape)


def coefficients(q):
    depth = STEPS
    moment = [None] * (2 * depth + 1)
    moment[0], moment[1] = q[0], q[1]
    for n in range(2, 2 * depth + 1):
        moment[n] = 2.0 * q[n] - moment[n % 2]
    gram = [
        [
            q[i + j] if abs(i - j) < 2 else 0.5 * (moment[i + j] + moment[abs(i - j)])
            for j in range(depth + 1)
        ]
        for i in range(depth + 1)
    ]

    def plus(a, b):
        return b if a is None else a if b is None else a + b

    def times(a, b):
        return None if a is None or b is None else a * b

    def change(v):
        moved = [None] * (depth + 1)
        for k in range(depth):
            if k == 0:
                entries = {0: center_shift, 1: half_range}
            else:
                entries = {
                    k - 1: half_range / 2.0,
                    k: center_shift,
                    k + 1: half_range / 2.0,
                }
            for i, value in entries.items():
                moved[i] = plus(moved[i], times(value, v[k]))
        return moved

    def quad(left, right):
        total = None
        for i in range(depth + 1):
            inner = None
            for j in range(depth + 1):
                inner = plus(inner, times(gram[i][j], right[j]))
            total = plus(total, times(left[i], inner))
        return total

    one = jnp.ones_like(q[0])
    xc = [None] * (depth + 1)
    rc = [one] + [None] * depth
    pc = [one] + [None] * depth
    rr = quad(rc, rc)
    for _ in range(depth):
        moved = change(pc)
        alpha = rr / quad(pc, moved)
        xc = [plus(x, times(alpha, p)) for x, p in zip(xc, pc)]
        rc = [plus(r, times(-alpha, m)) for r, m in zip(rc, moved)]
        following = quad(rc, rc)
        beta = following / rr
        pc = [plus(r, times(beta, p)) for r, p in zip(rc, pc)]
        rr = following
    return xc, rc


CHUNK = 2


def final_body(sums, guess, t0, t1, t2, t3, t4, sol_hbm, res_hbm, sol, res, sems):
    nx = t0.shape[0]
    rows, cols = tiles(t0.shape)
    packed = sums[0:SUB, :]
    for n in range(1, sums.shape[0] // SUB):
        packed = packed + sums[n * SUB : (n + 1) * SUB, :]
    packed = jnp.sum(packed, axis=0, keepdims=True)
    q = [
        jnp.broadcast_to(packed[:, n : n + 1], (SUB, LANE))
        for n in range(2 * STEPS + 1)
    ]
    xc, rc = coefficients(q)
    basis = [t0, t1, t2, t3, t4]
    steps = nx // CHUNK

    def copies(step):
        block = pl.ds(step * CHUNK, CHUNK)
        return (
            pltpu.make_async_copy(sol.at[block], sol_hbm.at[block], sems.at[0, step]),
            pltpu.make_async_copy(res.at[block], res_hbm.at[block], sems.at[1, step]),
        )

    def step_body(step, carry):
        for u in range(CHUNK):
            i = step * CHUNK + u
            for j in range(rows):
                for c in range(cols):
                    place = (i, *at(j, c))
                    values = [b[place] for b in basis]
                    x, r = guess[place], None
                    for k in range(STEPS + 1):
                        if xc[k] is not None:
                            x = x + xc[k] * values[k]
                        term = rc[k] * values[k]
                        r = term if r is None else r + term
                    sol[place] = x
                    res[place] = r
        for copy in copies(step):
            copy.start()
        return carry

    lax.fori_loop(0, steps, step_body, 0)

    def wait_body(step, carry):
        for copy in copies(step):
            copy.wait()
        return carry

    lax.fori_loop(0, steps, wait_body, 0)


def exchange(faces):
    xlow, xhigh, ylow, yhigh = faces
    nx, ny = lax.axis_size("gx"), lax.axis_size("gy")
    up_x = [(i, (i + 1) % nx) for i in range(nx)]
    up_y = [(i, (i + 1) % ny) for i in range(ny)]
    return (
        lax.ppermute(xhigh, "gx", up_x),
        lax.ppermute(xlow, "gx", [(b, a) for a, b in up_x]),
        lax.ppermute(yhigh, "gy", up_y),
        lax.ppermute(ylow, "gy", [(b, a) for a, b in up_y]),
    )


def all_sum(rows):
    parts = lax.all_to_all(rows[:, None, :], ("gx", "gy"), 0, 0)
    return parts[:, 0, :]


def fix(scales, t, halo):
    specs = [pl.BlockSpec(memory_space=pltpu.SMEM)] + [vmem] * 5
    outs = [f32(*t.shape)] + face_shapes(t)
    t, *faces = pl.pallas_call(
        fix_body,
        out_shape=outs,
        in_specs=specs,
        out_specs=[vmem] * 5,
        input_output_aliases={1: 0},
        compiler_params=pltpu.CompilerParams(vmem_limit_bytes=VMEM_LIMIT),
        cost_estimate=pl.CostEstimate(
            flops=t.size // 4, bytes_accessed=t.size, transcendentals=0
        ),
    )(scales, t, *halo)
    return t, faces


def shards(right_side, guess, diagonal):
    gx, gy = lax.axis_index("gx"), lax.axis_index("gy")
    nx, ny = lax.axis_size("gx"), lax.axis_size("gy")
    inside = jnp.stack([gx > 0, gx < nx - 1, gy > 0, gy < ny - 1]).astype(jnp.float32)
    size = guess.size
    faces = call(faces_body, face_shapes(guess), guess)
    halo = exchange(faces)
    (t,) = call(
        first_body, [f32(*guess.shape)], guess, right_side, diagonal, flops=20 * size
    )
    t, faces = fix(inside, t, halo)
    basis, sums = [t], []
    for k in range(STEPS):
        halo = exchange(faces)
        last = k == STEPS - 1
        count = 1 if k == 0 else 4 if last else 2
        given = [basis[k], diagonal] if k == 0 else [basis[k], basis[k - 1], diagonal]
        t, s = call(
            functools.partial(next_body, k, last),
            [f32(*guess.shape), f32(count, SUB, LANE)],
            *given,
            flops=24 * size,
        )
        sums.append(s)
        scales = inside * (-1.0 / half_range if k == 0 else -2.0 / half_range)
        if not last:
            t, faces = fix(scales, t, halo)
            basis.append(t)
    devices = nx * ny
    t4, rows = pl.pallas_call(
        close_body,
        out_shape=[f32(*guess.shape), f32(devices, LANE)],
        in_specs=[pl.BlockSpec(memory_space=pltpu.SMEM)] + [vmem] * 10,
        out_specs=[vmem] * 2,
        input_output_aliases={1: 0},
        compiler_params=pltpu.CompilerParams(vmem_limit_bytes=VMEM_LIMIT),
    )(scales, t, basis[3], *halo, *sums)
    summed = all_sum(rows)
    block = guess.shape
    return pl.pallas_call(
        final_body,
        out_shape=[f32(*block), f32(*block)],
        in_specs=[vmem] * 7,
        out_specs=[pl.BlockSpec(memory_space=pl.ANY)] * 2,
        scratch_shapes=[
            pltpu.VMEM(block, jnp.float32),
            pltpu.VMEM(block, jnp.float32),
            pltpu.SemaphoreType.DMA((2, block[0] // CHUNK)),
        ],
        compiler_params=pltpu.CompilerParams(vmem_limit_bytes=VMEM_LIMIT),
    )(summed, guess, *basis, t4)


def solution(mesh):
    return jax.shard_map(
        shards,
        mesh=mesh,
        in_specs=(P("gx", "gy", None),) * 3,
        out_specs=(P("gx", "gy", None),) * 2,
        check_vma=False,
    )
```

```python
import functools

import jax
import jax.numpy as jnp
from jax import lax
from jax.experimental import pallas as pl
from jax.experimental.pallas import tpu as pltpu
from jax.sharding import PartitionSpec as P

STEPS = 4
SUB, LANE = 8, 128
center_shift = 6.25
half_range = 6.25
VMEM_LIMIT = 40 * 1024 * 1024

vmem = pl.BlockSpec(memory_space=pltpu.VMEM)
smem = pl.BlockSpec(memory_space=pltpu.SMEM)
hbm = pl.BlockSpec(memory_space=pltpu.HBM)


def f32(*shape):
    return jax.ShapeDtypeStruct(shape, jnp.float32)


def kernel(body, outs, *args, specs=None, out_specs=None, scratch=(), alias=None, flops=0):
    size = sum(a.size * 4 for a in args) + sum(o.size * 4 for o in outs)
    return pl.pallas_call(
        body,
        out_shape=outs,
        in_specs=specs or [vmem] * len(args),
        out_specs=out_specs or [vmem] * len(outs),
        scratch_shapes=list(scratch),
        input_output_aliases=alias or {},
        compiler_params=pltpu.CompilerParams(vmem_limit_bytes=VMEM_LIMIT),
        cost_estimate=pl.CostEstimate(
            flops=flops, bytes_accessed=size, transcendentals=0
        ),
    )(*args)


def kept_shape(block):
    nx, ny, nz = block
    return nx, nz // LANE, ny, LANE


def tiles(shape):
    return shape[2] // SUB, shape[1]


def at(j, c):
    return c, pl.ds(j * SUB, SUB)


def spread(j, c, rows):
    return c, pl.ds(j, SUB, stride=rows)


def line(row, c, shape):
    nx, cols, ny, _ = shape
    return pl.ds(c * ny + row, nx, stride=cols * ny)


def flatten(ref):
    return ref.reshape(ref.shape[0] * ref.shape[1] * ref.shape[2], LANE)


def lanes(c):
    return pl.ds(c * LANE, LANE)


def tree(values):
    while len(values) > 1:
        pairs = [a + b for a, b in zip(values[0::2], values[1::2])]
        values = pairs + ([values[-1]] if len(values) % 2 else [])
    return values[0]


def face_shapes(shape):
    nx, cols, ny, _ = shape
    return [f32(cols, ny, LANE)] * 2 + [f32(cols, nx, LANE)] * 2


def faces_body(field, fx0, fx1, fy0, fy1, ends, low, high, sems):
    nx, ny, _ = field.shape
    cols = ends.shape[1]
    rows = ny // SUB
    copies = [[], [], [], []]
    for c in range(cols):
        for n, source, target in (
            (0, field.at[0, :, lanes(c)], ends.at[0, c]),
            (1, field.at[nx - 1, :, lanes(c)], ends.at[1, c]),
            (2, field.at[:, pl.ds(0, SUB), lanes(c)], low.at[:, c]),
            (3, field.at[:, pl.ds(ny - SUB, SUB), lanes(c)], high.at[:, c]),
        ):
            copies[n].append(pltpu.make_async_copy(source, target, sems.at[n, c]))
    for group in copies:
        for copy in group:
            copy.start()
    for n, out in enumerate((fx0, fx1)):
        for c in range(cols):
            copies[n][c].wait()
            for j in range(rows):
                out[at(j, c)] = ends[(n, *spread(j, c, rows))]
    for n, strip, row, out in ((2, low, 0, fy0), (3, high, SUB - 1, fy1)):
        flat = flatten(strip)
        for c in range(cols):
            copies[n][c].wait()
            out[c] = flat[line(row, c, strip.shape), :]


def neighbours(load, shape):
    rows, cols = shape
    sub = lax.broadcasted_iota(jnp.int32, (SUB, LANE), 0)
    lane = lax.broadcasted_iota(jnp.int32, (SUB, LANE), 1)
    zero = jnp.zeros((SUB, LANE), jnp.float32)
    for c in range(cols):
        mids = [load(0, j, c) for j in range(rows)]
        lowest = jnp.where(sub == 0, zero, pltpu.roll(mids[-1], 1, 0))
        highest = jnp.where(sub == SUB - 1, zero, pltpu.roll(mids[0], SUB - 1, 0))
        for j in range(rows):
            mid = mids[j]
            before = load(0, j, c - 1) if c > 0 else zero
            after = load(0, j, c + 1) if c + 1 < cols else zero
            terms = [
                mids[j - 1] if j > 0 else lowest,
                mids[j + 1] if j + 1 < rows else highest,
                pltpu.roll(jnp.where(lane == LANE - 1, before, mid), 1, 1),
                pltpu.roll(jnp.where(lane == 0, after, mid), LANE - 1, 1),
            ]
            terms += [v for v in (load(-1, j, c), load(1, j, c)) if v is not None]
            yield j, c, mid, tree(terms)


def sweep(nx, one, carry):
    carry = one(0, False, True, carry)
    carry = lax.fori_loop(1, nx - 1, lambda i, a: one(i, True, True, a), carry)
    return one(nx - 1, True, False, carry)


def first_body(
    right_hbm, guess_hbm, diagonal_hbm, out, shifted, guess, right, diagonal, sems
):
    nx = out.shape[0]
    rows, cols = tiles(out.shape)
    part = nx // PARTS
    copies = []
    for n in range(PARTS):
        block = pl.ds(n * part, part)
        copies.append(
            [
                pltpu.make_async_copy(
                    source.at[block, :, lanes(c)], target.at[block, c], sems.at[a, c, n]
                )
                for a, (source, target) in enumerate(
                    ((guess_hbm, guess), (right_hbm, right), (diagonal_hbm, diagonal))
                )
                for c in range(cols)
            ]
        )
    for group in copies:
        for copy in group:
            copy.start()

    def one(i, below, above):
        def load(di, j, c):
            if (di < 0 and not below) or (di > 0 and not above):
                return None
            return guess[(i + di, *spread(j, c, rows))]

        for j, c, mid, beside in neighbours(load, (rows, cols)):
            d = diagonal[(i, *spread(j, c, rows))]
            place = (i, *at(j, c))
            shifted[place] = d + (6.0 - center_shift)
            out[place] = right[(i, *spread(j, c, rows))] - ((6.0 + d) * mid - beside)

    def run(i, _):
        one(i, True, True)
        return 0

    for n in range(PARTS):
        for copy in copies[n]:
            copy.wait()
        if n == 0:
            one(0, False, True)
        start, stop = max(1, n * part - 1), (n + 1) * part - 1
        lax.fori_loop(start, stop, run, 0)
    one(nx - 1, True, False)


def next_body(index, last, *refs):
    if index == 0:
        current, shifted, out, sums = refs
    else:
        current, previous, shifted, out, sums = refs
    scale = 1.0 / half_range if index == 0 else 2.0 / half_range
    nx = out.shape[0]
    rows, cols = tiles(out.shape)
    count = sums.shape[0]

    def one(i, below, above, carry):
        def load(di, j, c):
            if (di < 0 and not below) or (di > 0 and not above):
                return None
            return current[(i + di, *at(j, c))]

        products = [[] for _ in range(count)]
        for j, c, mid, beside in neighbours(load, (rows, cols)):
            place = (i, *at(j, c))
            value = scale * (shifted[place] * mid - beside)
            added = [mid * mid]
            if index > 0:
                before = previous[place]
                value = value - before
                added.append(mid * before)
            if last:
                added += [mid * value, value * value]
            out[place] = value
            for group, product in zip(products, added):
                group.append(product)
            if j == rows - 1:
                carry = tuple(a + tree(g) for a, g in zip(carry, products))
                products = [[] for _ in range(count)]
        return carry

    zero = jnp.zeros((SUB, LANE), jnp.float32)
    total = sweep(nx, one, (zero,) * count)
    for n in range(count):
        sums[n] = total[n]


def add_edges(scale_ref, t, halo, changed):
    xlow, xhigh, ylow, yhigh = halo
    nx, _, ny, _ = t.shape
    rows, cols = tiles(t.shape)
    flat = flatten(t)
    for n, (row, layer) in enumerate(((0, ylow), (ny - 1, yhigh))):
        places = [(line(row, c, t.shape), slice(None)) for c in range(cols)]
        olds = [flat[place] for place in places]
        news = [old + scale_ref[2 + n] * layer[c] for c, old in enumerate(olds)]
        for place, old, new in zip(places, olds, news):
            flat[place] = new
            changed(None, place, old, new)
    for n, (i, layer) in enumerate(((0, xlow), (nx - 1, xhigh))):
        for c in range(cols):
            places = [(i, *at(j, c)) for j in range(rows)]
            olds = [t[place] for place in places]
            news = [old + scale_ref[n] * layer[at(j, c)] for j, old in enumerate(olds)]
            for j in range(rows):
                t[places[j]] = news[j]
                changed((n, j, c), places[j], olds[j], news[j])


def fix_body(scale_ref, t_in, xlow, xhigh, ylow, yhigh, t, fx0, fx1, fy0, fy1):
    ny = t.shape[2]
    _, cols = tiles(t.shape)

    def changed(where, place, old, new):
        if where is not None:
            n, j, c = where
            (fx0, fx1)[n][at(j, c)] = new

    add_edges(scale_ref, t, (xlow, xhigh, ylow, yhigh), changed)
    flat = flatten(t)
    for row, out in ((0, fy0), (ny - 1, fy1)):
        edge = [flat[line(row, c, t.shape), :] for c in range(cols)]
        for c in range(cols):
            out[c] = edge[c]


def close_body(scale_ref, t_in, before, xlow, xhigh, ylow, yhigh, s0, s1, s2, s3, t, out):
    flat = flatten(before)
    cross, square = [s3[2]], [s3[3]]

    def changed(where, place, old, new):
        beside = flat[place] if where is None else before[place]
        first = beside * (new - old)
        second = new * new - old * old
        for k in range(0, first.shape[0], SUB):
            cross.append(first[k : k + SUB])
            square.append(second[k : k + SUB])

    add_edges(scale_ref, t, (xlow, xhigh, ylow, yhigh), changed)
    parts = [s0[0], s1[1], s1[0], s2[1], s2[0], s3[1], s3[0], tree(cross), tree(square)]
    lane = lax.broadcasted_iota(jnp.int32, (SUB, LANE), 1)
    packed = jnp.zeros((SUB, LANE), jnp.float32)
    for n, part in enumerate(parts):
        total = jnp.sum(part, axis=1, keepdims=True)
        packed = jnp.where(lane == n, total, packed)
    packed = jnp.sum(packed, axis=0, keepdims=True)
    out[...] = jnp.broadcast_to(packed, out.shape)


def coefficients(q):
    depth = STEPS
    moment = [None] * (2 * depth + 1)
    moment[0], moment[1] = q[0], q[1]
    for n in range(2, 2 * depth + 1):
        moment[n] = 2.0 * q[n] - moment[n % 2]
    gram = [
        [
            q[i + j] if abs(i - j) < 2 else 0.5 * (moment[i + j] + moment[abs(i - j)])
            for j in range(depth + 1)
        ]
        for i in range(depth + 1)
    ]

    def plus(a, b):
        return b if a is None else a if b is None else a + b

    def times(a, b):
        return None if a is None or b is None else a * b

    def change(v):
        moved = [None] * (depth + 1)
        for k in range(depth):
            if k == 0:
                entries = {0: center_shift, 1: half_range}
            else:
                entries = {
                    k - 1: half_range / 2.0,
                    k: center_shift,
                    k + 1: half_range / 2.0,
                }
            for i, value in entries.items():
                moved[i] = plus(moved[i], times(value, v[k]))
        return moved

    def quad(left, right):
        total = None
        for i in range(depth + 1):
            inner = None
            for j in range(depth + 1):
                inner = plus(inner, times(gram[i][j], right[j]))
            total = plus(total, times(left[i], inner))
        return total

    one = jnp.ones_like(q[0])
    xc = [None] * (depth + 1)
    rc = [one] + [None] * depth
    pc = [one] + [None] * depth
    rr = quad(rc, rc)
    for _ in range(depth):
        moved = change(pc)
        alpha = rr / quad(pc, moved)
        xc = [plus(x, times(alpha, p)) for x, p in zip(xc, pc)]
        rc = [plus(r, times(-alpha, m)) for r, m in zip(rc, moved)]
        following = quad(rc, rc)
        beta = following / rr
        pc = [plus(r, times(beta, p)) for r, p in zip(rc, pc)]
        rr = following
    return xc, rc


CHUNK = 2
PARTS = 4


def final_body(sums, guess, t0, t1, t2, t3, t4, sol_hbm, res_hbm, sol, res, sems):
    nx = t0.shape[0]
    rows, cols = tiles(t0.shape)
    packed = tree([sums[pl.ds(n * SUB, SUB), :] for n in range(sums.shape[0] // SUB)])
    packed = jnp.sum(packed, axis=0, keepdims=True)
    q = [
        jnp.broadcast_to(packed[:, n : n + 1], (SUB, LANE))
        for n in range(2 * STEPS + 1)
    ]
    xc, rc = coefficients(q)
    basis = [t0, t1, t2, t3, t4]
    steps = nx // CHUNK

    def copies(step):
        block = pl.ds(step * CHUNK, CHUNK)
        return [
            pltpu.make_async_copy(
                source.at[block, c], target.at[block, :, lanes(c)], sems.at[n, c, step]
            )
            for n, (source, target) in enumerate(((sol, sol_hbm), (res, res_hbm)))
            for c in range(cols)
        ]

    def step_body(step, carry):
        for u in range(CHUNK):
            i = step * CHUNK + u
            for j in range(rows):
                for c in range(cols):
                    values = [b[(i, *at(j, c))] for b in basis]
                    place = (i, *spread(j, c, rows))
                    x, r = guess[place], None
                    for k in range(STEPS + 1):
                        if xc[k] is not None:
                            x = x + xc[k] * values[k]
                        term = rc[k] * values[k]
                        r = term if r is None else r + term
                    sol[place] = x
                    res[place] = r
        for copy in copies(step):
            copy.start()
        return carry

    lax.fori_loop(0, steps, step_body, 0)

    def wait_body(step, carry):
        for copy in copies(step):
            copy.wait()
        return carry

    lax.fori_loop(0, steps, wait_body, 0)


def exchange(faces):
    xlow, xhigh, ylow, yhigh = faces
    nx, ny = lax.axis_size("gx"), lax.axis_size("gy")
    up_x = [(i, (i + 1) % nx) for i in range(nx)]
    up_y = [(i, (i + 1) % ny) for i in range(ny)]
    return (
        lax.ppermute(xhigh, "gx", up_x),
        lax.ppermute(xlow, "gx", [(b, a) for a, b in up_x]),
        lax.ppermute(yhigh, "gy", up_y),
        lax.ppermute(ylow, "gy", [(b, a) for a, b in up_y]),
    )


def all_sum(rows):
    parts = lax.all_to_all(rows[:, None, :], ("gx", "gy"), 0, 0)
    return parts[:, 0, :]


def fix(scales, t, halo):
    t, *faces = kernel(
        fix_body,
        [f32(*t.shape)] + face_shapes(t.shape),
        scales,
        t,
        *halo,
        specs=[smem] + [vmem] * 5,
        alias={1: 0},
    )
    return t, faces


def shards(right_side, guess, diagonal):
    gx, gy = lax.axis_index("gx"), lax.axis_index("gy")
    nx, ny = lax.axis_size("gx"), lax.axis_size("gy")
    inside = jnp.stack([gx > 0, gx < nx - 1, gy > 0, gy < ny - 1]).astype(jnp.float32)
    right_side, guess, diagonal = (
        pltpu.with_memory_space_constraint(a, pltpu.HBM)
        for a in (right_side, guess, diagonal)
    )
    size, block = guess.size, guess.shape
    kept = kept_shape(block)
    nxl, cols, nyl, _ = kept
    faces = kernel(
        faces_body,
        face_shapes(kept),
        guess,
        specs=[hbm],
        scratch=[
            pltpu.VMEM((2, cols, nyl, LANE), jnp.float32),
            pltpu.VMEM((nxl, cols, SUB, LANE), jnp.float32),
            pltpu.VMEM((nxl, cols, SUB, LANE), jnp.float32),
            pltpu.SemaphoreType.DMA((4, cols)),
        ],
    )
    halo = exchange(faces)
    t, shifted, start = kernel(
        first_body,
        [f32(*kept)] * 3,
        right_side,
        guess,
        diagonal,
        specs=[hbm] * 3,
        scratch=[
            pltpu.VMEM(kept, jnp.float32),
            pltpu.VMEM(kept, jnp.float32),
            pltpu.SemaphoreType.DMA((3, cols, PARTS)),
        ],
        flops=20 * size,
    )
    t, faces = fix(inside, t, halo)
    basis, sums = [t], []
    for k in range(STEPS):
        halo = exchange(faces)
        last = k == STEPS - 1
        count = 1 if k == 0 else 4 if last else 2
        given = [basis[k], shifted] if k == 0 else [basis[k], basis[k - 1], shifted]
        t, s = kernel(
            functools.partial(next_body, k, last),
            [f32(*kept), f32(count, SUB, LANE)],
            *given,
            flops=24 * size,
        )
        sums.append(s)
        scales = inside * (-1.0 / half_range if k == 0 else -2.0 / half_range)
        if not last:
            t, faces = fix(scales, t, halo)
            basis.append(t)
    t4, rows = kernel(
        close_body,
        [f32(*kept), f32(nx * ny, LANE)],
        scales,
        t,
        basis[3],
        *halo,
        *sums,
        specs=[smem] + [vmem] * 10,
        alias={1: 0},
    )
    return kernel(
        final_body,
        [f32(*block), f32(*block)],
        all_sum(rows),
        start,
        *basis,
        t4,
        out_specs=[hbm] * 2,
        scratch=[
            pltpu.VMEM(kept, jnp.float32),
            pltpu.VMEM(kept, jnp.float32),
            pltpu.SemaphoreType.DMA((2, cols, nxl // CHUNK)),
        ],
    )


def solution(mesh):
    return jax.shard_map(
        shards,
        mesh=mesh,
        in_specs=(P("gx", "gy", None),) * 3,
        out_specs=(P("gx", "gy", None),) * 2,
        check_vma=False,
    )
```

```python
import functools

import jax
import jax.numpy as jnp
from jax import lax
from jax.experimental import pallas as pl
from jax.experimental.pallas import tpu as pltpu
from jax.sharding import PartitionSpec as P

STEPS = 4
SUB, LANE = 8, 128
center_shift = 6.25
half_range = 6.25
VMEM_LIMIT = 40 * 1024 * 1024

vmem = pl.BlockSpec(memory_space=pltpu.VMEM)
hbm = pl.BlockSpec(memory_space=pltpu.HBM)


def f32(*shape):
    return jax.ShapeDtypeStruct(shape, jnp.float32)


def kernel(body, outs, *args, specs=None, out_specs=None, scratch=(), alias=None, flops=0):
    size = sum(a.size * 4 for a in args) + sum(o.size * 4 for o in outs)
    return pl.pallas_call(
        body,
        out_shape=outs,
        in_specs=specs or [vmem] * len(args),
        out_specs=out_specs or [vmem] * len(outs),
        scratch_shapes=list(scratch),
        input_output_aliases=alias or {},
        compiler_params=pltpu.CompilerParams(vmem_limit_bytes=VMEM_LIMIT),
        cost_estimate=pl.CostEstimate(
            flops=flops, bytes_accessed=size, transcendentals=0
        ),
    )(*args)


def tree(values):
    while len(values) > 1:
        pairs = [a + b for a, b in zip(values[0::2], values[1::2])]
        values = pairs + ([values[-1]] if len(values) % 2 else [])
    return values[0]


def tiles(shape):
    return shape[1] // SUB, shape[2] // LANE


def layer(t_ref, i, below, above, emit, carry):
    rows, cols = tiles(t_ref.shape)
    sub = lax.broadcasted_iota(jnp.int32, (SUB, LANE), 0)
    lane = lax.broadcasted_iota(jnp.int32, (SUB, LANE), 1)
    first_sub, last_sub = sub == 0, sub == SUB - 1
    first_lane, last_lane = lane == 0, lane == LANE - 1

    def load(j, c, di=0):
        return t_ref[i + di, pl.ds(j * SUB, SUB), pl.ds(c * LANE, LANE)]

    zero = jnp.zeros((SUB, LANE), jnp.float32)
    now = [load(0, c) for c in range(cols)]
    fromlow = [zero] * cols
    for j in range(rows):
        after = [load(j + 1, c) for c in range(cols)] if j + 1 < rows else None
        right = [pltpu.roll(v, 1, 1) for v in now]
        left = [pltpu.roll(v, LANE - 1, 1) for v in now]
        down = [pltpu.roll(v, 1, 0) for v in now]
        for c in range(cols):
            up = pltpu.roll(now[c], SUB - 1, 0)
            nextup = pltpu.roll(after[c], SUB - 1, 0) if after is not None else zero
            s = jnp.where(first_sub, fromlow[c], down[c])
            s = s + jnp.where(last_sub, nextup, up)
            s = s + jnp.where(first_lane, right[c - 1] if c > 0 else zero, right[c])
            s = s + jnp.where(last_lane, left[c + 1] if c + 1 < cols else zero, left[c])
            if below:
                s = s + load(j, c, -1)
            if above:
                s = s + load(j, c, 1)
            carry = emit(i, j, c, now[c], s, carry)
        fromlow = down
        now = after
    return carry


def sweep(t_ref, emit, carry):
    nx = t_ref.shape[0]
    carry = layer(t_ref, 0, False, True, emit, carry)
    carry = lax.fori_loop(
        1, nx - 1, lambda i, a: layer(t_ref, i, True, True, emit, a), carry
    )
    return layer(t_ref, nx - 1, True, False, emit, carry)


def at(j, c):
    return pl.ds(j * SUB, SUB), pl.ds(c * LANE, LANE)


def swaps(count):
    near = [(i, i ^ 1) for i in range(count)]
    far = [(i, i) if i in (0, count - 1) else (i, ((i + 1) ^ 1) - 1) for i in range(count)]
    return near, far


def side(axis):
    index, count = lax.axis_index(axis), lax.axis_size(axis)
    odd = lax.rem(index, 2) == 1
    ends = jnp.logical_or(index == 0, index == count - 1)
    return odd, jnp.where(ends, 0.0, 1.0).astype(jnp.float32)


def exchange(faces):
    near_x, far_x, near_y, far_y = faces
    x, y = swaps(lax.axis_size("gx")), swaps(lax.axis_size("gy"))
    return (
        lax.ppermute(near_x, "gx", x[0]),
        lax.ppermute(far_x, "gx", x[1]),
        lax.ppermute(near_y, "gy", y[0]),
        lax.ppermute(far_y, "gy", y[1]),
    )


def face_shapes(t):
    nx, ny, nz = t.shape
    return [f32(ny, nz), f32(ny, nz), f32(nx, nz), f32(nx, nz)]


def faces_body(field, near_x, far_x, near_y, far_y, low, high, sems):
    nx, ny, _ = field.shape
    odd_x, _ = side("gx")
    odd_y, _ = side("gy")
    near_layer = jnp.where(odd_x, 0, nx - 1)
    copies = [
        pltpu.make_async_copy(field.at[near_layer], near_x, sems.at[0]),
        pltpu.make_async_copy(field.at[nx - 1 - near_layer], far_x, sems.at[1]),
        pltpu.make_async_copy(field.at[:, pl.ds(0, SUB)], low, sems.at[2]),
        pltpu.make_async_copy(field.at[:, pl.ds(ny - SUB, SUB)], high, sems.at[3]),
    ]
    for copy in copies:
        copy.start()
    for copy in copies:
        copy.wait()
    for i in range(nx):
        first, last = low[i, 0:1, :], high[i, SUB - 1 : SUB, :]
        near_y[i : i + 1, :] = jnp.where(odd_y, first, last)
        far_y[i : i + 1, :] = jnp.where(odd_y, last, first)


def first_body(guess, right_side, diagonal, out):
    def emit(i, j, c, mid, beside, carry):
        place = (i, *at(j, c))
        applied = (6.0 + diagonal[place]) * mid - beside
        out[place] = right_side[place] - applied
        return carry

    sweep(guess, emit, 0)


def next_body(index, last, *refs):
    if index == 0:
        current, diagonal, out, sums = refs
    else:
        current, previous, diagonal, out, sums = refs
    scale = 1.0 / half_range if index == 0 else 2.0 / half_range
    zero = jnp.zeros((SUB, LANE), jnp.float32)
    count = sums.shape[0]

    def emit(i, j, c, mid, beside, carry):
        place = (i, *at(j, c))
        d = diagonal[place]
        value = scale * ((d + (6.0 - center_shift)) * mid - beside)
        added = [mid * mid]
        if index > 0:
            before = previous[place]
            value = value - before
            added.append(mid * before)
        if last:
            added += [mid * value, value * value]
        out[place] = value
        return tuple(a + b for a, b in zip(carry, added))

    total = sweep(current, emit, (zero,) * count)
    for n in range(count):
        sums[n] = total[n]


def add_edges(scale, t, halo, changed):
    near_x, far_x, near_y, far_y = halo
    nx, ny, _ = t.shape
    rows, cols = tiles(t.shape)
    sub = lax.broadcasted_iota(jnp.int32, (SUB, LANE), 0)
    odd_x, has_x = side("gx")
    odd_y, has_y = side("gy")
    near_layer = jnp.where(odd_x, 0, nx - 1)
    far_scale_x, far_scale_y = scale * has_x, scale * has_y

    for i, layer, factor, n in (
        (near_layer, near_x, scale, 0),
        (nx - 1 - near_layer, far_x, far_scale_x, 1),
    ):
        for j in range(rows):
            places = [(i, *at(j, c)) for c in range(cols)]
            olds = [t[place] for place in places]
            news = [old + factor * layer[at(j, c)] for c, old in enumerate(olds)]
            for c in range(cols):
                t[places[c]] = news[c]
            changed(places, olds, news)

    low_scale = jnp.where(odd_y, scale, far_scale_y)
    high_scale = jnp.where(odd_y, far_scale_y, scale)
    for i in range(nx):
        places, olds, news = [], [], []
        for c in range(cols):
            lanes = pl.ds(c * LANE, LANE)
            near, far = near_y[pl.ds(i, 1), lanes], far_y[pl.ds(i, 1), lanes]
            low = low_scale * jnp.where(odd_y, near, far)
            high = high_scale * jnp.where(odd_y, far, near)
            for j, row, value in ((0, 0, low), (rows - 1, SUB - 1, high)):
                place = (i, *at(j, c))
                old = t[place]
                places.append(place)
                olds.append(old)
                news.append(old + jnp.where(sub == row, value, 0.0))
        for place, new in zip(places, news):
            t[place] = new
        changed(places, olds, news)


def fix_body(scale, t_in, near_x, far_x, near_y, far_y, t, nfx, ffx, nfy, ffy):
    nx, ny, _ = t.shape
    odd_x, _ = side("gx")
    odd_y, _ = side("gy")
    add_edges(scale, t, (near_x, far_x, near_y, far_y), lambda *_: None)
    near_layer = jnp.where(odd_x, 0, nx - 1)
    nfx[...] = t[near_layer]
    ffx[...] = t[nx - 1 - near_layer]
    for i in range(nx):
        first, last = t[i, 0:1, :], t[i, ny - 1 : ny, :]
        nfy[i : i + 1, :] = jnp.where(odd_y, first, last)
        ffy[i : i + 1, :] = jnp.where(odd_y, last, first)


def close_body(scale, t_in, before, near_x, far_x, near_y, far_y, s0, s1, s2, s3, t, out):
    cross, square = [s3[2]], [s3[3]]

    def changed(places, olds, news):
        cross.append(
            tree([before[p] * (new - old) for p, old, new in zip(places, olds, news)])
        )
        square.append(tree([new * new - old * old for old, new in zip(olds, news)]))

    add_edges(scale, t, (near_x, far_x, near_y, far_y), changed)
    parts = [s0[0], s1[1], s1[0], s2[1], s2[0], s3[1], s3[0], tree(cross), tree(square)]
    lane = lax.broadcasted_iota(jnp.int32, (SUB, LANE), 1)
    packed = jnp.zeros((SUB, LANE), jnp.float32)
    for n, part in enumerate(parts):
        total = jnp.sum(part, axis=1, keepdims=True)
        packed = jnp.where(lane == n, total, packed)
    packed = jnp.sum(packed, axis=0, keepdims=True)
    out[...] = jnp.broadcast_to(packed, out.shape)


def coefficients(q):
    depth = STEPS
    moment = [None] * (2 * depth + 1)
    moment[0], moment[1] = q[0], q[1]
    for n in range(2, 2 * depth + 1):
        moment[n] = 2.0 * q[n] - moment[n % 2]
    gram = [
        [
            q[i + j] if abs(i - j) < 2 else 0.5 * (moment[i + j] + moment[abs(i - j)])
            for j in range(depth + 1)
        ]
        for i in range(depth + 1)
    ]

    def plus(a, b):
        return b if a is None else a if b is None else a + b

    def times(a, b):
        return None if a is None or b is None else a * b

    def change(v):
        moved = [None] * (depth + 1)
        for k in range(depth):
            if k == 0:
                entries = {0: center_shift, 1: half_range}
            else:
                entries = {
                    k - 1: half_range / 2.0,
                    k: center_shift,
                    k + 1: half_range / 2.0,
                }
            for i, value in entries.items():
                moved[i] = plus(moved[i], times(value, v[k]))
        return moved

    def quad(left, right):
        total = None
        for i in range(depth + 1):
            inner = None
            for j in range(depth + 1):
                inner = plus(inner, times(gram[i][j], right[j]))
            total = plus(total, times(left[i], inner))
        return total

    one = jnp.ones_like(q[0])
    xc = [None] * (depth + 1)
    rc = [one] + [None] * depth
    pc = [one] + [None] * depth
    rr = quad(rc, rc)
    for _ in range(depth):
        moved = change(pc)
        alpha = rr / quad(pc, moved)
        xc = [plus(x, times(alpha, p)) for x, p in zip(xc, pc)]
        rc = [plus(r, times(-alpha, m)) for r, m in zip(rc, moved)]
        following = quad(rc, rc)
        beta = following / rr
        pc = [plus(r, times(beta, p)) for r, p in zip(rc, pc)]
        rr = following
    return xc, rc


CHUNK = 2


def final_body(sums, guess, t0, t1, t2, t3, t4, sol_hbm, res_hbm, sol, res, sems):
    nx = t0.shape[0]
    rows, cols = tiles(t0.shape)
    packed = tree([sums[pl.ds(n * SUB, SUB), :] for n in range(sums.shape[0] // SUB)])
    packed = jnp.sum(packed, axis=0, keepdims=True)
    q = [
        jnp.broadcast_to(packed[:, n : n + 1], (SUB, LANE))
        for n in range(2 * STEPS + 1)
    ]
    xc, rc = coefficients(q)
    basis = [t0, t1, t2, t3, t4]
    steps = nx // CHUNK

    def copies(step):
        block = pl.ds(step * CHUNK, CHUNK)
        return (
            pltpu.make_async_copy(sol.at[block], sol_hbm.at[block], sems.at[0, step]),
            pltpu.make_async_copy(res.at[block], res_hbm.at[block], sems.at[1, step]),
        )

    def step_body(step, carry):
        for u in range(CHUNK):
            i = step * CHUNK + u
            for j in range(rows):
                for c in range(cols):
                    place = (i, *at(j, c))
                    values = [b[place] for b in basis]
                    x, r = guess[place], None
                    for k in range(STEPS + 1):
                        if xc[k] is not None:
                            x = x + xc[k] * values[k]
                        term = rc[k] * values[k]
                        r = term if r is None else r + term
                    sol[place] = x
                    res[place] = r
        for copy in copies(step):
            copy.start()
        return carry

    lax.fori_loop(0, steps, step_body, 0)

    def wait_body(step, carry):
        for copy in copies(step):
            copy.wait()
        return carry

    lax.fori_loop(0, steps, wait_body, 0)


def all_sum(rows):
    parts = lax.all_to_all(rows[:, None, :], ("gx", "gy"), 0, 0)
    return parts[:, 0, :]


def fix(scale, t, halo):
    t, *faces = kernel(
        functools.partial(fix_body, scale),
        [f32(*t.shape)] + face_shapes(t),
        t,
        *halo,
        alias={0: 0},
    )
    return t, faces


def shards(right_side, guess, diagonal):
    devices = lax.axis_size("gx") * lax.axis_size("gy")
    size, block = guess.size, guess.shape
    strip = pltpu.VMEM((block[0], SUB, block[2]), jnp.float32)
    faces = kernel(
        faces_body,
        face_shapes(guess),
        pltpu.with_memory_space_constraint(guess, pltpu.HBM),
        specs=[hbm],
        scratch=[strip, strip, pltpu.SemaphoreType.DMA((4,))],
        flops=100000 * size,
    )
    guess, right_side, diagonal = (
        pltpu.with_memory_space_constraint(a, pltpu.VMEM)
        for a in (guess, right_side, diagonal)
    )
    halo = exchange(faces)
    (t,) = kernel(
        first_body, [f32(*block)], guess, right_side, diagonal, flops=20 * size
    )
    t, faces = fix(1.0, t, halo)
    basis, sums = [t], []
    for k in range(STEPS):
        halo = exchange(faces)
        last = k == STEPS - 1
        count = 1 if k == 0 else 4 if last else 2
        given = [basis[k], diagonal] if k == 0 else [basis[k], basis[k - 1], diagonal]
        t, s = kernel(
            functools.partial(next_body, k, last),
            [f32(*block), f32(count, SUB, LANE)],
            *given,
            flops=24 * size,
        )
        sums.append(s)
        scale = -1.0 / half_range if k == 0 else -2.0 / half_range
        if not last:
            t, faces = fix(scale, t, halo)
            basis.append(t)
    t4, rows = kernel(
        functools.partial(close_body, scale),
        [f32(*block), f32(devices, LANE)],
        t,
        basis[3],
        *halo,
        *sums,
        alias={0: 0},
    )
    return kernel(
        final_body,
        [f32(*block), f32(*block)],
        all_sum(rows),
        guess,
        *basis,
        t4,
        out_specs=[hbm] * 2,
        scratch=[
            pltpu.VMEM(block, jnp.float32),
            pltpu.VMEM(block, jnp.float32),
            pltpu.SemaphoreType.DMA((2, block[0] // CHUNK)),
        ],
    )


def solution(mesh):
    return jax.shard_map(
        shards,
        mesh=mesh,
        in_specs=(P("gx", "gy", None),) * 3,
        out_specs=(P("gx", "gy", None),) * 2,
        check_vma=False,
    )
```

```python
import functools

import jax
import jax.numpy as jnp
from jax import lax
from jax.experimental import pallas as pl
from jax.experimental.pallas import tpu as pltpu
from jax.sharding import PartitionSpec as P

STEPS = 4
SUB, LANE = 8, 128
center_shift = 6.25
half_range = 6.25
VMEM_LIMIT = 40 * 1024 * 1024

vmem = pl.BlockSpec(memory_space=pltpu.VMEM)
hbm = pl.BlockSpec(memory_space=pltpu.HBM)


def f32(*shape):
    return jax.ShapeDtypeStruct(shape, jnp.float32)


def kernel(body, outs, *args, specs=None, out_specs=None, scratch=(), alias=None, flops=0):
    size = sum(a.size * 4 for a in args) + sum(o.size * 4 for o in outs)
    return pl.pallas_call(
        body,
        out_shape=outs,
        in_specs=specs or [vmem] * len(args),
        out_specs=out_specs or [vmem] * len(outs),
        scratch_shapes=list(scratch),
        input_output_aliases=alias or {},
        compiler_params=pltpu.CompilerParams(vmem_limit_bytes=VMEM_LIMIT),
        cost_estimate=pl.CostEstimate(
            flops=flops, bytes_accessed=size, transcendentals=0
        ),
    )(*args)


def tree(values):
    while len(values) > 1:
        pairs = [a + b for a, b in zip(values[0::2], values[1::2])]
        values = pairs + ([values[-1]] if len(values) % 2 else [])
    return values[0]


def tiles(shape):
    return shape[1] // SUB, shape[2] // LANE


def layer(t_ref, i, below, above, emit, carry):
    rows, cols = tiles(t_ref.shape)
    sub = lax.broadcasted_iota(jnp.int32, (SUB, LANE), 0)
    lane = lax.broadcasted_iota(jnp.int32, (SUB, LANE), 1)
    first_sub, last_sub = sub == 0, sub == SUB - 1
    first_lane, last_lane = lane == 0, lane == LANE - 1

    def load(j, c, di=0):
        return t_ref[i + di, pl.ds(j * SUB, SUB), pl.ds(c * LANE, LANE)]

    zero = jnp.zeros((SUB, LANE), jnp.float32)
    now = [load(0, c) for c in range(cols)]
    fromlow = [zero] * cols
    for j in range(rows):
        after = [load(j + 1, c) for c in range(cols)] if j + 1 < rows else None
        right = [pltpu.roll(v, 1, 1) for v in now]
        left = [pltpu.roll(v, LANE - 1, 1) for v in now]
        down = [pltpu.roll(v, 1, 0) for v in now]
        for c in range(cols):
            up = pltpu.roll(now[c], SUB - 1, 0)
            nextup = pltpu.roll(after[c], SUB - 1, 0) if after is not None else zero
            s = jnp.where(first_sub, fromlow[c], down[c])
            s = s + jnp.where(last_sub, nextup, up)
            s = s + jnp.where(first_lane, right[c - 1] if c > 0 else zero, right[c])
            s = s + jnp.where(last_lane, left[c + 1] if c + 1 < cols else zero, left[c])
            if below:
                s = s + load(j, c, -1)
            if above:
                s = s + load(j, c, 1)
            carry = emit(i, j, c, now[c], s, carry)
        fromlow = down
        now = after
    return carry


def sweep(t_ref, emit, carry):
    nx = t_ref.shape[0]
    carry = layer(t_ref, 0, False, True, emit, carry)
    carry = lax.fori_loop(
        1, nx - 1, lambda i, a: layer(t_ref, i, True, True, emit, a), carry
    )
    return layer(t_ref, nx - 1, True, False, emit, carry)


def at(j, c):
    return pl.ds(j * SUB, SUB), pl.ds(c * LANE, LANE)


def swaps(count):
    near = [(i, i ^ 1) for i in range(count)]
    far = [(i, (i + 1) % count if i % 2 else (i - 1) % count) for i in range(count)]
    return near, far


def side(axis):
    index, count = lax.axis_index(axis), lax.axis_size(axis)
    odd = lax.rem(index, 2) == 1
    ends = jnp.logical_or(index == 0, index == count - 1)
    return odd, jnp.where(ends, 0.0, 1.0).astype(jnp.float32)


def exchange(faces):
    near_x, far_x, near_y, far_y = faces
    x, y = swaps(lax.axis_size("gx")), swaps(lax.axis_size("gy"))
    return (
        lax.ppermute(near_x, "gx", x[0]),
        lax.ppermute(far_x, "gx", x[1]),
        lax.ppermute(near_y, "gy", y[0]),
        lax.ppermute(far_y, "gy", y[1]),
    )


def face_shapes(t):
    nx, ny, nz = t.shape
    return [f32(ny, nz), f32(ny, nz), f32(nx, nz), f32(nx, nz)]


def faces_body(field, near_x, far_x, near_y, far_y, low, high, sems):
    nx, ny, _ = field.shape
    odd_x, _ = side("gx")
    odd_y, _ = side("gy")
    near_layer = jnp.where(odd_x, 0, nx - 1)
    copies = [
        pltpu.make_async_copy(field.at[near_layer], near_x, sems.at[0]),
        pltpu.make_async_copy(field.at[nx - 1 - near_layer], far_x, sems.at[1]),
        pltpu.make_async_copy(field.at[:, pl.ds(0, SUB)], low, sems.at[2]),
        pltpu.make_async_copy(field.at[:, pl.ds(ny - SUB, SUB)], high, sems.at[3]),
    ]
    for copy in copies:
        copy.start()
    for copy in copies:
        copy.wait()
    for i in range(nx):
        first, last = low[i, 0:1, :], high[i, SUB - 1 : SUB, :]
        near_y[i : i + 1, :] = jnp.where(odd_y, first, last)
        far_y[i : i + 1, :] = jnp.where(odd_y, last, first)


def first_body(guess, right_side, diagonal, out):
    def emit(i, j, c, mid, beside, carry):
        place = (i, *at(j, c))
        applied = (6.0 + diagonal[place]) * mid - beside
        out[place] = right_side[place] - applied
        return carry

    sweep(guess, emit, 0)


def next_body(index, last, *refs):
    if index == 0:
        current, diagonal, out, sums = refs
    else:
        current, previous, diagonal, out, sums = refs
    scale = 1.0 / half_range if index == 0 else 2.0 / half_range
    zero = jnp.zeros((SUB, LANE), jnp.float32)
    count = sums.shape[0]

    def emit(i, j, c, mid, beside, carry):
        place = (i, *at(j, c))
        d = diagonal[place]
        value = scale * ((d + (6.0 - center_shift)) * mid - beside)
        added = [mid * mid]
        if index > 0:
            before = previous[place]
            value = value - before
            added.append(mid * before)
        if last:
            added += [mid * value, value * value]
        out[place] = value
        return tuple(a + b for a, b in zip(carry, added))

    total = sweep(current, emit, (zero,) * count)
    for n in range(count):
        sums[n] = total[n]


def add_edges(scale, t, halo, changed):
    near_x, far_x, near_y, far_y = halo
    nx, ny, _ = t.shape
    rows, cols = tiles(t.shape)
    sub = lax.broadcasted_iota(jnp.int32, (SUB, LANE), 0)
    odd_x, has_x = side("gx")
    odd_y, has_y = side("gy")
    near_layer = jnp.where(odd_x, 0, nx - 1)
    far_scale_x, far_scale_y = scale * has_x, scale * has_y

    for i, layer, factor, n in (
        (near_layer, near_x, scale, 0),
        (nx - 1 - near_layer, far_x, far_scale_x, 1),
    ):
        for j in range(rows):
            places = [(i, *at(j, c)) for c in range(cols)]
            olds = [t[place] for place in places]
            news = [old + factor * layer[at(j, c)] for c, old in enumerate(olds)]
            for c in range(cols):
                t[places[c]] = news[c]
            changed(places, olds, news)

    low_scale = jnp.where(odd_y, scale, far_scale_y)
    high_scale = jnp.where(odd_y, far_scale_y, scale)
    for i in range(nx):
        places, olds, news = [], [], []
        for c in range(cols):
            lanes = pl.ds(c * LANE, LANE)
            near, far = near_y[pl.ds(i, 1), lanes], far_y[pl.ds(i, 1), lanes]
            low = low_scale * jnp.where(odd_y, near, far)
            high = high_scale * jnp.where(odd_y, far, near)
            for j, row, value in ((0, 0, low), (rows - 1, SUB - 1, high)):
                place = (i, *at(j, c))
                old = t[place]
                places.append(place)
                olds.append(old)
                news.append(old + jnp.where(sub == row, value, 0.0))
        for place, new in zip(places, news):
            t[place] = new
        changed(places, olds, news)


def fix_body(scale, t_in, near_x, far_x, near_y, far_y, t, nfx, ffx, nfy, ffy):
    nx, ny, _ = t.shape
    odd_x, _ = side("gx")
    odd_y, _ = side("gy")
    add_edges(scale, t, (near_x, far_x, near_y, far_y), lambda *_: None)
    near_layer = jnp.where(odd_x, 0, nx - 1)
    nfx[...] = t[near_layer]
    ffx[...] = t[nx - 1 - near_layer]
    for i in range(nx):
        first, last = t[i, 0:1, :], t[i, ny - 1 : ny, :]
        nfy[i : i + 1, :] = jnp.where(odd_y, first, last)
        ffy[i : i + 1, :] = jnp.where(odd_y, last, first)


def close_body(scale, t_in, before, near_x, far_x, near_y, far_y, s0, s1, s2, s3, t, out):
    cross, square = [s3[2]], [s3[3]]

    def changed(places, olds, news):
        cross.append(
            tree([before[p] * (new - old) for p, old, new in zip(places, olds, news)])
        )
        square.append(tree([new * new - old * old for old, new in zip(olds, news)]))

    add_edges(scale, t, (near_x, far_x, near_y, far_y), changed)
    parts = [s0[0], s1[1], s1[0], s2[1], s2[0], s3[1], s3[0], tree(cross), tree(square)]
    lane = lax.broadcasted_iota(jnp.int32, (SUB, LANE), 1)
    packed = jnp.zeros((SUB, LANE), jnp.float32)
    for n, part in enumerate(parts):
        total = jnp.sum(part, axis=1, keepdims=True)
        packed = jnp.where(lane == n, total, packed)
    packed = jnp.sum(packed, axis=0, keepdims=True)
    out[...] = jnp.broadcast_to(packed, out.shape)


def coefficients(q):
    depth = STEPS
    moment = [None] * (2 * depth + 1)
    moment[0], moment[1] = q[0], q[1]
    for n in range(2, 2 * depth + 1):
        moment[n] = 2.0 * q[n] - moment[n % 2]
    gram = [
        [
            q[i + j] if abs(i - j) < 2 else 0.5 * (moment[i + j] + moment[abs(i - j)])
            for j in range(depth + 1)
        ]
        for i in range(depth + 1)
    ]

    def plus(a, b):
        return b if a is None else a if b is None else a + b

    def times(a, b):
        return None if a is None or b is None else a * b

    def change(v):
        moved = [None] * (depth + 1)
        for k in range(depth):
            if k == 0:
                entries = {0: center_shift, 1: half_range}
            else:
                entries = {
                    k - 1: half_range / 2.0,
                    k: center_shift,
                    k + 1: half_range / 2.0,
                }
            for i, value in entries.items():
                moved[i] = plus(moved[i], times(value, v[k]))
        return moved

    def quad(left, right):
        total = None
        for i in range(depth + 1):
            inner = None
            for j in range(depth + 1):
                inner = plus(inner, times(gram[i][j], right[j]))
            total = plus(total, times(left[i], inner))
        return total

    one = jnp.ones_like(q[0])
    xc = [None] * (depth + 1)
    rc = [one] + [None] * depth
    pc = [one] + [None] * depth
    rr = quad(rc, rc)
    for _ in range(depth):
        moved = change(pc)
        alpha = rr / quad(pc, moved)
        xc = [plus(x, times(alpha, p)) for x, p in zip(xc, pc)]
        rc = [plus(r, times(-alpha, m)) for r, m in zip(rc, moved)]
        following = quad(rc, rc)
        beta = following / rr
        pc = [plus(r, times(beta, p)) for r, p in zip(rc, pc)]
        rr = following
    return xc, rc


CHUNK = 2


def final_body(sums, guess, t0, t1, t2, t3, t4, sol_hbm, res_hbm, sol, res, sems):
    nx = t0.shape[0]
    rows, cols = tiles(t0.shape)
    packed = tree([sums[pl.ds(n * SUB, SUB), :] for n in range(sums.shape[0] // SUB)])
    packed = jnp.sum(packed, axis=0, keepdims=True)
    q = [
        jnp.broadcast_to(packed[:, n : n + 1], (SUB, LANE))
        for n in range(2 * STEPS + 1)
    ]
    xc, rc = coefficients(q)
    basis = [t0, t1, t2, t3, t4]
    steps = nx // CHUNK

    def copies(step):
        block = pl.ds(step * CHUNK, CHUNK)
        return (
            pltpu.make_async_copy(sol.at[block], sol_hbm.at[block], sems.at[0, step]),
            pltpu.make_async_copy(res.at[block], res_hbm.at[block], sems.at[1, step]),
        )

    def step_body(step, carry):
        for u in range(CHUNK):
            i = step * CHUNK + u
            for j in range(rows):
                for c in range(cols):
                    place = (i, *at(j, c))
                    values = [b[place] for b in basis]
                    x, r = guess[place], None
                    for k in range(STEPS + 1):
                        if xc[k] is not None:
                            x = x + xc[k] * values[k]
                        term = rc[k] * values[k]
                        r = term if r is None else r + term
                    sol[place] = x
                    res[place] = r
        for copy in copies(step):
            copy.start()
        return carry

    lax.fori_loop(0, steps, step_body, 0)

    def wait_body(step, carry):
        for copy in copies(step):
            copy.wait()
        return carry

    lax.fori_loop(0, steps, wait_body, 0)


def all_sum(rows):
    parts = lax.all_to_all(rows[:, None, :], ("gx", "gy"), 0, 0)
    return parts[:, 0, :]


def fix(scale, t, halo):
    t, *faces = kernel(
        functools.partial(fix_body, scale),
        [f32(*t.shape)] + face_shapes(t),
        t,
        *halo,
        alias={0: 0},
    )
    return t, faces


def shards(right_side, guess, diagonal):
    devices = lax.axis_size("gx") * lax.axis_size("gy")
    size, block = guess.size, guess.shape
    strip = pltpu.VMEM((block[0], SUB, block[2]), jnp.float32)
    faces = kernel(
        faces_body,
        face_shapes(guess),
        pltpu.with_memory_space_constraint(guess, pltpu.HBM),
        specs=[hbm],
        scratch=[strip, strip, pltpu.SemaphoreType.DMA((4,))],
        flops=100000 * size,
    )
    guess, right_side, diagonal = (
        pltpu.with_memory_space_constraint(a, pltpu.VMEM)
        for a in (guess, right_side, diagonal)
    )
    halo = exchange(faces)
    (t,) = kernel(
        first_body, [f32(*block)], guess, right_side, diagonal, flops=20 * size
    )
    t, faces = fix(1.0, t, halo)
    basis, sums = [t], []
    for k in range(STEPS):
        halo = exchange(faces)
        last = k == STEPS - 1
        count = 1 if k == 0 else 4 if last else 2
        given = [basis[k], diagonal] if k == 0 else [basis[k], basis[k - 1], diagonal]
        t, s = kernel(
            functools.partial(next_body, k, last),
            [f32(*block), f32(count, SUB, LANE)],
            *given,
            flops=24 * size,
        )
        sums.append(s)
        scale = -1.0 / half_range if k == 0 else -2.0 / half_range
        if not last:
            t, faces = fix(scale, t, halo)
            basis.append(t)
    t4, rows = kernel(
        functools.partial(close_body, scale),
        [f32(*block), f32(devices, LANE)],
        t,
        basis[3],
        *halo,
        *sums,
        alias={0: 0},
    )
    return kernel(
        final_body,
        [f32(*block), f32(*block)],
        all_sum(rows),
        guess,
        *basis,
        t4,
        out_specs=[hbm] * 2,
        scratch=[
            pltpu.VMEM(block, jnp.float32),
            pltpu.VMEM(block, jnp.float32),
            pltpu.SemaphoreType.DMA((2, block[0] // CHUNK)),
        ],
    )


def solution(mesh):
    return jax.shard_map(
        shards,
        mesh=mesh,
        in_specs=(P("gx", "gy", None),) * 3,
        out_specs=(P("gx", "gy", None),) * 2,
        check_vma=False,
    )
```

```python
import functools

import jax
import jax.numpy as jnp
from jax import lax
from jax.experimental import pallas as pl
from jax.experimental.pallas import tpu as pltpu
from jax.sharding import PartitionSpec as P

STEPS = 4
SUB, LANE = 8, 128
center_shift = 6.25
half_range = 6.25
VMEM_LIMIT = 40 * 1024 * 1024

vmem = pl.BlockSpec(memory_space=pltpu.VMEM)
hbm = pl.BlockSpec(memory_space=pltpu.HBM)


def f32(*shape):
    return jax.ShapeDtypeStruct(shape, jnp.float32)


def kernel(body, outs, *args, specs=None, out_specs=None, scratch=(), alias=None, flops=0):
    size = sum(a.size * 4 for a in args) + sum(o.size * 4 for o in outs)
    return pl.pallas_call(
        body,
        out_shape=outs,
        in_specs=specs or [vmem] * len(args),
        out_specs=out_specs or [vmem] * len(outs),
        scratch_shapes=list(scratch),
        input_output_aliases=alias or {},
        compiler_params=pltpu.CompilerParams(vmem_limit_bytes=VMEM_LIMIT),
        cost_estimate=pl.CostEstimate(
            flops=flops, bytes_accessed=size, transcendentals=0
        ),
    )(*args)


def tree(values):
    while len(values) > 1:
        pairs = [a + b for a, b in zip(values[0::2], values[1::2])]
        values = pairs + ([values[-1]] if len(values) % 2 else [])
    return values[0]


def tiles(shape):
    return shape[1] // SUB, shape[2] // LANE


def layer(t_ref, i, below, above, emit, carry):
    rows, cols = tiles(t_ref.shape)
    sub = lax.broadcasted_iota(jnp.int32, (SUB, LANE), 0)
    lane = lax.broadcasted_iota(jnp.int32, (SUB, LANE), 1)
    first_sub, last_sub = sub == 0, sub == SUB - 1
    first_lane, last_lane = lane == 0, lane == LANE - 1

    def load(j, c, di=0):
        return t_ref[i + di, pl.ds(j * SUB, SUB), pl.ds(c * LANE, LANE)]

    zero = jnp.zeros((SUB, LANE), jnp.float32)
    now = [load(0, c) for c in range(cols)]
    fromlow = [zero] * cols
    for j in range(rows):
        after = [load(j + 1, c) for c in range(cols)] if j + 1 < rows else None
        right = [pltpu.roll(v, 1, 1) for v in now]
        left = [pltpu.roll(v, LANE - 1, 1) for v in now]
        down = [pltpu.roll(v, 1, 0) for v in now]
        for c in range(cols):
            up = pltpu.roll(now[c], SUB - 1, 0)
            nextup = pltpu.roll(after[c], SUB - 1, 0) if after is not None else zero
            s = jnp.where(first_sub, fromlow[c], down[c])
            s = s + jnp.where(last_sub, nextup, up)
            s = s + jnp.where(first_lane, right[c - 1] if c > 0 else zero, right[c])
            s = s + jnp.where(last_lane, left[c + 1] if c + 1 < cols else zero, left[c])
            if below:
                s = s + load(j, c, -1)
            if above:
                s = s + load(j, c, 1)
            carry = emit(i, j, c, now[c], s, carry)
        fromlow = down
        now = after
    return carry


def sweep(t_ref, emit, carry):
    nx = t_ref.shape[0]
    carry = layer(t_ref, 0, False, True, emit, carry)
    carry = lax.fori_loop(
        1, nx - 1, lambda i, a: layer(t_ref, i, True, True, emit, a), carry
    )
    return layer(t_ref, nx - 1, True, False, emit, carry)


def at(j, c):
    return pl.ds(j * SUB, SUB), pl.ds(c * LANE, LANE)


def swaps(count):
    near = [(i, i ^ 1) for i in range(count)]
    far = [(i, (i + 1) % count if i % 2 else (i - 1) % count) for i in range(count)]
    return near, far


def side(axis):
    index, count = lax.axis_index(axis), lax.axis_size(axis)
    odd = lax.rem(index, 2) == 1
    ends = jnp.logical_or(index == 0, index == count - 1)
    return odd, jnp.where(ends, 0.0, 1.0).astype(jnp.float32)


def exchange(faces):
    near_x, far_x, near_y, far_y = faces
    x, y = swaps(lax.axis_size("gx")), swaps(lax.axis_size("gy"))
    far_x = lax.ppermute(far_x, "gx", x[1])
    near_x = lax.ppermute(near_x, "gx", x[0])
    far_y = lax.ppermute(far_y, "gy", y[1])
    near_y = lax.ppermute(near_y, "gy", y[0])
    return near_x, far_x, near_y, far_y


def face_shapes(t):
    nx, ny, nz = t.shape
    return [f32(ny, nz), f32(ny, nz), f32(nx, nz), f32(nx, nz)]


def faces_body(field, near_x, far_x, near_y, far_y, low, high, sems):
    nx, ny, _ = field.shape
    odd_x, _ = side("gx")
    odd_y, _ = side("gy")
    near_layer = jnp.where(odd_x, 0, nx - 1)
    copies = [
        pltpu.make_async_copy(field.at[near_layer], near_x, sems.at[0]),
        pltpu.make_async_copy(field.at[nx - 1 - near_layer], far_x, sems.at[1]),
        pltpu.make_async_copy(field.at[:, pl.ds(0, SUB)], low, sems.at[2]),
        pltpu.make_async_copy(field.at[:, pl.ds(ny - SUB, SUB)], high, sems.at[3]),
    ]
    for copy in copies:
        copy.start()
    for copy in copies:
        copy.wait()
    for i in range(nx):
        first, last = low[i, 0:1, :], high[i, SUB - 1 : SUB, :]
        near_y[i : i + 1, :] = jnp.where(odd_y, first, last)
        far_y[i : i + 1, :] = jnp.where(odd_y, last, first)


def first_body(guess, right_side, diagonal, out):
    def emit(i, j, c, mid, beside, carry):
        place = (i, *at(j, c))
        applied = (6.0 + diagonal[place]) * mid - beside
        out[place] = right_side[place] - applied
        return carry

    sweep(guess, emit, 0)


def next_body(index, last, *refs):
    if index == 0:
        current, diagonal, out, sums = refs
    else:
        current, previous, diagonal, out, sums = refs
    scale = 1.0 / half_range if index == 0 else 2.0 / half_range
    zero = jnp.zeros((SUB, LANE), jnp.float32)
    count = sums.shape[0]

    def emit(i, j, c, mid, beside, carry):
        place = (i, *at(j, c))
        d = diagonal[place]
        value = scale * ((d + (6.0 - center_shift)) * mid - beside)
        added = [mid * mid]
        if index > 0:
            before = previous[place]
            value = value - before
            added.append(mid * before)
        if last:
            added += [mid * value, value * value]
        out[place] = value
        return tuple(a + b for a, b in zip(carry, added))

    total = sweep(current, emit, (zero,) * count)
    for n in range(count):
        sums[n] = total[n]


def add_edges(scale, t, halo, changed):
    near_x, far_x, near_y, far_y = halo
    nx, ny, _ = t.shape
    rows, cols = tiles(t.shape)
    sub = lax.broadcasted_iota(jnp.int32, (SUB, LANE), 0)
    odd_x, has_x = side("gx")
    odd_y, has_y = side("gy")
    near_layer = jnp.where(odd_x, 0, nx - 1)
    far_scale_x, far_scale_y = scale * has_x, scale * has_y

    for i, layer, factor, n in (
        (near_layer, near_x, scale, 0),
        (nx - 1 - near_layer, far_x, far_scale_x, 1),
    ):
        for j in range(rows):
            places = [(i, *at(j, c)) for c in range(cols)]
            olds = [t[place] for place in places]
            news = [old + factor * layer[at(j, c)] for c, old in enumerate(olds)]
            for c in range(cols):
                t[places[c]] = news[c]
            changed(places, olds, news)

    low_scale = jnp.where(odd_y, scale, far_scale_y)
    high_scale = jnp.where(odd_y, far_scale_y, scale)
    for i in range(nx):
        places, olds, news = [], [], []
        for c in range(cols):
            lanes = pl.ds(c * LANE, LANE)
            near, far = near_y[pl.ds(i, 1), lanes], far_y[pl.ds(i, 1), lanes]
            low = low_scale * jnp.where(odd_y, near, far)
            high = high_scale * jnp.where(odd_y, far, near)
            for j, row, value in ((0, 0, low), (rows - 1, SUB - 1, high)):
                place = (i, *at(j, c))
                old = t[place]
                places.append(place)
                olds.append(old)
                news.append(old + jnp.where(sub == row, value, 0.0))
        for place, new in zip(places, news):
            t[place] = new
        changed(places, olds, news)


def fix_body(scale, t_in, near_x, far_x, near_y, far_y, t, nfx, ffx, nfy, ffy):
    nx, ny, _ = t.shape
    odd_x, _ = side("gx")
    odd_y, _ = side("gy")
    add_edges(scale, t, (near_x, far_x, near_y, far_y), lambda *_: None)
    near_layer = jnp.where(odd_x, 0, nx - 1)
    nfx[...] = t[near_layer]
    ffx[...] = t[nx - 1 - near_layer]
    for i in range(nx):
        first, last = t[i, 0:1, :], t[i, ny - 1 : ny, :]
        nfy[i : i + 1, :] = jnp.where(odd_y, first, last)
        ffy[i : i + 1, :] = jnp.where(odd_y, last, first)


def close_body(scale, t_in, before, near_x, far_x, near_y, far_y, s0, s1, s2, s3, t, out):
    cross, square = [s3[2]], [s3[3]]

    def changed(places, olds, news):
        cross.append(
            tree([before[p] * (new - old) for p, old, new in zip(places, olds, news)])
        )
        square.append(tree([new * new - old * old for old, new in zip(olds, news)]))

    add_edges(scale, t, (near_x, far_x, near_y, far_y), changed)
    parts = [s0[0], s1[1], s1[0], s2[1], s2[0], s3[1], s3[0], tree(cross), tree(square)]
    lane = lax.broadcasted_iota(jnp.int32, (SUB, LANE), 1)
    packed = jnp.zeros((SUB, LANE), jnp.float32)
    for n, part in enumerate(parts):
        total = jnp.sum(part, axis=1, keepdims=True)
        packed = jnp.where(lane == n, total, packed)
    packed = jnp.sum(packed, axis=0, keepdims=True)
    out[...] = jnp.broadcast_to(packed, out.shape)


def coefficients(q):
    depth = STEPS
    moment = [None] * (2 * depth + 1)
    moment[0], moment[1] = q[0], q[1]
    for n in range(2, 2 * depth + 1):
        moment[n] = 2.0 * q[n] - moment[n % 2]
    gram = [
        [
            q[i + j] if abs(i - j) < 2 else 0.5 * (moment[i + j] + moment[abs(i - j)])
            for j in range(depth + 1)
        ]
        for i in range(depth + 1)
    ]

    def plus(a, b):
        return b if a is None else a if b is None else a + b

    def times(a, b):
        return None if a is None or b is None else a * b

    def change(v):
        moved = [None] * (depth + 1)
        for k in range(depth):
            if k == 0:
                entries = {0: center_shift, 1: half_range}
            else:
                entries = {
                    k - 1: half_range / 2.0,
                    k: center_shift,
                    k + 1: half_range / 2.0,
                }
            for i, value in entries.items():
                moved[i] = plus(moved[i], times(value, v[k]))
        return moved

    def quad(left, right):
        total = None
        for i in range(depth + 1):
            inner = None
            for j in range(depth + 1):
                inner = plus(inner, times(gram[i][j], right[j]))
            total = plus(total, times(left[i], inner))
        return total

    one = jnp.ones_like(q[0])
    xc = [None] * (depth + 1)
    rc = [one] + [None] * depth
    pc = [one] + [None] * depth
    rr = quad(rc, rc)
    for _ in range(depth):
        moved = change(pc)
        alpha = rr / quad(pc, moved)
        xc = [plus(x, times(alpha, p)) for x, p in zip(xc, pc)]
        rc = [plus(r, times(-alpha, m)) for r, m in zip(rc, moved)]
        following = quad(rc, rc)
        beta = following / rr
        pc = [plus(r, times(beta, p)) for r, p in zip(rc, pc)]
        rr = following
    return xc, rc


CHUNK = 2


def final_body(sums, guess, t0, t1, t2, t3, t4, sol_hbm, res_hbm, sol, res, sems):
    nx = t0.shape[0]
    rows, cols = tiles(t0.shape)
    packed = tree([sums[pl.ds(n * SUB, SUB), :] for n in range(sums.shape[0] // SUB)])
    packed = jnp.sum(packed, axis=0, keepdims=True)
    q = [
        jnp.broadcast_to(packed[:, n : n + 1], (SUB, LANE))
        for n in range(2 * STEPS + 1)
    ]
    xc, rc = coefficients(q)
    basis = [t0, t1, t2, t3, t4]
    steps = nx // CHUNK

    def copies(step):
        block = pl.ds(step * CHUNK, CHUNK)
        return (
            pltpu.make_async_copy(sol.at[block], sol_hbm.at[block], sems.at[0, step]),
            pltpu.make_async_copy(res.at[block], res_hbm.at[block], sems.at[1, step]),
        )

    def step_body(step, carry):
        for u in range(CHUNK):
            i = step * CHUNK + u
            for j in range(rows):
                for c in range(cols):
                    place = (i, *at(j, c))
                    values = [b[place] for b in basis]
                    x, r = guess[place], None
                    for k in range(STEPS + 1):
                        if xc[k] is not None:
                            x = x + xc[k] * values[k]
                        term = rc[k] * values[k]
                        r = term if r is None else r + term
                    sol[place] = x
                    res[place] = r
        for copy in copies(step):
            copy.start()
        return carry

    lax.fori_loop(0, steps, step_body, 0)

    def wait_body(step, carry):
        for copy in copies(step):
            copy.wait()
        return carry

    lax.fori_loop(0, steps, wait_body, 0)


def all_sum(rows):
    parts = lax.all_to_all(rows[:, None, :], ("gx", "gy"), 0, 0)
    return parts[:, 0, :]


def fix(scale, t, halo):
    t, *faces = kernel(
        functools.partial(fix_body, scale),
        [f32(*t.shape)] + face_shapes(t),
        t,
        *halo,
        alias={0: 0},
    )
    return t, faces


def shards(right_side, guess, diagonal):
    devices = lax.axis_size("gx") * lax.axis_size("gy")
    size, block = guess.size, guess.shape
    strip = pltpu.VMEM((block[0], SUB, block[2]), jnp.float32)
    faces = kernel(
        faces_body,
        face_shapes(guess),
        pltpu.with_memory_space_constraint(guess, pltpu.HBM),
        specs=[hbm],
        scratch=[strip, strip, pltpu.SemaphoreType.DMA((4,))],
        flops=100000 * size,
    )
    guess, right_side, diagonal = (
        pltpu.with_memory_space_constraint(a, pltpu.VMEM)
        for a in (guess, right_side, diagonal)
    )
    halo = exchange(faces)
    (t,) = kernel(
        first_body, [f32(*block)], guess, right_side, diagonal, flops=20 * size
    )
    t, faces = fix(1.0, t, halo)
    basis, sums = [t], []
    for k in range(STEPS):
        halo = exchange(faces)
        last = k == STEPS - 1
        count = 1 if k == 0 else 4 if last else 2
        given = [basis[k], diagonal] if k == 0 else [basis[k], basis[k - 1], diagonal]
        t, s = kernel(
            functools.partial(next_body, k, last),
            [f32(*block), f32(count, SUB, LANE)],
            *given,
            flops=24 * size,
        )
        sums.append(s)
        scale = -1.0 / half_range if k == 0 else -2.0 / half_range
        if not last:
            t, faces = fix(scale, t, halo)
            basis.append(t)
    t4, rows = kernel(
        functools.partial(close_body, scale),
        [f32(*block), f32(devices, LANE)],
        t,
        basis[3],
        *halo,
        *sums,
        alias={0: 0},
    )
    return kernel(
        final_body,
        [f32(*block), f32(*block)],
        all_sum(rows),
        guess,
        *basis,
        t4,
        out_specs=[hbm] * 2,
        scratch=[
            pltpu.VMEM(block, jnp.float32),
            pltpu.VMEM(block, jnp.float32),
            pltpu.SemaphoreType.DMA((2, block[0] // CHUNK)),
        ],
    )


def solution(mesh):
    return jax.shard_map(
        shards,
        mesh=mesh,
        in_specs=(P("gx", "gy", None),) * 3,
        out_specs=(P("gx", "gy", None),) * 2,
        check_vma=False,
    )
```

```python
import functools

import jax
import jax.numpy as jnp
from jax import lax
from jax.experimental import pallas as pl
from jax.experimental.pallas import tpu as pltpu
from jax.sharding import PartitionSpec as P

STEPS = 4
SUB, LANE = 8, 128
center_shift = 6.25
half_range = 6.25
VMEM_LIMIT = 40 * 1024 * 1024

vmem = pl.BlockSpec(memory_space=pltpu.VMEM)
hbm = pl.BlockSpec(memory_space=pltpu.HBM)


def f32(*shape):
    return jax.ShapeDtypeStruct(shape, jnp.float32)


def kernel(body, outs, *args, specs=None, out_specs=None, scratch=(), alias=None, flops=0):
    size = sum(a.size * 4 for a in args) + sum(o.size * 4 for o in outs)
    return pl.pallas_call(
        body,
        out_shape=outs,
        in_specs=specs or [vmem] * len(args),
        out_specs=out_specs or [vmem] * len(outs),
        scratch_shapes=list(scratch),
        input_output_aliases=alias or {},
        compiler_params=pltpu.CompilerParams(vmem_limit_bytes=VMEM_LIMIT),
        cost_estimate=pl.CostEstimate(
            flops=flops, bytes_accessed=size, transcendentals=0
        ),
    )(*args)


def tree(values):
    while len(values) > 1:
        pairs = [a + b for a, b in zip(values[0::2], values[1::2])]
        values = pairs + ([values[-1]] if len(values) % 2 else [])
    return values[0]


def tiles(shape):
    return shape[1] // SUB, shape[2] // LANE


def layer(t_ref, i, below, above, emit, carry):
    rows, cols = tiles(t_ref.shape)
    sub = lax.broadcasted_iota(jnp.int32, (SUB, LANE), 0)
    lane = lax.broadcasted_iota(jnp.int32, (SUB, LANE), 1)
    first_sub, last_sub = sub == 0, sub == SUB - 1
    first_lane, last_lane = lane == 0, lane == LANE - 1

    def load(j, c, di=0):
        return t_ref[i + di, pl.ds(j * SUB, SUB), pl.ds(c * LANE, LANE)]

    zero = jnp.zeros((SUB, LANE), jnp.float32)
    now = [load(0, c) for c in range(cols)]
    fromlow = [zero] * cols
    for j in range(rows):
        after = [load(j + 1, c) for c in range(cols)] if j + 1 < rows else None
        right = [pltpu.roll(v, 1, 1) for v in now]
        left = [pltpu.roll(v, LANE - 1, 1) for v in now]
        down = [pltpu.roll(v, 1, 0) for v in now]
        for c in range(cols):
            up = pltpu.roll(now[c], SUB - 1, 0)
            nextup = pltpu.roll(after[c], SUB - 1, 0) if after is not None else zero
            s = jnp.where(first_sub, fromlow[c], down[c])
            s = s + jnp.where(last_sub, nextup, up)
            s = s + jnp.where(first_lane, right[c - 1] if c > 0 else zero, right[c])
            s = s + jnp.where(last_lane, left[c + 1] if c + 1 < cols else zero, left[c])
            if below:
                s = s + load(j, c, -1)
            if above:
                s = s + load(j, c, 1)
            carry = emit(i, j, c, now[c], s, carry)
        fromlow = down
        now = after
    return carry


def sweep(t_ref, emit, carry):
    nx = t_ref.shape[0]
    carry = layer(t_ref, 0, False, True, emit, carry)
    carry = lax.fori_loop(
        1, nx - 1, lambda i, a: layer(t_ref, i, True, True, emit, a), carry
    )
    return layer(t_ref, nx - 1, True, False, emit, carry)


def at(j, c):
    return pl.ds(j * SUB, SUB), pl.ds(c * LANE, LANE)


def swaps(count):
    near = [(i, i ^ 1) for i in range(count)]
    far = [(i, (i + 1) % count if i % 2 else (i - 1) % count) for i in range(count)]
    return near, far


def side(axis):
    index, count = lax.axis_index(axis), lax.axis_size(axis)
    odd = lax.rem(index, 2) == 1
    ends = jnp.logical_or(index == 0, index == count - 1)
    return odd, jnp.where(ends, 0.0, 1.0).astype(jnp.float32)


def exchange(faces):
    far_x, near_x, far_y, near_y = faces
    x, y = swaps(lax.axis_size("gx")), swaps(lax.axis_size("gy"))
    far_x = lax.ppermute(far_x, "gx", x[1])
    near_x = lax.ppermute(near_x, "gx", x[0])
    far_y = lax.ppermute(far_y, "gy", y[1])
    near_y = lax.ppermute(near_y, "gy", y[0])
    return far_x, near_x, far_y, near_y


def face_shapes(t):
    nx, ny, nz = t.shape
    return [f32(ny, nz), f32(ny, nz), f32(nx, nz), f32(nx, nz)]


def faces_body(field, far_x, near_x, far_y, near_y, low, high, sems):
    nx, ny, _ = field.shape
    odd_x, _ = side("gx")
    odd_y, _ = side("gy")
    near_layer = jnp.where(odd_x, 0, nx - 1)
    copies = [
        pltpu.make_async_copy(field.at[near_layer], near_x, sems.at[0]),
        pltpu.make_async_copy(field.at[nx - 1 - near_layer], far_x, sems.at[1]),
        pltpu.make_async_copy(field.at[:, pl.ds(0, SUB)], low, sems.at[2]),
        pltpu.make_async_copy(field.at[:, pl.ds(ny - SUB, SUB)], high, sems.at[3]),
    ]
    for copy in copies:
        copy.start()
    for copy in copies:
        copy.wait()
    for i in range(nx):
        first, last = low[i, 0:1, :], high[i, SUB - 1 : SUB, :]
        near_y[i : i + 1, :] = jnp.where(odd_y, first, last)
        far_y[i : i + 1, :] = jnp.where(odd_y, last, first)


def first_body(guess, right_side, diagonal, out):
    def emit(i, j, c, mid, beside, carry):
        place = (i, *at(j, c))
        applied = (6.0 + diagonal[place]) * mid - beside
        out[place] = right_side[place] - applied
        return carry

    sweep(guess, emit, 0)


def next_body(index, last, *refs):
    if index == 0:
        current, diagonal, out, sums = refs
    else:
        current, previous, diagonal, out, sums = refs
    scale = 1.0 / half_range if index == 0 else 2.0 / half_range
    zero = jnp.zeros((SUB, LANE), jnp.float32)
    count = sums.shape[0]

    def emit(i, j, c, mid, beside, carry):
        place = (i, *at(j, c))
        d = diagonal[place]
        value = scale * ((d + (6.0 - center_shift)) * mid - beside)
        added = [mid * mid]
        if index > 0:
            before = previous[place]
            value = value - before
            added.append(mid * before)
        if last:
            added += [mid * value, value * value]
        out[place] = value
        return tuple(a + b for a, b in zip(carry, added))

    total = sweep(current, emit, (zero,) * count)
    for n in range(count):
        sums[n] = total[n]


def add_edges(scale, t, halo, changed):
    far_x, near_x, far_y, near_y = halo
    nx, ny, _ = t.shape
    rows, cols = tiles(t.shape)
    sub = lax.broadcasted_iota(jnp.int32, (SUB, LANE), 0)
    odd_x, has_x = side("gx")
    odd_y, has_y = side("gy")
    near_layer = jnp.where(odd_x, 0, nx - 1)
    far_scale_x, far_scale_y = scale * has_x, scale * has_y

    for i, layer, factor, n in (
        (near_layer, near_x, scale, 0),
        (nx - 1 - near_layer, far_x, far_scale_x, 1),
    ):
        for j in range(rows):
            places = [(i, *at(j, c)) for c in range(cols)]
            olds = [t[place] for place in places]
            news = [old + factor * layer[at(j, c)] for c, old in enumerate(olds)]
            for c in range(cols):
                t[places[c]] = news[c]
            changed(places, olds, news)

    low_scale = jnp.where(odd_y, scale, far_scale_y)
    high_scale = jnp.where(odd_y, far_scale_y, scale)
    for i in range(nx):
        places, olds, news = [], [], []
        for c in range(cols):
            lanes = pl.ds(c * LANE, LANE)
            near, far = near_y[pl.ds(i, 1), lanes], far_y[pl.ds(i, 1), lanes]
            low = low_scale * jnp.where(odd_y, near, far)
            high = high_scale * jnp.where(odd_y, far, near)
            for j, row, value in ((0, 0, low), (rows - 1, SUB - 1, high)):
                place = (i, *at(j, c))
                old = t[place]
                places.append(place)
                olds.append(old)
                news.append(old + jnp.where(sub == row, value, 0.0))
        for place, new in zip(places, news):
            t[place] = new
        changed(places, olds, news)


def fix_body(scale, t_in, far_x, near_x, far_y, near_y, t, ffx, nfx, ffy, nfy):
    nx, ny, _ = t.shape
    odd_x, _ = side("gx")
    odd_y, _ = side("gy")
    add_edges(scale, t, (far_x, near_x, far_y, near_y), lambda *_: None)
    near_layer = jnp.where(odd_x, 0, nx - 1)
    nfx[...] = t[near_layer]
    ffx[...] = t[nx - 1 - near_layer]
    for i in range(nx):
        first, last = t[i, 0:1, :], t[i, ny - 1 : ny, :]
        nfy[i : i + 1, :] = jnp.where(odd_y, first, last)
        ffy[i : i + 1, :] = jnp.where(odd_y, last, first)


def close_body(scale, t_in, before, far_x, near_x, far_y, near_y, s0, s1, s2, s3, t, out):
    cross, square = [s3[2]], [s3[3]]

    def changed(places, olds, news):
        cross.append(
            tree([before[p] * (new - old) for p, old, new in zip(places, olds, news)])
        )
        square.append(tree([new * new - old * old for old, new in zip(olds, news)]))

    add_edges(scale, t, (far_x, near_x, far_y, near_y), changed)
    parts = [s0[0], s1[1], s1[0], s2[1], s2[0], s3[1], s3[0], tree(cross), tree(square)]
    lane = lax.broadcasted_iota(jnp.int32, (SUB, LANE), 1)
    packed = jnp.zeros((SUB, LANE), jnp.float32)
    for n, part in enumerate(parts):
        total = jnp.sum(part, axis=1, keepdims=True)
        packed = jnp.where(lane == n, total, packed)
    packed = jnp.sum(packed, axis=0, keepdims=True)
    out[...] = jnp.broadcast_to(packed, out.shape)


def coefficients(q):
    depth = STEPS
    moment = [None] * (2 * depth + 1)
    moment[0], moment[1] = q[0], q[1]
    for n in range(2, 2 * depth + 1):
        moment[n] = 2.0 * q[n] - moment[n % 2]
    gram = [
        [
            q[i + j] if abs(i - j) < 2 else 0.5 * (moment[i + j] + moment[abs(i - j)])
            for j in range(depth + 1)
        ]
        for i in range(depth + 1)
    ]

    def plus(a, b):
        return b if a is None else a if b is None else a + b

    def times(a, b):
        return None if a is None or b is None else a * b

    def change(v):
        moved = [None] * (depth + 1)
        for k in range(depth):
            if k == 0:
                entries = {0: center_shift, 1: half_range}
            else:
                entries = {
                    k - 1: half_range / 2.0,
                    k: center_shift,
                    k + 1: half_range / 2.0,
                }
            for i, value in entries.items():
                moved[i] = plus(moved[i], times(value, v[k]))
        return moved

    def quad(left, right):
        total = None
        for i in range(depth + 1):
            inner = None
            for j in range(depth + 1):
                inner = plus(inner, times(gram[i][j], right[j]))
            total = plus(total, times(left[i], inner))
        return total

    one = jnp.ones_like(q[0])
    xc = [None] * (depth + 1)
    rc = [one] + [None] * depth
    pc = [one] + [None] * depth
    rr = quad(rc, rc)
    for _ in range(depth):
        moved = change(pc)
        alpha = rr / quad(pc, moved)
        xc = [plus(x, times(alpha, p)) for x, p in zip(xc, pc)]
        rc = [plus(r, times(-alpha, m)) for r, m in zip(rc, moved)]
        following = quad(rc, rc)
        beta = following / rr
        pc = [plus(r, times(beta, p)) for r, p in zip(rc, pc)]
        rr = following
    return xc, rc


CHUNK = 2


def final_body(sums, guess, t0, t1, t2, t3, t4, sol_hbm, res_hbm, sol, res, sems):
    nx = t0.shape[0]
    rows, cols = tiles(t0.shape)
    packed = tree([sums[pl.ds(n * SUB, SUB), :] for n in range(sums.shape[0] // SUB)])
    packed = jnp.sum(packed, axis=0, keepdims=True)
    q = [
        jnp.broadcast_to(packed[:, n : n + 1], (SUB, LANE))
        for n in range(2 * STEPS + 1)
    ]
    xc, rc = coefficients(q)
    basis = [t0, t1, t2, t3, t4]
    steps = nx // CHUNK

    def copies(step):
        block = pl.ds(step * CHUNK, CHUNK)
        return (
            pltpu.make_async_copy(sol.at[block], sol_hbm.at[block], sems.at[0, step]),
            pltpu.make_async_copy(res.at[block], res_hbm.at[block], sems.at[1, step]),
        )

    def step_body(step, carry):
        for u in range(CHUNK):
            i = step * CHUNK + u
            for j in range(rows):
                for c in range(cols):
                    place = (i, *at(j, c))
                    values = [b[place] for b in basis]
                    x, r = guess[place], None
                    for k in range(STEPS + 1):
                        if xc[k] is not None:
                            x = x + xc[k] * values[k]
                        term = rc[k] * values[k]
                        r = term if r is None else r + term
                    sol[place] = x
                    res[place] = r
        for copy in copies(step):
            copy.start()
        return carry

    lax.fori_loop(0, steps, step_body, 0)

    def wait_body(step, carry):
        for copy in copies(step):
            copy.wait()
        return carry

    lax.fori_loop(0, steps, wait_body, 0)


def all_sum(rows):
    parts = lax.all_to_all(rows[:, None, :], ("gx", "gy"), 0, 0)
    return parts[:, 0, :]


def fix(scale, t, halo):
    t, *faces = kernel(
        functools.partial(fix_body, scale),
        [f32(*t.shape)] + face_shapes(t),
        t,
        *halo,
        alias={0: 0},
    )
    return t, faces


def shards(right_side, guess, diagonal):
    devices = lax.axis_size("gx") * lax.axis_size("gy")
    size, block = guess.size, guess.shape
    strip = pltpu.VMEM((block[0], SUB, block[2]), jnp.float32)
    faces = kernel(
        faces_body,
        face_shapes(guess),
        pltpu.with_memory_space_constraint(guess, pltpu.HBM),
        specs=[hbm],
        scratch=[strip, strip, pltpu.SemaphoreType.DMA((4,))],
        flops=100000 * size,
    )
    guess, right_side, diagonal = (
        pltpu.with_memory_space_constraint(a, pltpu.VMEM)
        for a in (guess, right_side, diagonal)
    )
    halo = exchange(faces)
    (t,) = kernel(
        first_body, [f32(*block)], guess, right_side, diagonal, flops=20 * size
    )
    t, faces = fix(1.0, t, halo)
    basis, sums = [t], []
    for k in range(STEPS):
        halo = exchange(faces)
        last = k == STEPS - 1
        count = 1 if k == 0 else 4 if last else 2
        given = [basis[k], diagonal] if k == 0 else [basis[k], basis[k - 1], diagonal]
        t, s = kernel(
            functools.partial(next_body, k, last),
            [f32(*block), f32(count, SUB, LANE)],
            *given,
            flops=24 * size,
        )
        sums.append(s)
        scale = -1.0 / half_range if k == 0 else -2.0 / half_range
        if not last:
            t, faces = fix(scale, t, halo)
            basis.append(t)
    t4, rows = kernel(
        functools.partial(close_body, scale),
        [f32(*block), f32(devices, LANE)],
        t,
        basis[3],
        *halo,
        *sums,
        alias={0: 0},
    )
    return kernel(
        final_body,
        [f32(*block), f32(*block)],
        all_sum(rows),
        guess,
        *basis,
        t4,
        out_specs=[hbm] * 2,
        scratch=[
            pltpu.VMEM(block, jnp.float32),
            pltpu.VMEM(block, jnp.float32),
            pltpu.SemaphoreType.DMA((2, block[0] // CHUNK)),
        ],
    )


def solution(mesh):
    return jax.shard_map(
        shards,
        mesh=mesh,
        in_specs=(P("gx", "gy", None),) * 3,
        out_specs=(P("gx", "gy", None),) * 2,
        check_vma=False,
    )
```

```python
import functools

import jax
import jax.numpy as jnp
from jax import lax
from jax.experimental import pallas as pl
from jax.experimental.pallas import tpu as pltpu
from jax.sharding import PartitionSpec as P

STEPS = 4
SUB, LANE = 8, 128
center_shift = 6.25
half_range = 6.25
VMEM_LIMIT = 40 * 1024 * 1024

vmem = pl.BlockSpec(memory_space=pltpu.VMEM)
hbm = pl.BlockSpec(memory_space=pltpu.HBM)


def f32(*shape):
    return jax.ShapeDtypeStruct(shape, jnp.float32)


def kernel(body, outs, *args, specs=None, out_specs=None, scratch=(), alias=None, flops=0):
    size = sum(a.size * 4 for a in args) + sum(o.size * 4 for o in outs)
    return pl.pallas_call(
        body,
        out_shape=outs,
        in_specs=specs or [vmem] * len(args),
        out_specs=out_specs or [vmem] * len(outs),
        scratch_shapes=list(scratch),
        input_output_aliases=alias or {},
        compiler_params=pltpu.CompilerParams(vmem_limit_bytes=VMEM_LIMIT),
        cost_estimate=pl.CostEstimate(
            flops=flops, bytes_accessed=size, transcendentals=0
        ),
    )(*args)


def tree(values):
    while len(values) > 1:
        pairs = [a + b for a, b in zip(values[0::2], values[1::2])]
        values = pairs + ([values[-1]] if len(values) % 2 else [])
    return values[0]


def tiles(shape):
    return shape[1] // SUB, shape[2] // LANE


def layer(t_ref, i, below, above, emit, carry):
    rows, cols = tiles(t_ref.shape)
    sub = lax.broadcasted_iota(jnp.int32, (SUB, LANE), 0)
    lane = lax.broadcasted_iota(jnp.int32, (SUB, LANE), 1)
    first_sub, last_sub = sub == 0, sub == SUB - 1
    first_lane, last_lane = lane == 0, lane == LANE - 1

    def load(j, c, di=0):
        return t_ref[i + di, pl.ds(j * SUB, SUB), pl.ds(c * LANE, LANE)]

    zero = jnp.zeros((SUB, LANE), jnp.float32)
    now = [load(0, c) for c in range(cols)]
    fromlow = [zero] * cols
    for j in range(rows):
        after = [load(j + 1, c) for c in range(cols)] if j + 1 < rows else None
        right = [pltpu.roll(v, 1, 1) for v in now]
        left = [pltpu.roll(v, LANE - 1, 1) for v in now]
        down = [pltpu.roll(v, 1, 0) for v in now]
        for c in range(cols):
            up = pltpu.roll(now[c], SUB - 1, 0)
            nextup = pltpu.roll(after[c], SUB - 1, 0) if after is not None else zero
            s = jnp.where(first_sub, fromlow[c], down[c])
            s = s + jnp.where(last_sub, nextup, up)
            s = s + jnp.where(first_lane, right[c - 1] if c > 0 else zero, right[c])
            s = s + jnp.where(last_lane, left[c + 1] if c + 1 < cols else zero, left[c])
            if below:
                s = s + load(j, c, -1)
            if above:
                s = s + load(j, c, 1)
            carry = emit(i, j, c, now[c], s, carry)
        fromlow = down
        now = after
    return carry


def sweep(t_ref, emit, carry):
    nx = t_ref.shape[0]
    carry = layer(t_ref, 0, False, True, emit, carry)
    carry = lax.fori_loop(
        1, nx - 1, lambda i, a: layer(t_ref, i, True, True, emit, a), carry
    )
    return layer(t_ref, nx - 1, True, False, emit, carry)


def at(j, c):
    return pl.ds(j * SUB, SUB), pl.ds(c * LANE, LANE)


def swaps(nx, ny):
    def pairs(partner):
        return [
            (i * ny + j, x * ny + y)
            for i in range(nx)
            for j in range(ny)
            for x, y in [partner(i, j)]
        ]

    def far(i):
        return i + 1 if i % 2 else i - 1

    return (
        pairs(lambda i, j: (far(i), j) if 0 < i < nx - 1 else (i, j ^ 1)),
        pairs(lambda i, j: (i ^ 1, j)),
        pairs(lambda i, j: (i, far(j)) if 0 < j < ny - 1 else (i ^ 1, j)),
        pairs(lambda i, j: (i, j ^ 1)),
    )


def side(axis):
    index, count = lax.axis_index(axis), lax.axis_size(axis)
    odd = lax.rem(index, 2) == 1
    ends = jnp.logical_or(index == 0, index == count - 1)
    return odd, jnp.where(ends, 0.0, 1.0).astype(jnp.float32)


def exchange(faces):
    perms = swaps(lax.axis_size("gx"), lax.axis_size("gy"))
    return [lax.ppermute(f, ("gx", "gy"), perm) for f, perm in zip(faces, perms)]


def face_shapes(t):
    nx, ny, nz = t.shape
    return [f32(ny, nz), f32(ny, nz), f32(nx, nz), f32(nx, nz)]


def x_faces_body(field, far_x, near_x, sems):
    nx = field.shape[0]
    odd_x, _ = side("gx")
    near_layer = jnp.where(odd_x, 0, nx - 1)
    copies = [
        pltpu.make_async_copy(field.at[nx - 1 - near_layer], far_x, sems.at[0]),
        pltpu.make_async_copy(field.at[near_layer], near_x, sems.at[1]),
    ]
    for copy in copies:
        copy.start()
    for copy in copies:
        copy.wait()


def y_faces_body(field, far_y, near_y, low, high, sems):
    nx, ny, _ = field.shape
    odd_y, _ = side("gy")
    copies = [
        pltpu.make_async_copy(field.at[:, pl.ds(0, SUB)], low, sems.at[0]),
        pltpu.make_async_copy(field.at[:, pl.ds(ny - SUB, SUB)], high, sems.at[1]),
    ]
    for copy in copies:
        copy.start()
    for copy in copies:
        copy.wait()
    for i in range(nx):
        first, last = low[i, 0:1, :], high[i, SUB - 1 : SUB, :]
        near_y[i : i + 1, :] = jnp.where(odd_y, first, last)
        far_y[i : i + 1, :] = jnp.where(odd_y, last, first)


def first_body(guess, right_side, diagonal, out):
    def emit(i, j, c, mid, beside, carry):
        place = (i, *at(j, c))
        applied = (6.0 + diagonal[place]) * mid - beside
        out[place] = right_side[place] - applied
        return carry

    sweep(guess, emit, 0)


def next_body(index, last, *refs):
    if index == 0:
        current, diagonal, out, sums = refs
    else:
        current, previous, diagonal, out, sums = refs
    scale = 1.0 / half_range if index == 0 else 2.0 / half_range
    zero = jnp.zeros((SUB, LANE), jnp.float32)
    count = sums.shape[0]

    def emit(i, j, c, mid, beside, carry):
        place = (i, *at(j, c))
        d = diagonal[place]
        value = scale * ((d + (6.0 - center_shift)) * mid - beside)
        added = [mid * mid]
        if index > 0:
            before = previous[place]
            value = value - before
            added.append(mid * before)
        if last:
            added += [mid * value, value * value]
        out[place] = value
        return tuple(a + b for a, b in zip(carry, added))

    total = sweep(current, emit, (zero,) * count)
    for n in range(count):
        sums[n] = total[n]


def add_edges(scale, t, halo, changed):
    far_x, near_x, far_y, near_y = halo
    nx, ny, _ = t.shape
    rows, cols = tiles(t.shape)
    sub = lax.broadcasted_iota(jnp.int32, (SUB, LANE), 0)
    odd_x, has_x = side("gx")
    odd_y, has_y = side("gy")
    near_layer = jnp.where(odd_x, 0, nx - 1)
    far_scale_x, far_scale_y = scale * has_x, scale * has_y

    for i, layer, factor, n in (
        (near_layer, near_x, scale, 0),
        (nx - 1 - near_layer, far_x, far_scale_x, 1),
    ):
        for j in range(rows):
            places = [(i, *at(j, c)) for c in range(cols)]
            olds = [t[place] for place in places]
            news = [old + factor * layer[at(j, c)] for c, old in enumerate(olds)]
            for c in range(cols):
                t[places[c]] = news[c]
            changed(places, olds, news)

    low_scale = jnp.where(odd_y, scale, far_scale_y)
    high_scale = jnp.where(odd_y, far_scale_y, scale)
    for i in range(nx):
        places, olds, news = [], [], []
        for c in range(cols):
            lanes = pl.ds(c * LANE, LANE)
            near, far = near_y[pl.ds(i, 1), lanes], far_y[pl.ds(i, 1), lanes]
            low = low_scale * jnp.where(odd_y, near, far)
            high = high_scale * jnp.where(odd_y, far, near)
            for j, row, value in ((0, 0, low), (rows - 1, SUB - 1, high)):
                place = (i, *at(j, c))
                old = t[place]
                places.append(place)
                olds.append(old)
                news.append(old + jnp.where(sub == row, value, 0.0))
        for place, new in zip(places, news):
            t[place] = new
        changed(places, olds, news)


def fix_body(scale, t_in, far_x, near_x, far_y, near_y, t, ffx, nfx, ffy, nfy):
    nx, ny, _ = t.shape
    odd_x, _ = side("gx")
    odd_y, _ = side("gy")
    add_edges(scale, t, (far_x, near_x, far_y, near_y), lambda *_: None)
    near_layer = jnp.where(odd_x, 0, nx - 1)
    nfx[...] = t[near_layer]
    ffx[...] = t[nx - 1 - near_layer]
    for i in range(nx):
        first, last = t[i, 0:1, :], t[i, ny - 1 : ny, :]
        nfy[i : i + 1, :] = jnp.where(odd_y, first, last)
        ffy[i : i + 1, :] = jnp.where(odd_y, last, first)


def close_body(scale, t_in, before, far_x, near_x, far_y, near_y, s0, s1, s2, s3, t, out):
    cross, square = [s3[2]], [s3[3]]

    def changed(places, olds, news):
        cross.append(
            tree([before[p] * (new - old) for p, old, new in zip(places, olds, news)])
        )
        square.append(tree([new * new - old * old for old, new in zip(olds, news)]))

    add_edges(scale, t, (far_x, near_x, far_y, near_y), changed)
    parts = [s0[0], s1[1], s1[0], s2[1], s2[0], s3[1], s3[0], tree(cross), tree(square)]
    lane = lax.broadcasted_iota(jnp.int32, (SUB, LANE), 1)
    packed = jnp.zeros((SUB, LANE), jnp.float32)
    for n, part in enumerate(parts):
        total = jnp.sum(part, axis=1, keepdims=True)
        packed = jnp.where(lane == n, total, packed)
    packed = jnp.sum(packed, axis=0, keepdims=True)
    out[...] = jnp.broadcast_to(packed, out.shape)


def coefficients(q):
    depth = STEPS
    moment = [None] * (2 * depth + 1)
    moment[0], moment[1] = q[0], q[1]
    for n in range(2, 2 * depth + 1):
        moment[n] = 2.0 * q[n] - moment[n % 2]
    gram = [
        [
            q[i + j] if abs(i - j) < 2 else 0.5 * (moment[i + j] + moment[abs(i - j)])
            for j in range(depth + 1)
        ]
        for i in range(depth + 1)
    ]

    def plus(a, b):
        return b if a is None else a if b is None else a + b

    def times(a, b):
        return None if a is None or b is None else a * b

    def change(v):
        moved = [None] * (depth + 1)
        for k in range(depth):
            if k == 0:
                entries = {0: center_shift, 1: half_range}
            else:
                entries = {
                    k - 1: half_range / 2.0,
                    k: center_shift,
                    k + 1: half_range / 2.0,
                }
            for i, value in entries.items():
                moved[i] = plus(moved[i], times(value, v[k]))
        return moved

    def quad(left, right):
        total = None
        for i in range(depth + 1):
            inner = None
            for j in range(depth + 1):
                inner = plus(inner, times(gram[i][j], right[j]))
            total = plus(total, times(left[i], inner))
        return total

    one = jnp.ones_like(q[0])
    xc = [None] * (depth + 1)
    rc = [one] + [None] * depth
    pc = [one] + [None] * depth
    rr = quad(rc, rc)
    for _ in range(depth):
        moved = change(pc)
        alpha = rr / quad(pc, moved)
        xc = [plus(x, times(alpha, p)) for x, p in zip(xc, pc)]
        rc = [plus(r, times(-alpha, m)) for r, m in zip(rc, moved)]
        following = quad(rc, rc)
        beta = following / rr
        pc = [plus(r, times(beta, p)) for r, p in zip(rc, pc)]
        rr = following
    return xc, rc


CHUNK = 2


def final_body(sums, guess, t0, t1, t2, t3, t4, sol_hbm, res_hbm, sol, res, sems):
    nx = t0.shape[0]
    rows, cols = tiles(t0.shape)
    packed = tree([sums[pl.ds(n * SUB, SUB), :] for n in range(sums.shape[0] // SUB)])
    packed = jnp.sum(packed, axis=0, keepdims=True)
    q = [
        jnp.broadcast_to(packed[:, n : n + 1], (SUB, LANE))
        for n in range(2 * STEPS + 1)
    ]
    xc, rc = coefficients(q)
    basis = [t0, t1, t2, t3, t4]
    steps = nx // CHUNK

    def copies(step):
        block = pl.ds(step * CHUNK, CHUNK)
        return (
            pltpu.make_async_copy(sol.at[block], sol_hbm.at[block], sems.at[0, step]),
            pltpu.make_async_copy(res.at[block], res_hbm.at[block], sems.at[1, step]),
        )

    def step_body(step, carry):
        for u in range(CHUNK):
            i = step * CHUNK + u
            for j in range(rows):
                for c in range(cols):
                    place = (i, *at(j, c))
                    values = [b[place] for b in basis]
                    x, r = guess[place], None
                    for k in range(STEPS + 1):
                        if xc[k] is not None:
                            x = x + xc[k] * values[k]
                        term = rc[k] * values[k]
                        r = term if r is None else r + term
                    sol[place] = x
                    res[place] = r
        for copy in copies(step):
            copy.start()
        return carry

    lax.fori_loop(0, steps, step_body, 0)

    def wait_body(step, carry):
        for copy in copies(step):
            copy.wait()
        return carry

    lax.fori_loop(0, steps, wait_body, 0)


def all_sum(rows):
    parts = lax.all_to_all(rows[:, None, :], ("gx", "gy"), 0, 0)
    return parts[:, 0, :]


def fix(scale, t, halo):
    t, *faces = kernel(
        functools.partial(fix_body, scale),
        [f32(*t.shape)] + face_shapes(t),
        t,
        *halo,
        alias={0: 0},
    )
    return t, faces


def shards(right_side, guess, diagonal):
    devices = lax.axis_size("gx") * lax.axis_size("gy")
    size, block = guess.size, guess.shape
    strip = pltpu.VMEM((block[0], SUB, block[2]), jnp.float32)
    source = pltpu.with_memory_space_constraint(guess, pltpu.HBM)
    shapes = face_shapes(guess)
    faces = kernel(
        x_faces_body,
        shapes[:2],
        source,
        specs=[hbm],
        scratch=[pltpu.SemaphoreType.DMA((2,))],
        flops=100000 * size,
    ) + kernel(
        y_faces_body,
        shapes[2:],
        source,
        specs=[hbm],
        scratch=[strip, strip, pltpu.SemaphoreType.DMA((2,))],
        flops=1000 * size,
    )
    guess, right_side, diagonal = (
        pltpu.with_memory_space_constraint(a, pltpu.VMEM)
        for a in (guess, right_side, diagonal)
    )
    halo = exchange(faces)
    (t,) = kernel(
        first_body, [f32(*block)], guess, right_side, diagonal, flops=20 * size
    )
    t, faces = fix(1.0, t, halo)
    basis, sums = [t], []
    for k in range(STEPS):
        halo = exchange(faces)
        last = k == STEPS - 1
        count = 1 if k == 0 else 4 if last else 2
        given = [basis[k], diagonal] if k == 0 else [basis[k], basis[k - 1], diagonal]
        t, s = kernel(
            functools.partial(next_body, k, last),
            [f32(*block), f32(count, SUB, LANE)],
            *given,
            flops=24 * size,
        )
        sums.append(s)
        scale = -1.0 / half_range if k == 0 else -2.0 / half_range
        if not last:
            t, faces = fix(scale, t, halo)
            basis.append(t)
    t4, rows = kernel(
        functools.partial(close_body, scale),
        [f32(*block), f32(devices, LANE)],
        t,
        basis[3],
        *halo,
        *sums,
        alias={0: 0},
    )
    return kernel(
        final_body,
        [f32(*block), f32(*block)],
        all_sum(rows),
        guess,
        *basis,
        t4,
        out_specs=[hbm] * 2,
        scratch=[
            pltpu.VMEM(block, jnp.float32),
            pltpu.VMEM(block, jnp.float32),
            pltpu.SemaphoreType.DMA((2, block[0] // CHUNK)),
        ],
    )


def solution(mesh):
    return jax.shard_map(
        shards,
        mesh=mesh,
        in_specs=(P("gx", "gy", None),) * 3,
        out_specs=(P("gx", "gy", None),) * 2,
        check_vma=False,
    )
```

```python
import functools

import jax
import jax.numpy as jnp
from jax import lax
from jax.experimental import pallas as pl
from jax.experimental.pallas import tpu as pltpu
from jax.sharding import PartitionSpec as P

STEPS = 4
SUB, LANE = 8, 128
center_shift = 6.25
half_range = 6.25
VMEM_LIMIT = 40 * 1024 * 1024

vmem = pl.BlockSpec(memory_space=pltpu.VMEM)
hbm = pl.BlockSpec(memory_space=pltpu.HBM)


def f32(*shape):
    return jax.ShapeDtypeStruct(shape, jnp.float32)


def kernel(body, outs, *args, specs=None, out_specs=None, scratch=(), alias=None, flops=0):
    size = sum(a.size * 4 for a in args) + sum(o.size * 4 for o in outs)
    return pl.pallas_call(
        body,
        out_shape=outs,
        in_specs=specs or [vmem] * len(args),
        out_specs=out_specs or [vmem] * len(outs),
        scratch_shapes=list(scratch),
        input_output_aliases=alias or {},
        compiler_params=pltpu.CompilerParams(vmem_limit_bytes=VMEM_LIMIT),
        cost_estimate=pl.CostEstimate(
            flops=flops, bytes_accessed=size, transcendentals=0
        ),
    )(*args)


def tree(values):
    while len(values) > 1:
        pairs = [a + b for a, b in zip(values[0::2], values[1::2])]
        values = pairs + ([values[-1]] if len(values) % 2 else [])
    return values[0]


def tiles(shape):
    return shape[1] // SUB, shape[2] // LANE


def layer(t_ref, i, below, above, emit, carry):
    rows, cols = tiles(t_ref.shape)
    sub = lax.broadcasted_iota(jnp.int32, (SUB, LANE), 0)
    lane = lax.broadcasted_iota(jnp.int32, (SUB, LANE), 1)
    first_sub, last_sub = sub == 0, sub == SUB - 1
    first_lane, last_lane = lane == 0, lane == LANE - 1

    def load(j, c, di=0):
        return t_ref[i + di, pl.ds(j * SUB, SUB), pl.ds(c * LANE, LANE)]

    zero = jnp.zeros((SUB, LANE), jnp.float32)
    now = [load(0, c) for c in range(cols)]
    fromlow = [zero] * cols
    for j in range(rows):
        after = [load(j + 1, c) for c in range(cols)] if j + 1 < rows else None
        right = [pltpu.roll(v, 1, 1) for v in now]
        left = [pltpu.roll(v, LANE - 1, 1) for v in now]
        down = [pltpu.roll(v, 1, 0) for v in now]
        for c in range(cols):
            up = pltpu.roll(now[c], SUB - 1, 0)
            nextup = pltpu.roll(after[c], SUB - 1, 0) if after is not None else zero
            s = jnp.where(first_sub, fromlow[c], down[c])
            s = s + jnp.where(last_sub, nextup, up)
            s = s + jnp.where(first_lane, right[c - 1] if c > 0 else zero, right[c])
            s = s + jnp.where(last_lane, left[c + 1] if c + 1 < cols else zero, left[c])
            if below:
                s = s + load(j, c, -1)
            if above:
                s = s + load(j, c, 1)
            carry = emit(i, j, c, now[c], s, carry)
        fromlow = down
        now = after
    return carry


def sweep(t_ref, emit, carry):
    nx = t_ref.shape[0]
    carry = layer(t_ref, 0, False, True, emit, carry)
    carry = lax.fori_loop(
        1, nx - 1, lambda i, a: layer(t_ref, i, True, True, emit, a), carry
    )
    return layer(t_ref, nx - 1, True, False, emit, carry)


def at(j, c):
    return pl.ds(j * SUB, SUB), pl.ds(c * LANE, LANE)


def swaps(nx, ny):
    def pairs(partner):
        return [
            (i * ny + j, x * ny + y)
            for i in range(nx)
            for j in range(ny)
            for x, y in [partner(i, j)]
        ]

    def far(i):
        return i + 1 if i % 2 else i - 1

    return (
        pairs(lambda i, j: (far(i), j) if 0 < i < nx - 1 else (i, j ^ 1)),
        pairs(lambda i, j: (i ^ 1, j)),
        pairs(lambda i, j: (i, far(j)) if 0 < j < ny - 1 else (i ^ 1, j)),
        pairs(lambda i, j: (i, j ^ 1)),
    )


def side(axis):
    index, count = lax.axis_index(axis), lax.axis_size(axis)
    odd = lax.rem(index, 2) == 1
    ends = jnp.logical_or(index == 0, index == count - 1)
    return odd, jnp.where(ends, 0.0, 1.0).astype(jnp.float32)


def exchange(faces, which=range(4)):
    perms = swaps(lax.axis_size("gx"), lax.axis_size("gy"))
    return [lax.ppermute(f, ("gx", "gy"), perms[n]) for f, n in zip(faces, which)]


def face_shapes(t, *depth):
    nx, ny, nz = t.shape
    return [f32(*depth, ny, nz)] * 2 + [f32(*depth, nx, nz)] * 2


def x_faces_body(field, far_x, near_x, sems):
    nx = field.shape[0]
    odd_x, _ = side("gx")
    near_layer = jnp.where(odd_x, 0, nx - 1)
    copies = [
        pltpu.make_async_copy(field.at[nx - 1 - near_layer], far_x, sems.at[0]),
        pltpu.make_async_copy(field.at[near_layer], near_x, sems.at[1]),
    ]
    for copy in copies:
        copy.start()
    for copy in copies:
        copy.wait()


def y_faces_body(field, far_y, near_y, low, high, sems):
    nx, ny, _ = field.shape
    odd_y, _ = side("gy")
    copies = [
        pltpu.make_async_copy(field.at[:, pl.ds(0, SUB)], low, sems.at[0]),
        pltpu.make_async_copy(field.at[:, pl.ds(ny - SUB, SUB)], high, sems.at[1]),
    ]
    for copy in copies:
        copy.start()
    for copy in copies:
        copy.wait()
    for i in range(nx):
        first, last = low[i, 0:1, :], high[i, SUB - 1 : SUB, :]
        near_y[i : i + 1, :] = jnp.where(odd_y, first, last)
        far_y[i : i + 1, :] = jnp.where(odd_y, last, first)


def first_body(guess, right_side, diagonal, out):
    def emit(i, j, c, mid, beside, carry):
        place = (i, *at(j, c))
        applied = (6.0 + diagonal[place]) * mid - beside
        out[place] = right_side[place] - applied
        return carry

    sweep(guess, emit, 0)


def next_body(index, *refs):
    if index == 0:
        current, diagonal = refs[:2]
    else:
        current, previous, diagonal = refs[:3]
    out, sums = refs[-2:]
    scale = 1.0 / half_range if index == 0 else 2.0 / half_range
    zero = jnp.zeros((SUB, LANE), jnp.float32)
    count = sums.shape[0]

    def emit(i, j, c, mid, beside, carry):
        place = (i, *at(j, c))
        d = diagonal[place]
        value = scale * ((d + (6.0 - center_shift)) * mid - beside)
        added = [mid * mid]
        if index > 0:
            before = previous[place]
            value = value - before
            added.append(mid * before)
        out[place] = value
        return tuple(a + b for a, b in zip(carry, added))

    total = sweep(current, emit, (zero,) * count)
    for n in range(count):
        sums[n] = total[n]


def add_edges(scale, t, halo):
    far_x, near_x, far_y, near_y = halo
    nx, ny, _ = t.shape
    rows, cols = tiles(t.shape)
    sub = lax.broadcasted_iota(jnp.int32, (SUB, LANE), 0)
    odd_x, has_x = side("gx")
    odd_y, has_y = side("gy")
    near_layer = jnp.where(odd_x, 0, nx - 1)
    far_scale_x, far_scale_y = scale * has_x, scale * has_y

    for i, layer, factor, n in (
        (near_layer, near_x, scale, 0),
        (nx - 1 - near_layer, far_x, far_scale_x, 1),
    ):
        for j in range(rows):
            places = [(i, *at(j, c)) for c in range(cols)]
            olds = [t[place] for place in places]
            news = [old + factor * layer[at(j, c)] for c, old in enumerate(olds)]
            for c in range(cols):
                t[places[c]] = news[c]

    low_scale = jnp.where(odd_y, scale, far_scale_y)
    high_scale = jnp.where(odd_y, far_scale_y, scale)
    for i in range(nx):
        places, olds, news = [], [], []
        for c in range(cols):
            lanes = pl.ds(c * LANE, LANE)
            near, far = near_y[pl.ds(i, 1), lanes], far_y[pl.ds(i, 1), lanes]
            low = low_scale * jnp.where(odd_y, near, far)
            high = high_scale * jnp.where(odd_y, far, near)
            for j, row, value in ((0, 0, low), (rows - 1, SUB - 1, high)):
                place = (i, *at(j, c))
                old = t[place]
                places.append(place)
                olds.append(old)
                news.append(old + jnp.where(sub == row, value, 0.0))
        for place, new in zip(places, news):
            t[place] = new


def fix_body(scale, t_in, far_x, near_x, far_y, near_y, *refs):
    t, ffx, nfx, ffy, nfy = refs[-5:]
    add_edges(scale, t, (far_x, near_x, first_of(far_y), first_of(near_y)))
    if len(refs) == 6:
        write_faces(t, ffx, nfx, ffy.at[0], nfy.at[0])
        write_rows(refs[0], 0, ffy.at[1], nfy.at[1])
    else:
        write_faces(t, ffx, nfx, ffy, nfy)


def first_of(ref):
    return ref.at[0] if len(ref.shape) == 3 else ref


def write_rows(t, n, far_row, near_row):
    nx, ny, _ = t.shape
    odd_y, _ = side("gy")
    for i in range(nx):
        first, last = t[i, n : n + 1, :], t[i, ny - 1 - n : ny - n, :]
        near_row[i : i + 1, :] = jnp.where(odd_y, first, last)
        far_row[i : i + 1, :] = jnp.where(odd_y, last, first)


def write_faces(t, ffx, nfx, ffy, nfy):
    nx = t.shape[0]
    odd_x, _ = side("gx")
    for n in range(1 if len(ffx.shape) == 2 else ffx.shape[0]):
        views = [r.at[n] if len(r.shape) == 3 else r for r in (ffx, nfx, ffy, nfy)]
        far_layer, near_layer, far_row, near_row = views
        place = jnp.where(odd_x, n, nx - 1 - n)
        near_layer[...] = t[place]
        far_layer[...] = t[nx - 1 - place]
        write_rows(t, n, far_row, near_row)


def diagonal_x_body(diagonal, after, far, near):
    nx = diagonal.shape[0]
    odd_x, _ = side("gx")
    place = jnp.where(odd_x, 0, nx - 1)
    near[...] = diagonal[place]
    far[...] = diagonal[nx - 1 - place]


def corner_body(far_y, near_y, far, near):
    nx = far_y.shape[1]
    odd_x, _ = side("gx")
    near[...] = jnp.zeros_like(near)
    far[...] = jnp.zeros_like(far)
    for n, line in enumerate((near_y, far_y)):
        first, last = line[0, 0:1, :], line[0, nx - 1 : nx, :]
        near[n : n + 1, :] = jnp.where(odd_x, first, last)
        far[n : n + 1, :] = jnp.where(odd_x, last, first)


def plane(tile, shape, low, high, others, emit, carry, wanted):
    rows, cols = shape
    sub = lax.broadcasted_iota(jnp.int32, (SUB, LANE), 0)
    lane = lax.broadcasted_iota(jnp.int32, (SUB, LANE), 1)
    zero = jnp.zeros((SUB, LANE), jnp.float32)
    for j in wanted:
        mids = [tile(j, c) for c in range(cols)]
        right = [pltpu.roll(v, 1, 1) for v in mids]
        left = [pltpu.roll(v, LANE - 1, 1) for v in mids]
        for c, mid in enumerate(mids):
            before = pltpu.roll(tile(j - 1, c), 1, 0) if j > 0 else low(c)
            after = pltpu.roll(tile(j + 1, c), SUB - 1, 0) if j + 1 < rows else high(c)
            terms = [
                jnp.where(sub == 0, before, pltpu.roll(mid, 1, 0)),
                jnp.where(sub == SUB - 1, after, pltpu.roll(mid, SUB - 1, 0)),
                jnp.where(lane == 0, right[c - 1] if c > 0 else zero, right[c]),
                jnp.where(
                    lane == LANE - 1, left[c + 1] if c + 1 < cols else zero, left[c]
                ),
            ]
            carry = emit(j, c, mid, tree(terms + others(j, c)), carry)
    return carry


def advance(mid, beside, diagonal, before):
    scale = 2.0 / half_range
    return scale * ((diagonal + (6.0 - center_shift)) * mid - beside) - before


def products(mid, before, value, carry):
    added = (mid * before, mid * mid, mid * value, value * value)
    return tuple(a + b for a, b in zip(carry, added))


def ahead_body(current, previous, diagonal, out, sums):
    nx = current.shape[0]
    rows, cols = tiles(current.shape)

    def one(i, carry):
        def emit(j, c, mid, beside, carry):
            place = (i, *at(j, c))
            before = previous[place]
            value = advance(mid, beside, diagonal[place], before)
            out[place] = value
            return products(mid, before, value, carry)

        return plane(
            lambda j, c: current[(i, *at(j, c))],
            (rows, cols),
            None,
            None,
            lambda j, c: [current[(i - 1, *at(j, c))], current[(i + 1, *at(j, c))]],
            emit,
            carry,
            range(1, rows - 1),
        )

    zero = jnp.zeros((SUB, LANE), jnp.float32)
    total = lax.fori_loop(2, nx - 2, one, (zero,) * 4)
    for n in range(4):
        sums[n] = total[n]


def close_body(*refs):
    (t3_in, t4_in, previous, diagonal), refs = refs[:4], refs[4:]
    (far_x, near_x, far_y, near_y, own_far, own_near), refs = refs[:6], refs[6:]
    (far_c, near_c), older, beyond, refs = refs[:2], refs[2:6], refs[6:8], refs[8:]
    beyond = [*beyond, older[2].at[1], older[3].at[1]]
    older = [*older[:2], older[2].at[0], older[3].at[0]]
    s0, s1, s2, s3, t3, t4, out, hx, hy = refs
    nx, ny, _ = t3.shape
    rows, cols = tiles(t3.shape)
    odd_x, has_x = side("gx")
    odd_y, has_y = side("gy")
    near_layer = jnp.where(odd_x, 0, nx - 1)

    def lanes(c):
        return pl.ds(c * LANE, LANE)

    def spread(line):
        return jnp.broadcast_to(line, (SUB, LANE))

    def outer(target, halo, inner, edges, odd, factor, old, diag):
        near_edge, far_edge = edges

        def low(c):
            return spread(jnp.where(odd, near_edge(c), far_edge(c)))

        def high(c):
            return spread(jnp.where(odd, far_edge(c), near_edge(c)))

        def emit(j, c, mid, beside, carry):
            value = advance(mid, beside, diag[at(j, c)], old[at(j, c)])
            target[at(j, c)] = value if factor is None else factor * value
            return carry

        shape = (halo.shape[1] // SUB, cols)
        plane(
            lambda j, c: halo[(0, *at(j, c))],
            shape,
            low,
            high,
            lambda j, c: [halo[(1, *at(j, c))], inner(j, c)],
            emit,
            0,
            range(shape[0]),
        )

    for n, (halo, corner, layer_index, factor, old, diag) in enumerate(
        (
            (near_x, near_c, near_layer, None, older[1], beyond[1]),
            (far_x, far_c, nx - 1 - near_layer, has_x, older[0], beyond[0]),
        )
    ):
        edges = (
            lambda c, corner=corner: corner[0:1, lanes(c)],
            lambda c, corner=corner: has_y * corner[1:2, lanes(c)],
        )

        def inner(j, c, place=layer_index):
            return previous[(place, *at(j, c))]

        outer(hx.at[n], halo, inner, edges, odd_y, factor, old, diag)
    for n, (halo, own, factor, old, diag) in enumerate(
        (
            (near_y, own_near, None, older[3], beyond[3]),
            (far_y, own_far, has_y, older[2], beyond[2]),
        )
    ):
        edges = (
            lambda c, n=n: near_c[n : n + 1, lanes(c)],
            lambda c, n=n: has_x * far_c[n : n + 1, lanes(c)],
        )

        def inner(j, c, own=own):
            return own[(0, *at(j, c))]

        outer(hy.at[n], halo, inner, edges, odd_x, factor, old, diag)

    scale = -2.0 / half_range
    add_edges(scale, t3, [r.at[0] for r in (far_x, near_x, far_y, near_y)])
    low_x, low_y = jnp.where(odd_x, 0, 1), jnp.where(odd_y, 0, 1)

    def one(i, below, above, wanted, carry):
        def others(j, c):
            return [
                t3[(i - 1, *at(j, c))] if below else hx[(low_x, *at(j, c))],
                t3[(i + 1, *at(j, c))] if above else hx[(1 - low_x, *at(j, c))],
            ]

        def emit(j, c, mid, beside, carry):
            place = (i, *at(j, c))
            before = previous[place]
            value = advance(mid, beside, diagonal[place], before)
            t4[place] = value
            return products(mid, before, value, carry)

        return plane(
            lambda j, c: t3[(i, *at(j, c))],
            (rows, cols),
            lambda c: spread(hy[low_y, pl.ds(i, 1), lanes(c)]),
            lambda c: spread(hy[1 - low_y, pl.ds(i, 1), lanes(c)]),
            others,
            emit,
            carry,
            wanted,
        )

    sums = tuple(s3[n] for n in range(4))
    sums = one(0, False, True, range(rows), sums)
    sums = one(1, True, True, range(rows), sums)
    for i in range(2, nx - 2):
        sums = one(i, True, True, (0, rows - 1), sums)
    sums = one(nx - 2, True, True, range(rows), sums)
    sums = one(nx - 1, True, False, range(rows), sums)
    parts = [s0[0], s1[1], s1[0], s2[1], s2[0], *sums]
    lane = lax.broadcasted_iota(jnp.int32, (SUB, LANE), 1)
    packed = jnp.zeros((SUB, LANE), jnp.float32)
    for n, part in enumerate(parts):
        total = jnp.sum(part, axis=1, keepdims=True)
        packed = jnp.where(lane == n, total, packed)
    packed = jnp.sum(packed, axis=0, keepdims=True)
    out[...] = jnp.broadcast_to(packed, out.shape)


def coefficients(q):
    depth = STEPS
    moment = [None] * (2 * depth + 1)
    moment[0], moment[1] = q[0], q[1]
    for n in range(2, 2 * depth + 1):
        moment[n] = 2.0 * q[n] - moment[n % 2]
    gram = [
        [
            q[i + j] if abs(i - j) < 2 else 0.5 * (moment[i + j] + moment[abs(i - j)])
            for j in range(depth + 1)
        ]
        for i in range(depth + 1)
    ]

    def plus(a, b):
        return b if a is None else a if b is None else a + b

    def times(a, b):
        return None if a is None or b is None else a * b

    def change(v):
        moved = [None] * (depth + 1)
        for k in range(depth):
            if k == 0:
                entries = {0: center_shift, 1: half_range}
            else:
                entries = {
                    k - 1: half_range / 2.0,
                    k: center_shift,
                    k + 1: half_range / 2.0,
                }
            for i, value in entries.items():
                moved[i] = plus(moved[i], times(value, v[k]))
        return moved

    def quad(left, right):
        total = None
        for i in range(depth + 1):
            inner = None
            for j in range(depth + 1):
                inner = plus(inner, times(gram[i][j], right[j]))
            total = plus(total, times(left[i], inner))
        return total

    one = jnp.ones_like(q[0])
    xc = [None] * (depth + 1)
    rc = [one] + [None] * depth
    pc = [one] + [None] * depth
    rr = quad(rc, rc)
    for _ in range(depth):
        moved = change(pc)
        alpha = rr / quad(pc, moved)
        xc = [plus(x, times(alpha, p)) for x, p in zip(xc, pc)]
        rc = [plus(r, times(-alpha, m)) for r, m in zip(rc, moved)]
        following = quad(rc, rc)
        beta = following / rr
        pc = [plus(r, times(beta, p)) for r, p in zip(rc, pc)]
        rr = following
    return xc, rc


CHUNK = 2


def final_body(sums, guess, t0, t1, t2, t3, t4, sol_hbm, res_hbm, sol, res, sems):
    nx = t0.shape[0]
    rows, cols = tiles(t0.shape)
    packed = tree([sums[pl.ds(n * SUB, SUB), :] for n in range(sums.shape[0] // SUB)])
    packed = jnp.sum(packed, axis=0, keepdims=True)
    q = [
        jnp.broadcast_to(packed[:, n : n + 1], (SUB, LANE))
        for n in range(2 * STEPS + 1)
    ]
    xc, rc = coefficients(q)
    basis = [t0, t1, t2, t3, t4]
    steps = nx // CHUNK

    def copies(step):
        block = pl.ds(step * CHUNK, CHUNK)
        return (
            pltpu.make_async_copy(sol.at[block], sol_hbm.at[block], sems.at[0, step]),
            pltpu.make_async_copy(res.at[block], res_hbm.at[block], sems.at[1, step]),
        )

    def step_body(step, carry):
        for u in range(CHUNK):
            i = step * CHUNK + u
            for j in range(rows):
                for c in range(cols):
                    place = (i, *at(j, c))
                    values = [b[place] for b in basis]
                    x, r = guess[place], None
                    for k in range(STEPS + 1):
                        if xc[k] is not None:
                            x = x + xc[k] * values[k]
                        term = rc[k] * values[k]
                        r = term if r is None else r + term
                    sol[place] = x
                    res[place] = r
        for copy in copies(step):
            copy.start()
        return carry

    lax.fori_loop(0, steps, step_body, 0)

    def wait_body(step, carry):
        for copy in copies(step):
            copy.wait()
        return carry

    lax.fori_loop(0, steps, wait_body, 0)


def all_sum(rows):
    parts = lax.all_to_all(rows[:, None, :], ("gx", "gy"), 0, 0)
    return parts[:, 0, :]


def fix(scale, t, halo, x_depth=(), y_depth=(), extra=()):
    t, *faces = kernel(
        functools.partial(fix_body, scale),
        [f32(*t.shape)] + face_shapes(t, *x_depth)[:2] + face_shapes(t, *y_depth)[2:],
        t,
        *halo,
        *extra,
        alias={0: 0},
    )
    return t, faces


def shards(right_side, guess, diagonal):
    devices = lax.axis_size("gx") * lax.axis_size("gy")
    size, block = guess.size, guess.shape
    strip = pltpu.VMEM((block[0], SUB, block[2]), jnp.float32)
    source = pltpu.with_memory_space_constraint(guess, pltpu.HBM)
    shapes = face_shapes(guess)
    faces = kernel(
        x_faces_body,
        shapes[:2],
        source,
        specs=[hbm],
        scratch=[pltpu.SemaphoreType.DMA((2,))],
        flops=100000 * size,
    ) + kernel(
        y_faces_body,
        shapes[2:],
        source,
        specs=[hbm],
        scratch=[strip, strip, pltpu.SemaphoreType.DMA((2,))],
        flops=1000 * size,
    )
    guess, right_side, diagonal = (
        pltpu.with_memory_space_constraint(a, pltpu.VMEM)
        for a in (guess, right_side, diagonal)
    )
    halo = exchange(faces)
    (t,) = kernel(
        first_body, [f32(*block)], guess, right_side, diagonal, flops=20 * size
    )
    t, faces = fix(1.0, t, halo)
    basis, sums, halos, beyond = [t], [], [], []
    for k in range(STEPS - 1):
        halos.append(exchange(faces))
        given = [basis[k], diagonal] if k == 0 else [basis[k], basis[k - 1], diagonal]
        t, s = kernel(
            functools.partial(next_body, k),
            [f32(*block), f32(1 if k == 0 else 2, SUB, LANE)],
            *given,
            *(beyond if k == 1 else ()),
            flops=24 * size,
        )
        sums.append(s)
        basis.append(t)
        if k < STEPS - 2:
            scale = -1.0 / half_range if k == 0 else -2.0 / half_range
            if k == 0:
                edge = kernel(diagonal_x_body, shapes[:2], diagonal, s)
                beyond = exchange(edge, (0, 1))
                depths, extra = ((), (2,)), (diagonal,)
            else:
                depths, extra = ((2,), (2,)), ()
            basis[-1], faces = fix(scale, t, halos[k], *depths, extra=extra)
    corner = kernel(corner_body, [f32(SUB, block[2])] * 2, *halos[-1][2:])
    corners = exchange(corner, (0, 1))
    t4, s = kernel(
        ahead_body,
        [f32(*block), f32(4, SUB, LANE)],
        basis[3],
        basis[2],
        diagonal,
        flops=12 * size,
    )
    basis[3], t4, rows = kernel(
        close_body,
        [f32(*block), f32(*block), f32(devices, LANE)],
        basis[3],
        t4,
        basis[2],
        diagonal,
        *halos[-1],
        *faces[2:],
        *corners,
        *halos[-2],
        *beyond,
        *sums,
        s,
        alias={0: 0, 1: 1},
        scratch=[
            pltpu.VMEM((2, block[1], block[2]), jnp.float32),
            pltpu.VMEM((2, block[0], block[2]), jnp.float32),
        ],
    )
    return kernel(
        final_body,
        [f32(*block), f32(*block)],
        all_sum(rows),
        guess,
        *basis,
        t4,
        out_specs=[hbm] * 2,
        scratch=[
            pltpu.VMEM(block, jnp.float32),
            pltpu.VMEM(block, jnp.float32),
            pltpu.SemaphoreType.DMA((2, block[0] // CHUNK)),
        ],
    )


def solution(mesh):
    return jax.shard_map(
        shards,
        mesh=mesh,
        in_specs=(P("gx", "gy", None),) * 3,
        out_specs=(P("gx", "gy", None),) * 2,
        check_vma=False,
    )
```

```python
import functools

import jax
import jax.numpy as jnp
from jax import lax
from jax.experimental import pallas as pl
from jax.experimental.pallas import tpu as pltpu
from jax.sharding import PartitionSpec as P

STEPS = 4
SUB, LANE = 8, 128
center_shift = 6.25
half_range = 6.25
VMEM_LIMIT = 40 * 1024 * 1024

vmem = pl.BlockSpec(memory_space=pltpu.VMEM)
hbm = pl.BlockSpec(memory_space=pltpu.HBM)


def f32(*shape):
    return jax.ShapeDtypeStruct(shape, jnp.float32)


def kernel(body, outs, *args, specs=None, out_specs=None, scratch=(), alias=None, flops=0):
    size = sum(a.size * 4 for a in args) + sum(o.size * 4 for o in outs)
    return pl.pallas_call(
        body,
        out_shape=outs,
        in_specs=specs or [vmem] * len(args),
        out_specs=out_specs or [vmem] * len(outs),
        scratch_shapes=list(scratch),
        input_output_aliases=alias or {},
        compiler_params=pltpu.CompilerParams(vmem_limit_bytes=VMEM_LIMIT),
        cost_estimate=pl.CostEstimate(
            flops=flops, bytes_accessed=size, transcendentals=0
        ),
    )(*args)


def tree(values):
    while len(values) > 1:
        pairs = [a + b for a, b in zip(values[0::2], values[1::2])]
        values = pairs + ([values[-1]] if len(values) % 2 else [])
    return values[0]


def tiles(shape):
    return shape[1] // SUB, shape[2] // LANE


def layer(t_ref, i, below, above, emit, carry):
    rows, cols = tiles(t_ref.shape)
    sub = lax.broadcasted_iota(jnp.int32, (SUB, LANE), 0)
    lane = lax.broadcasted_iota(jnp.int32, (SUB, LANE), 1)
    first_sub, last_sub = sub == 0, sub == SUB - 1
    first_lane, last_lane = lane == 0, lane == LANE - 1

    def load(j, c, di=0):
        return t_ref[i + di, pl.ds(j * SUB, SUB), pl.ds(c * LANE, LANE)]

    zero = jnp.zeros((SUB, LANE), jnp.float32)
    now = [load(0, c) for c in range(cols)]
    fromlow = [zero] * cols
    for j in range(rows):
        after = [load(j + 1, c) for c in range(cols)] if j + 1 < rows else None
        right = [pltpu.roll(v, 1, 1) for v in now]
        left = [pltpu.roll(v, LANE - 1, 1) for v in now]
        down = [pltpu.roll(v, 1, 0) for v in now]
        for c in range(cols):
            up = pltpu.roll(now[c], SUB - 1, 0)
            nextup = pltpu.roll(after[c], SUB - 1, 0) if after is not None else zero
            s = jnp.where(first_sub, fromlow[c], down[c])
            s = s + jnp.where(last_sub, nextup, up)
            s = s + jnp.where(first_lane, right[c - 1] if c > 0 else zero, right[c])
            s = s + jnp.where(last_lane, left[c + 1] if c + 1 < cols else zero, left[c])
            if below:
                s = s + load(j, c, -1)
            if above:
                s = s + load(j, c, 1)
            carry = emit(i, j, c, now[c], s, carry)
        fromlow = down
        now = after
    return carry


def sweep(t_ref, emit, carry):
    nx = t_ref.shape[0]
    carry = layer(t_ref, 0, False, True, emit, carry)
    carry = lax.fori_loop(
        1, nx - 1, lambda i, a: layer(t_ref, i, True, True, emit, a), carry
    )
    return layer(t_ref, nx - 1, True, False, emit, carry)


def at(j, c):
    return pl.ds(j * SUB, SUB), pl.ds(c * LANE, LANE)


def swaps(nx, ny):
    def pairs(partner):
        return [
            (i * ny + j, x * ny + y)
            for i in range(nx)
            for j in range(ny)
            for x, y in [partner(i, j)]
        ]

    def far(i):
        return i + 1 if i % 2 else i - 1

    return (
        pairs(lambda i, j: (far(i), j) if 0 < i < nx - 1 else (i, j ^ 1)),
        pairs(lambda i, j: (i ^ 1, j)),
        pairs(lambda i, j: (i, far(j)) if 0 < j < ny - 1 else (i ^ (nx // 8), j)),
        pairs(lambda i, j: (i, j ^ 1)),
    )


def side(axis):
    index, count = lax.axis_index(axis), lax.axis_size(axis)
    odd = lax.rem(index, 2) == 1
    ends = jnp.logical_or(index == 0, index == count - 1)
    return odd, jnp.where(ends, 0.0, 1.0).astype(jnp.float32)


def exchange(faces, which=range(4)):
    perms = swaps(lax.axis_size("gx"), lax.axis_size("gy"))
    return [lax.ppermute(f, ("gx", "gy"), perms[n]) for f, n in zip(faces, which)]


def face_shapes(t, *depth):
    nx, ny, nz = t.shape
    return [f32(*depth, ny, nz)] * 2 + [f32(*depth, nx, nz)] * 2


def x_faces_body(field, far_x, near_x, sems):
    nx = field.shape[0]
    odd_x, _ = side("gx")
    near_layer = jnp.where(odd_x, 0, nx - 1)
    copies = [
        pltpu.make_async_copy(field.at[nx - 1 - near_layer], far_x, sems.at[0]),
        pltpu.make_async_copy(field.at[near_layer], near_x, sems.at[1]),
    ]
    for copy in copies:
        copy.start()
    for copy in copies:
        copy.wait()


def y_faces_body(field, far_y, near_y, low, high, sems):
    nx, ny, _ = field.shape
    odd_y, _ = side("gy")
    copies = [
        pltpu.make_async_copy(field.at[:, pl.ds(0, SUB)], low, sems.at[0]),
        pltpu.make_async_copy(field.at[:, pl.ds(ny - SUB, SUB)], high, sems.at[1]),
    ]
    for copy in copies:
        copy.start()
    for copy in copies:
        copy.wait()
    for i in range(nx):
        first, last = low[i, 0:1, :], high[i, SUB - 1 : SUB, :]
        near_y[i : i + 1, :] = jnp.where(odd_y, first, last)
        far_y[i : i + 1, :] = jnp.where(odd_y, last, first)


def first_body(guess, right_side, diagonal, out):
    def emit(i, j, c, mid, beside, carry):
        place = (i, *at(j, c))
        applied = (6.0 + diagonal[place]) * mid - beside
        out[place] = right_side[place] - applied
        return carry

    sweep(guess, emit, 0)


def next_body(index, *refs):
    if index == 0:
        current, diagonal = refs[:2]
    else:
        current, previous, diagonal = refs[:3]
    out, sums = refs[-2:]
    scale = 1.0 / half_range if index == 0 else 2.0 / half_range
    zero = jnp.zeros((SUB, LANE), jnp.float32)
    count = sums.shape[0]

    def emit(i, j, c, mid, beside, carry):
        place = (i, *at(j, c))
        d = diagonal[place]
        value = scale * ((d + (6.0 - center_shift)) * mid - beside)
        added = [mid * mid]
        if index > 0:
            before = previous[place]
            value = value - before
            added.append(mid * before)
        out[place] = value
        return tuple(a + b for a, b in zip(carry, added))

    total = sweep(current, emit, (zero,) * count)
    for n in range(count):
        sums[n] = total[n]


def add_edges(scale, t, halo):
    far_x, near_x, far_y, near_y = halo
    nx, ny, _ = t.shape
    rows, cols = tiles(t.shape)
    sub = lax.broadcasted_iota(jnp.int32, (SUB, LANE), 0)
    odd_x, has_x = side("gx")
    odd_y, has_y = side("gy")
    near_layer = jnp.where(odd_x, 0, nx - 1)
    far_scale_x, far_scale_y = scale * has_x, scale * has_y

    for i, layer, factor, n in (
        (near_layer, near_x, scale, 0),
        (nx - 1 - near_layer, far_x, far_scale_x, 1),
    ):
        for j in range(rows):
            places = [(i, *at(j, c)) for c in range(cols)]
            olds = [t[place] for place in places]
            news = [old + factor * layer[at(j, c)] for c, old in enumerate(olds)]
            for c in range(cols):
                t[places[c]] = news[c]

    low_scale = jnp.where(odd_y, scale, far_scale_y)
    high_scale = jnp.where(odd_y, far_scale_y, scale)
    for i in range(nx):
        places, olds, news = [], [], []
        for c in range(cols):
            lanes = pl.ds(c * LANE, LANE)
            near, far = near_y[pl.ds(i, 1), lanes], far_y[pl.ds(i, 1), lanes]
            low = low_scale * jnp.where(odd_y, near, far)
            high = high_scale * jnp.where(odd_y, far, near)
            for j, row, value in ((0, 0, low), (rows - 1, SUB - 1, high)):
                place = (i, *at(j, c))
                old = t[place]
                places.append(place)
                olds.append(old)
                news.append(old + jnp.where(sub == row, value, 0.0))
        for place, new in zip(places, news):
            t[place] = new


def fix_body(scale, t_in, far_x, near_x, far_y, near_y, *refs):
    t, ffx, nfx, ffy, nfy = refs[-5:]
    add_edges(scale, t, (far_x, near_x, first_of(far_y), first_of(near_y)))
    if len(refs) == 6:
        write_faces(t, ffx, nfx, ffy.at[0], nfy.at[0])
        write_rows(refs[0], 0, ffy.at[1], nfy.at[1])
    else:
        write_faces(t, ffx, nfx, ffy, nfy)


def first_of(ref):
    return ref.at[0] if len(ref.shape) == 3 else ref


def write_rows(t, n, far_row, near_row):
    nx, ny, _ = t.shape
    odd_y, _ = side("gy")
    for i in range(nx):
        first, last = t[i, n : n + 1, :], t[i, ny - 1 - n : ny - n, :]
        near_row[i : i + 1, :] = jnp.where(odd_y, first, last)
        far_row[i : i + 1, :] = jnp.where(odd_y, last, first)


def write_faces(t, ffx, nfx, ffy, nfy):
    nx = t.shape[0]
    odd_x, _ = side("gx")
    for n in range(1 if len(ffx.shape) == 2 else ffx.shape[0]):
        views = [r.at[n] if len(r.shape) == 3 else r for r in (ffx, nfx, ffy, nfy)]
        far_layer, near_layer, far_row, near_row = views
        place = jnp.where(odd_x, n, nx - 1 - n)
        near_layer[...] = t[place]
        far_layer[...] = t[nx - 1 - place]
        write_rows(t, n, far_row, near_row)


def diagonal_x_body(diagonal, *refs):
    far, near = refs[-2:]
    nx = diagonal.shape[0]
    odd_x, _ = side("gx")
    place = jnp.where(odd_x, 0, nx - 1)
    near[...] = diagonal[place]
    far[...] = diagonal[nx - 1 - place]


def corner_body(far_y, near_y, after, far, near):
    nx = far_y.shape[1]
    odd_x, _ = side("gx")
    near[...] = jnp.zeros_like(near)
    far[...] = jnp.zeros_like(far)
    for n, line in enumerate((near_y, far_y)):
        first, last = line[0, 0:1, :], line[0, nx - 1 : nx, :]
        near[n : n + 1, :] = jnp.where(odd_x, first, last)
        far[n : n + 1, :] = jnp.where(odd_x, last, first)


def plane(tile, shape, low, high, others, emit, carry, wanted):
    rows, cols = shape
    sub = lax.broadcasted_iota(jnp.int32, (SUB, LANE), 0)
    lane = lax.broadcasted_iota(jnp.int32, (SUB, LANE), 1)
    zero = jnp.zeros((SUB, LANE), jnp.float32)
    for j in wanted:
        mids = [tile(j, c) for c in range(cols)]
        right = [pltpu.roll(v, 1, 1) for v in mids]
        left = [pltpu.roll(v, LANE - 1, 1) for v in mids]
        for c, mid in enumerate(mids):
            before = pltpu.roll(tile(j - 1, c), 1, 0) if j > 0 else low(c)
            after = pltpu.roll(tile(j + 1, c), SUB - 1, 0) if j + 1 < rows else high(c)
            terms = [
                jnp.where(sub == 0, before, pltpu.roll(mid, 1, 0)),
                jnp.where(sub == SUB - 1, after, pltpu.roll(mid, SUB - 1, 0)),
                jnp.where(lane == 0, right[c - 1] if c > 0 else zero, right[c]),
                jnp.where(
                    lane == LANE - 1, left[c + 1] if c + 1 < cols else zero, left[c]
                ),
            ]
            carry = emit(j, c, mid, tree(terms + others(j, c)), carry)
    return carry


def advance(mid, beside, diagonal, before):
    scale = 2.0 / half_range
    return scale * ((diagonal + (6.0 - center_shift)) * mid - beside) - before


def products(mid, before, value, carry):
    added = (mid * before, mid * mid, mid * value, value * value)
    return tuple(a + b for a, b in zip(carry, added))


def ahead_body(current, previous, diagonal, out, sums):
    nx = current.shape[0]
    rows, cols = tiles(current.shape)

    def one(i, carry):
        def emit(j, c, mid, beside, carry):
            place = (i, *at(j, c))
            before = previous[place]
            value = advance(mid, beside, diagonal[place], before)
            out[place] = value
            return products(mid, before, value, carry)

        return plane(
            lambda j, c: current[(i, *at(j, c))],
            (rows, cols),
            None,
            None,
            lambda j, c: [current[(i - 1, *at(j, c))], current[(i + 1, *at(j, c))]],
            emit,
            carry,
            range(1, rows - 1),
        )

    zero = jnp.zeros((SUB, LANE), jnp.float32)
    total = lax.fori_loop(2, nx - 2, one, (zero,) * 4)
    for n in range(4):
        sums[n] = total[n]


def close_body(*refs):
    (t3_in, t4_in, previous, diagonal), refs = refs[:4], refs[4:]
    (far_x, near_x, far_y, near_y, own_far, own_near), refs = refs[:6], refs[6:]
    (far_c, near_c), older, beyond, refs = refs[:2], refs[2:6], refs[6:8], refs[8:]
    beyond = [*beyond, older[2].at[1], older[3].at[1]]
    older = [*older[:2], older[2].at[0], older[3].at[0]]
    s0, s1, s2, s3, t3, t4, out, hx, hy = refs
    nx, ny, _ = t3.shape
    rows, cols = tiles(t3.shape)
    odd_x, has_x = side("gx")
    odd_y, has_y = side("gy")
    near_layer = jnp.where(odd_x, 0, nx - 1)

    def lanes(c):
        return pl.ds(c * LANE, LANE)

    def spread(line):
        return jnp.broadcast_to(line, (SUB, LANE))

    def outer(target, halo, inner, edges, odd, factor, old, diag):
        near_edge, far_edge = edges

        def low(c):
            return spread(jnp.where(odd, near_edge(c), far_edge(c)))

        def high(c):
            return spread(jnp.where(odd, far_edge(c), near_edge(c)))

        def emit(j, c, mid, beside, carry):
            value = advance(mid, beside, diag[at(j, c)], old[at(j, c)])
            target[at(j, c)] = value if factor is None else factor * value
            return carry

        shape = (halo.shape[1] // SUB, cols)
        plane(
            lambda j, c: halo[(0, *at(j, c))],
            shape,
            low,
            high,
            lambda j, c: [halo[(1, *at(j, c))], inner(j, c)],
            emit,
            0,
            range(shape[0]),
        )

    for n, (halo, corner, layer_index, factor, old, diag) in enumerate(
        (
            (near_x, near_c, near_layer, None, older[1], beyond[1]),
            (far_x, far_c, nx - 1 - near_layer, has_x, older[0], beyond[0]),
        )
    ):
        edges = (
            lambda c, corner=corner: corner[0:1, lanes(c)],
            lambda c, corner=corner: has_y * corner[1:2, lanes(c)],
        )

        def inner(j, c, place=layer_index):
            return previous[(place, *at(j, c))]

        outer(hx.at[n], halo, inner, edges, odd_y, factor, old, diag)
    for n, (halo, own, factor, old, diag) in enumerate(
        (
            (near_y, own_near, None, older[3], beyond[3]),
            (far_y, own_far, has_y, older[2], beyond[2]),
        )
    ):
        edges = (
            lambda c, n=n: near_c[n : n + 1, lanes(c)],
            lambda c, n=n: has_x * far_c[n : n + 1, lanes(c)],
        )

        def inner(j, c, own=own):
            return own[(0, *at(j, c))]

        outer(hy.at[n], halo, inner, edges, odd_x, factor, old, diag)

    scale = -2.0 / half_range
    add_edges(scale, t3, [r.at[0] for r in (far_x, near_x, far_y, near_y)])
    low_x, low_y = jnp.where(odd_x, 0, 1), jnp.where(odd_y, 0, 1)

    def one(i, below, above, wanted, carry):
        def others(j, c):
            return [
                t3[(i - 1, *at(j, c))] if below else hx[(low_x, *at(j, c))],
                t3[(i + 1, *at(j, c))] if above else hx[(1 - low_x, *at(j, c))],
            ]

        def emit(j, c, mid, beside, carry):
            place = (i, *at(j, c))
            before = previous[place]
            value = advance(mid, beside, diagonal[place], before)
            t4[place] = value
            return products(mid, before, value, carry)

        return plane(
            lambda j, c: t3[(i, *at(j, c))],
            (rows, cols),
            lambda c: spread(hy[low_y, pl.ds(i, 1), lanes(c)]),
            lambda c: spread(hy[1 - low_y, pl.ds(i, 1), lanes(c)]),
            others,
            emit,
            carry,
            wanted,
        )

    sums = tuple(s3[n] for n in range(4))
    sums = one(0, False, True, range(rows), sums)
    sums = one(1, True, True, range(rows), sums)
    for i in range(2, nx - 2):
        sums = one(i, True, True, (0, rows - 1), sums)
    sums = one(nx - 2, True, True, range(rows), sums)
    sums = one(nx - 1, True, False, range(rows), sums)
    parts = [s0[0], s1[1], s1[0], s2[1], s2[0], *sums]
    lane = lax.broadcasted_iota(jnp.int32, (SUB, LANE), 1)
    packed = jnp.zeros((SUB, LANE), jnp.float32)
    for n, part in enumerate(parts):
        total = jnp.sum(part, axis=1, keepdims=True)
        packed = jnp.where(lane == n, total, packed)
    packed = jnp.sum(packed, axis=0, keepdims=True)
    out[...] = jnp.broadcast_to(packed, out.shape)


def coefficients(q):
    depth = STEPS
    moment = [None] * (2 * depth + 1)
    moment[0], moment[1] = q[0], q[1]
    for n in range(2, 2 * depth + 1):
        moment[n] = 2.0 * q[n] - moment[n % 2]
    gram = [
        [
            q[i + j] if abs(i - j) < 2 else 0.5 * (moment[i + j] + moment[abs(i - j)])
            for j in range(depth + 1)
        ]
        for i in range(depth + 1)
    ]

    def plus(a, b):
        return b if a is None else a if b is None else a + b

    def times(a, b):
        return None if a is None or b is None else a * b

    def change(v):
        moved = [None] * (depth + 1)
        for k in range(depth):
            if k == 0:
                entries = {0: center_shift, 1: half_range}
            else:
                entries = {
                    k - 1: half_range / 2.0,
                    k: center_shift,
                    k + 1: half_range / 2.0,
                }
            for i, value in entries.items():
                moved[i] = plus(moved[i], times(value, v[k]))
        return moved

    def quad(left, right):
        total = None
        for i in range(depth + 1):
            inner = None
            for j in range(depth + 1):
                inner = plus(inner, times(gram[i][j], right[j]))
            total = plus(total, times(left[i], inner))
        return total

    one = jnp.ones_like(q[0])
    xc = [None] * (depth + 1)
    rc = [one] + [None] * depth
    pc = [one] + [None] * depth
    rr = quad(rc, rc)
    for _ in range(depth):
        moved = change(pc)
        alpha = rr / quad(pc, moved)
        xc = [plus(x, times(alpha, p)) for x, p in zip(xc, pc)]
        rc = [plus(r, times(-alpha, m)) for r, m in zip(rc, moved)]
        following = quad(rc, rc)
        beta = following / rr
        pc = [plus(r, times(beta, p)) for r, p in zip(rc, pc)]
        rr = following
    return xc, rc


CHUNK = 2


def final_body(sums, guess, t0, t1, t2, t3, t4, sol_hbm, res_hbm, sol, res, sems):
    nx = t0.shape[0]
    rows, cols = tiles(t0.shape)
    packed = tree([sums[pl.ds(n * SUB, SUB), :] for n in range(sums.shape[0] // SUB)])
    packed = jnp.sum(packed, axis=0, keepdims=True)
    q = [
        jnp.broadcast_to(packed[:, n : n + 1], (SUB, LANE))
        for n in range(2 * STEPS + 1)
    ]
    xc, rc = coefficients(q)
    basis = [t0, t1, t2, t3, t4]
    steps = nx // CHUNK

    def copies(step):
        block = pl.ds(step * CHUNK, CHUNK)
        return (
            pltpu.make_async_copy(sol.at[block], sol_hbm.at[block], sems.at[0, step]),
            pltpu.make_async_copy(res.at[block], res_hbm.at[block], sems.at[1, step]),
        )

    def step_body(step, carry):
        for u in range(CHUNK):
            i = step * CHUNK + u
            for j in range(rows):
                for c in range(cols):
                    place = (i, *at(j, c))
                    values = [b[place] for b in basis]
                    x, r = guess[place], None
                    for k in range(STEPS + 1):
                        if xc[k] is not None:
                            x = x + xc[k] * values[k]
                        term = rc[k] * values[k]
                        r = term if r is None else r + term
                    sol[place] = x
                    res[place] = r
        for copy in copies(step):
            copy.start()
        return carry

    lax.fori_loop(0, steps, step_body, 0)

    def wait_body(step, carry):
        for copy in copies(step):
            copy.wait()
        return carry

    lax.fori_loop(0, steps, wait_body, 0)


def all_sum(rows):
    parts = lax.all_to_all(rows[:, None, :], ("gx", "gy"), 0, 0)
    return parts[:, 0, :]


def fix(scale, t, halo, x_depth=(), y_depth=(), extra=()):
    t, *faces = kernel(
        functools.partial(fix_body, scale),
        [f32(*t.shape)] + face_shapes(t, *x_depth)[:2] + face_shapes(t, *y_depth)[2:],
        t,
        *halo,
        *extra,
        alias={0: 0},
    )
    return t, faces


def shards(right_side, guess, diagonal):
    devices = lax.axis_size("gx") * lax.axis_size("gy")
    size, block = guess.size, guess.shape
    strip = pltpu.VMEM((block[0], SUB, block[2]), jnp.float32)
    source = pltpu.with_memory_space_constraint(guess, pltpu.HBM)
    shapes = face_shapes(guess)
    faces = kernel(
        x_faces_body,
        shapes[:2],
        source,
        specs=[hbm],
        scratch=[pltpu.SemaphoreType.DMA((2,))],
        flops=100000 * size,
    ) + kernel(
        y_faces_body,
        shapes[2:],
        source,
        specs=[hbm],
        scratch=[strip, strip, pltpu.SemaphoreType.DMA((2,))],
        flops=1000 * size,
    )
    guess, right_side, diagonal = (
        pltpu.with_memory_space_constraint(a, pltpu.VMEM)
        for a in (guess, right_side, diagonal)
    )
    halo = exchange(faces)
    (t,) = kernel(
        first_body, [f32(*block)], guess, right_side, diagonal, flops=20 * size
    )
    t, faces = fix(1.0, t, halo)
    basis, sums, halos, beyond = [t], [], [], []
    for k in range(STEPS - 1):
        halos.append(exchange(faces))
        given = [basis[k], diagonal] if k == 0 else [basis[k], basis[k - 1], diagonal]
        t, s = kernel(
            functools.partial(next_body, k),
            [f32(*block), f32(1 if k == 0 else 2, SUB, LANE)],
            *given,
            *(beyond if k == 1 else ()),
            flops=24 * size,
        )
        sums.append(s)
        basis.append(t)
        if k < STEPS - 2:
            scale = -1.0 / half_range if k == 0 else -2.0 / half_range
            if k == 0:
                edge = kernel(
                    diagonal_x_body, shapes[:2], diagonal, s, *halos[0][2:]
                )
                beyond = exchange(edge, (0, 1))
                depths, extra = ((), (2,)), (diagonal,)
            else:
                depths, extra = ((2,), (2,)), ()
            basis[-1], faces = fix(scale, t, halos[k], *depths, extra=extra)
    corner = kernel(corner_body, [f32(SUB, block[2])] * 2, *halos[-1][2:], s)
    corners = exchange(corner, (0, 1))
    t4, s = kernel(
        ahead_body,
        [f32(*block), f32(4, SUB, LANE)],
        basis[3],
        basis[2],
        diagonal,
        flops=12 * size,
    )
    basis[3], t4, rows = kernel(
        close_body,
        [f32(*block), f32(*block), f32(devices, LANE)],
        basis[3],
        t4,
        basis[2],
        diagonal,
        *halos[-1],
        *faces[2:],
        *corners,
        *halos[-2],
        *beyond,
        *sums,
        s,
        alias={0: 0, 1: 1},
        scratch=[
            pltpu.VMEM((2, block[1], block[2]), jnp.float32),
            pltpu.VMEM((2, block[0], block[2]), jnp.float32),
        ],
    )
    return kernel(
        final_body,
        [f32(*block), f32(*block)],
        all_sum(rows),
        guess,
        *basis,
        t4,
        out_specs=[hbm] * 2,
        scratch=[
            pltpu.VMEM(block, jnp.float32),
            pltpu.VMEM(block, jnp.float32),
            pltpu.SemaphoreType.DMA((2, block[0] // CHUNK)),
        ],
    )


def solution(mesh):
    return jax.shard_map(
        shards,
        mesh=mesh,
        in_specs=(P("gx", "gy", None),) * 3,
        out_specs=(P("gx", "gy", None),) * 2,
        check_vma=False,
    )
```

```python
import functools

import jax
import jax.numpy as jnp
from jax import lax
from jax.experimental import pallas as pl
from jax.experimental.pallas import tpu as pltpu
from jax.sharding import PartitionSpec as P

STEPS = 4
SUB, LANE = 8, 128
center_shift = 6.25
half_range = 6.25
VMEM_LIMIT = 40 * 1024 * 1024

vmem = pl.BlockSpec(memory_space=pltpu.VMEM)
hbm = pl.BlockSpec(memory_space=pltpu.HBM)


def f32(*shape):
    return jax.ShapeDtypeStruct(shape, jnp.float32)


def kernel(body, outs, *args, specs=None, out_specs=None, scratch=(), alias=None, flops=0):
    size = sum(a.size * 4 for a in args) + sum(o.size * 4 for o in outs)
    return pl.pallas_call(
        body,
        out_shape=outs,
        in_specs=specs or [vmem] * len(args),
        out_specs=out_specs or [vmem] * len(outs),
        scratch_shapes=list(scratch),
        input_output_aliases=alias or {},
        compiler_params=pltpu.CompilerParams(vmem_limit_bytes=VMEM_LIMIT),
        cost_estimate=pl.CostEstimate(
            flops=flops, bytes_accessed=size, transcendentals=0
        ),
    )(*args)


def tree(values):
    while len(values) > 1:
        pairs = [a + b for a, b in zip(values[0::2], values[1::2])]
        values = pairs + ([values[-1]] if len(values) % 2 else [])
    return values[0]


def tiles(shape):
    return shape[1] // SUB, shape[2] // LANE


def layer(t_ref, i, below, above, emit, carry):
    rows, cols = tiles(t_ref.shape)
    sub = lax.broadcasted_iota(jnp.int32, (SUB, LANE), 0)
    lane = lax.broadcasted_iota(jnp.int32, (SUB, LANE), 1)
    first_sub, last_sub = sub == 0, sub == SUB - 1
    first_lane, last_lane = lane == 0, lane == LANE - 1

    def load(j, c, di=0):
        return t_ref[i + di, pl.ds(j * SUB, SUB), pl.ds(c * LANE, LANE)]

    zero = jnp.zeros((SUB, LANE), jnp.float32)
    now = [load(0, c) for c in range(cols)]
    fromlow = [zero] * cols
    for j in range(rows):
        after = [load(j + 1, c) for c in range(cols)] if j + 1 < rows else None
        right = [pltpu.roll(v, 1, 1) for v in now]
        left = [pltpu.roll(v, LANE - 1, 1) for v in now]
        down = [pltpu.roll(v, 1, 0) for v in now]
        for c in range(cols):
            up = pltpu.roll(now[c], SUB - 1, 0)
            nextup = pltpu.roll(after[c], SUB - 1, 0) if after is not None else zero
            s = jnp.where(first_sub, fromlow[c], down[c])
            s = s + jnp.where(last_sub, nextup, up)
            s = s + jnp.where(first_lane, right[c - 1] if c > 0 else zero, right[c])
            s = s + jnp.where(last_lane, left[c + 1] if c + 1 < cols else zero, left[c])
            if below:
                s = s + load(j, c, -1)
            if above:
                s = s + load(j, c, 1)
            carry = emit(i, j, c, now[c], s, carry)
        fromlow = down
        now = after
    return carry


def sweep(t_ref, emit, carry):
    nx = t_ref.shape[0]
    carry = layer(t_ref, 0, False, True, emit, carry)
    carry = lax.fori_loop(
        1, nx - 1, lambda i, a: layer(t_ref, i, True, True, emit, a), carry
    )
    return layer(t_ref, nx - 1, True, False, emit, carry)


def at(j, c):
    return pl.ds(j * SUB, SUB), pl.ds(c * LANE, LANE)


def swaps(nx, ny):
    def pairs(partner):
        return [
            (i * ny + j, x * ny + y)
            for i in range(nx)
            for j in range(ny)
            for x, y in [partner(i, j)]
        ]

    def far(i):
        return i + 1 if i % 2 else i - 1

    return (
        pairs(lambda i, j: (far(i), j) if 0 < i < nx - 1 else (i, j ^ 1)),
        pairs(lambda i, j: (i ^ 1, j)),
        pairs(lambda i, j: (i, far(j)) if 0 < j < ny - 1 else (i, ny - 1 - j)),
        pairs(lambda i, j: (i, j ^ 1)),
    )


def side(axis):
    index, count = lax.axis_index(axis), lax.axis_size(axis)
    odd = lax.rem(index, 2) == 1
    ends = jnp.logical_or(index == 0, index == count - 1)
    return odd, jnp.where(ends, 0.0, 1.0).astype(jnp.float32)


def exchange(faces, which=range(4)):
    perms = swaps(lax.axis_size("gx"), lax.axis_size("gy"))
    return [lax.ppermute(f, ("gx", "gy"), perms[n]) for f, n in zip(faces, which)]


def face_shapes(t, *depth):
    nx, ny, nz = t.shape
    return [f32(*depth, ny, nz)] * 2 + [f32(*depth, nx, nz)] * 2


def x_faces_body(field, far_x, near_x, sems):
    nx = field.shape[0]
    odd_x, _ = side("gx")
    near_layer = jnp.where(odd_x, 0, nx - 1)
    copies = [
        pltpu.make_async_copy(field.at[nx - 1 - near_layer], far_x, sems.at[0]),
        pltpu.make_async_copy(field.at[near_layer], near_x, sems.at[1]),
    ]
    for copy in copies:
        copy.start()
    for copy in copies:
        copy.wait()


def y_faces_body(field, far_y, near_y, low, high, sems):
    nx, ny, _ = field.shape
    odd_y, _ = side("gy")
    copies = [
        pltpu.make_async_copy(field.at[:, pl.ds(0, SUB)], low, sems.at[0]),
        pltpu.make_async_copy(field.at[:, pl.ds(ny - SUB, SUB)], high, sems.at[1]),
    ]
    for copy in copies:
        copy.start()
    for copy in copies:
        copy.wait()
    for i in range(nx):
        first, last = low[i, 0:1, :], high[i, SUB - 1 : SUB, :]
        near_y[i : i + 1, :] = jnp.where(odd_y, first, last)
        far_y[i : i + 1, :] = jnp.where(odd_y, last, first)


def first_body(guess, right_side, diagonal, out):
    def emit(i, j, c, mid, beside, carry):
        place = (i, *at(j, c))
        applied = (6.0 + diagonal[place]) * mid - beside
        out[place] = right_side[place] - applied
        return carry

    sweep(guess, emit, 0)


def next_body(index, *refs):
    if index == 0:
        current, diagonal = refs[:2]
    else:
        current, previous, diagonal = refs[:3]
    out, sums = refs[-2:]
    scale = 1.0 / half_range if index == 0 else 2.0 / half_range
    zero = jnp.zeros((SUB, LANE), jnp.float32)
    count = sums.shape[0]

    def emit(i, j, c, mid, beside, carry):
        place = (i, *at(j, c))
        d = diagonal[place]
        value = scale * ((d + (6.0 - center_shift)) * mid - beside)
        added = [mid * mid]
        if index > 0:
            before = previous[place]
            value = value - before
            added.append(mid * before)
        out[place] = value
        return tuple(a + b for a, b in zip(carry, added))

    total = sweep(current, emit, (zero,) * count)
    for n in range(count):
        sums[n] = total[n]


def add_edges(scale, t, halo):
    far_x, near_x, far_y, near_y = halo
    nx, ny, _ = t.shape
    rows, cols = tiles(t.shape)
    sub = lax.broadcasted_iota(jnp.int32, (SUB, LANE), 0)
    odd_x, has_x = side("gx")
    odd_y, has_y = side("gy")
    near_layer = jnp.where(odd_x, 0, nx - 1)
    far_scale_x, far_scale_y = scale * has_x, scale * has_y

    for i, layer, factor, n in (
        (near_layer, near_x, scale, 0),
        (nx - 1 - near_layer, far_x, far_scale_x, 1),
    ):
        for j in range(rows):
            places = [(i, *at(j, c)) for c in range(cols)]
            olds = [t[place] for place in places]
            news = [old + factor * layer[at(j, c)] for c, old in enumerate(olds)]
            for c in range(cols):
                t[places[c]] = news[c]

    low_scale = jnp.where(odd_y, scale, far_scale_y)
    high_scale = jnp.where(odd_y, far_scale_y, scale)
    for i in range(nx):
        places, olds, news = [], [], []
        for c in range(cols):
            lanes = pl.ds(c * LANE, LANE)
            near, far = near_y[pl.ds(i, 1), lanes], far_y[pl.ds(i, 1), lanes]
            low = low_scale * jnp.where(odd_y, near, far)
            high = high_scale * jnp.where(odd_y, far, near)
            for j, row, value in ((0, 0, low), (rows - 1, SUB - 1, high)):
                place = (i, *at(j, c))
                old = t[place]
                places.append(place)
                olds.append(old)
                news.append(old + jnp.where(sub == row, value, 0.0))
        for place, new in zip(places, news):
            t[place] = new


def fix_body(scale, t_in, far_x, near_x, far_y, near_y, *refs):
    t, ffx, nfx, ffy, nfy = refs[-5:]
    add_edges(scale, t, (far_x, near_x, first_of(far_y), first_of(near_y)))
    if len(refs) == 6:
        write_faces(t, ffx, nfx, ffy.at[0], nfy.at[0])
        write_rows(refs[0], 0, ffy.at[1], nfy.at[1])
    else:
        write_faces(t, ffx, nfx, ffy, nfy)


def first_of(ref):
    return ref.at[0] if len(ref.shape) == 3 else ref


def write_rows(t, n, far_row, near_row):
    nx, ny, _ = t.shape
    odd_y, _ = side("gy")
    for i in range(nx):
        first, last = t[i, n : n + 1, :], t[i, ny - 1 - n : ny - n, :]
        near_row[i : i + 1, :] = jnp.where(odd_y, first, last)
        far_row[i : i + 1, :] = jnp.where(odd_y, last, first)


def write_faces(t, ffx, nfx, ffy, nfy):
    nx = t.shape[0]
    odd_x, _ = side("gx")
    for n in range(1 if len(ffx.shape) == 2 else ffx.shape[0]):
        views = [r.at[n] if len(r.shape) == 3 else r for r in (ffx, nfx, ffy, nfy)]
        far_layer, near_layer, far_row, near_row = views
        place = jnp.where(odd_x, n, nx - 1 - n)
        near_layer[...] = t[place]
        far_layer[...] = t[nx - 1 - place]
        write_rows(t, n, far_row, near_row)


def diagonal_x_body(diagonal, *refs):
    far, near = refs[-2:]
    nx = diagonal.shape[0]
    odd_x, _ = side("gx")
    place = jnp.where(odd_x, 0, nx - 1)
    near[...] = diagonal[place]
    far[...] = diagonal[nx - 1 - place]


def corner_body(far_y, near_y, after, far, near):
    nx = far_y.shape[1]
    odd_x, _ = side("gx")
    near[...] = jnp.zeros_like(near)
    far[...] = jnp.zeros_like(far)
    for n, line in enumerate((near_y, far_y)):
        first, last = line[0, 0:1, :], line[0, nx - 1 : nx, :]
        near[n : n + 1, :] = jnp.where(odd_x, first, last)
        far[n : n + 1, :] = jnp.where(odd_x, last, first)


def plane(tile, shape, low, high, others, emit, carry, wanted):
    rows, cols = shape
    sub = lax.broadcasted_iota(jnp.int32, (SUB, LANE), 0)
    lane = lax.broadcasted_iota(jnp.int32, (SUB, LANE), 1)
    zero = jnp.zeros((SUB, LANE), jnp.float32)
    for j in wanted:
        mids = [tile(j, c) for c in range(cols)]
        right = [pltpu.roll(v, 1, 1) for v in mids]
        left = [pltpu.roll(v, LANE - 1, 1) for v in mids]
        for c, mid in enumerate(mids):
            before = pltpu.roll(tile(j - 1, c), 1, 0) if j > 0 else low(c)
            after = pltpu.roll(tile(j + 1, c), SUB - 1, 0) if j + 1 < rows else high(c)
            terms = [
                jnp.where(sub == 0, before, pltpu.roll(mid, 1, 0)),
                jnp.where(sub == SUB - 1, after, pltpu.roll(mid, SUB - 1, 0)),
                jnp.where(lane == 0, right[c - 1] if c > 0 else zero, right[c]),
                jnp.where(
                    lane == LANE - 1, left[c + 1] if c + 1 < cols else zero, left[c]
                ),
            ]
            carry = emit(j, c, mid, tree(terms + others(j, c)), carry)
    return carry


def advance(mid, beside, diagonal, before):
    scale = 2.0 / half_range
    return scale * ((diagonal + (6.0 - center_shift)) * mid - beside) - before


def products(mid, before, value, carry):
    added = (mid * before, mid * mid, mid * value, value * value)
    return tuple(a + b for a, b in zip(carry, added))


def ahead_body(current, previous, diagonal, out, sums):
    nx = current.shape[0]
    rows, cols = tiles(current.shape)

    def one(i, carry):
        def emit(j, c, mid, beside, carry):
            place = (i, *at(j, c))
            before = previous[place]
            value = advance(mid, beside, diagonal[place], before)
            out[place] = value
            return products(mid, before, value, carry)

        return plane(
            lambda j, c: current[(i, *at(j, c))],
            (rows, cols),
            None,
            None,
            lambda j, c: [current[(i - 1, *at(j, c))], current[(i + 1, *at(j, c))]],
            emit,
            carry,
            range(1, rows - 1),
        )

    zero = jnp.zeros((SUB, LANE), jnp.float32)
    total = lax.fori_loop(2, nx - 2, one, (zero,) * 4)
    for n in range(4):
        sums[n] = total[n]


def close_body(*refs):
    (t3_in, t4_in, previous, diagonal), refs = refs[:4], refs[4:]
    (far_x, near_x, far_y, near_y, own_far, own_near), refs = refs[:6], refs[6:]
    (far_c, near_c), older, beyond, refs = refs[:2], refs[2:6], refs[6:8], refs[8:]
    beyond = [*beyond, older[2].at[1], older[3].at[1]]
    older = [*older[:2], older[2].at[0], older[3].at[0]]
    s0, s1, s2, s3, t3, t4, out, hx, hy = refs
    nx, ny, _ = t3.shape
    rows, cols = tiles(t3.shape)
    odd_x, has_x = side("gx")
    odd_y, has_y = side("gy")
    near_layer = jnp.where(odd_x, 0, nx - 1)

    def lanes(c):
        return pl.ds(c * LANE, LANE)

    def spread(line):
        return jnp.broadcast_to(line, (SUB, LANE))

    def outer(target, halo, inner, edges, odd, factor, old, diag):
        near_edge, far_edge = edges

        def low(c):
            return spread(jnp.where(odd, near_edge(c), far_edge(c)))

        def high(c):
            return spread(jnp.where(odd, far_edge(c), near_edge(c)))

        def emit(j, c, mid, beside, carry):
            value = advance(mid, beside, diag[at(j, c)], old[at(j, c)])
            target[at(j, c)] = value if factor is None else factor * value
            return carry

        shape = (halo.shape[1] // SUB, cols)
        plane(
            lambda j, c: halo[(0, *at(j, c))],
            shape,
            low,
            high,
            lambda j, c: [halo[(1, *at(j, c))], inner(j, c)],
            emit,
            0,
            range(shape[0]),
        )

    for n, (halo, corner, layer_index, factor, old, diag) in enumerate(
        (
            (near_x, near_c, near_layer, None, older[1], beyond[1]),
            (far_x, far_c, nx - 1 - near_layer, has_x, older[0], beyond[0]),
        )
    ):
        edges = (
            lambda c, corner=corner: corner[0:1, lanes(c)],
            lambda c, corner=corner: has_y * corner[1:2, lanes(c)],
        )

        def inner(j, c, place=layer_index):
            return previous[(place, *at(j, c))]

        outer(hx.at[n], halo, inner, edges, odd_y, factor, old, diag)
    for n, (halo, own, factor, old, diag) in enumerate(
        (
            (near_y, own_near, None, older[3], beyond[3]),
            (far_y, own_far, has_y, older[2], beyond[2]),
        )
    ):
        edges = (
            lambda c, n=n: near_c[n : n + 1, lanes(c)],
            lambda c, n=n: has_x * far_c[n : n + 1, lanes(c)],
        )

        def inner(j, c, own=own):
            return own[(0, *at(j, c))]

        outer(hy.at[n], halo, inner, edges, odd_x, factor, old, diag)

    scale = -2.0 / half_range
    add_edges(scale, t3, [r.at[0] for r in (far_x, near_x, far_y, near_y)])
    low_x, low_y = jnp.where(odd_x, 0, 1), jnp.where(odd_y, 0, 1)

    def one(i, below, above, wanted, carry):
        def others(j, c):
            return [
                t3[(i - 1, *at(j, c))] if below else hx[(low_x, *at(j, c))],
                t3[(i + 1, *at(j, c))] if above else hx[(1 - low_x, *at(j, c))],
            ]

        def emit(j, c, mid, beside, carry):
            place = (i, *at(j, c))
            before = previous[place]
            value = advance(mid, beside, diagonal[place], before)
            t4[place] = value
            return products(mid, before, value, carry)

        return plane(
            lambda j, c: t3[(i, *at(j, c))],
            (rows, cols),
            lambda c: spread(hy[low_y, pl.ds(i, 1), lanes(c)]),
            lambda c: spread(hy[1 - low_y, pl.ds(i, 1), lanes(c)]),
            others,
            emit,
            carry,
            wanted,
        )

    sums = tuple(s3[n] for n in range(4))
    sums = one(0, False, True, range(rows), sums)
    sums = one(1, True, True, range(rows), sums)
    for i in range(2, nx - 2):
        sums = one(i, True, True, (0, rows - 1), sums)
    sums = one(nx - 2, True, True, range(rows), sums)
    sums = one(nx - 1, True, False, range(rows), sums)
    parts = [s0[0], s1[1], s1[0], s2[1], s2[0], *sums]
    lane = lax.broadcasted_iota(jnp.int32, (SUB, LANE), 1)
    packed = jnp.zeros((SUB, LANE), jnp.float32)
    for n, part in enumerate(parts):
        total = jnp.sum(part, axis=1, keepdims=True)
        packed = jnp.where(lane == n, total, packed)
    packed = jnp.sum(packed, axis=0, keepdims=True)
    out[...] = jnp.broadcast_to(packed, out.shape)


def coefficients(q):
    depth = STEPS
    moment = [None] * (2 * depth + 1)
    moment[0], moment[1] = q[0], q[1]
    for n in range(2, 2 * depth + 1):
        moment[n] = 2.0 * q[n] - moment[n % 2]
    gram = [
        [
            q[i + j] if abs(i - j) < 2 else 0.5 * (moment[i + j] + moment[abs(i - j)])
            for j in range(depth + 1)
        ]
        for i in range(depth + 1)
    ]

    def plus(a, b):
        return b if a is None else a if b is None else a + b

    def times(a, b):
        return None if a is None or b is None else a * b

    def change(v):
        moved = [None] * (depth + 1)
        for k in range(depth):
            if k == 0:
                entries = {0: center_shift, 1: half_range}
            else:
                entries = {
                    k - 1: half_range / 2.0,
                    k: center_shift,
                    k + 1: half_range / 2.0,
                }
            for i, value in entries.items():
                moved[i] = plus(moved[i], times(value, v[k]))
        return moved

    def quad(left, right):
        total = None
        for i in range(depth + 1):
            inner = None
            for j in range(depth + 1):
                inner = plus(inner, times(gram[i][j], right[j]))
            total = plus(total, times(left[i], inner))
        return total

    one = jnp.ones_like(q[0])
    xc = [None] * (depth + 1)
    rc = [one] + [None] * depth
    pc = [one] + [None] * depth
    rr = quad(rc, rc)
    for _ in range(depth):
        moved = change(pc)
        alpha = rr / quad(pc, moved)
        xc = [plus(x, times(alpha, p)) for x, p in zip(xc, pc)]
        rc = [plus(r, times(-alpha, m)) for r, m in zip(rc, moved)]
        following = quad(rc, rc)
        beta = following / rr
        pc = [plus(r, times(beta, p)) for r, p in zip(rc, pc)]
        rr = following
    return xc, rc


CHUNK = 2


def final_body(sums, guess, t0, t1, t2, t3, t4, sol_hbm, res_hbm, sol, res, sems):
    nx = t0.shape[0]
    rows, cols = tiles(t0.shape)
    packed = tree([sums[pl.ds(n * SUB, SUB), :] for n in range(sums.shape[0] // SUB)])
    packed = jnp.sum(packed, axis=0, keepdims=True)
    q = [
        jnp.broadcast_to(packed[:, n : n + 1], (SUB, LANE))
        for n in range(2 * STEPS + 1)
    ]
    xc, rc = coefficients(q)
    basis = [t0, t1, t2, t3, t4]
    steps = nx // CHUNK

    def copies(step):
        block = pl.ds(step * CHUNK, CHUNK)
        return (
            pltpu.make_async_copy(sol.at[block], sol_hbm.at[block], sems.at[0, step]),
            pltpu.make_async_copy(res.at[block], res_hbm.at[block], sems.at[1, step]),
        )

    def step_body(step, carry):
        for u in range(CHUNK):
            i = step * CHUNK + u
            for j in range(rows):
                for c in range(cols):
                    place = (i, *at(j, c))
                    values = [b[place] for b in basis]
                    x, r = guess[place], None
                    for k in range(STEPS + 1):
                        if xc[k] is not None:
                            x = x + xc[k] * values[k]
                        term = rc[k] * values[k]
                        r = term if r is None else r + term
                    sol[place] = x
                    res[place] = r
        for copy in copies(step):
            copy.start()
        return carry

    lax.fori_loop(0, steps, step_body, 0)

    def wait_body(step, carry):
        for copy in copies(step):
            copy.wait()
        return carry

    lax.fori_loop(0, steps, wait_body, 0)


def all_sum(rows):
    parts = lax.all_to_all(rows[:, None, :], ("gx", "gy"), 0, 0)
    return parts[:, 0, :]


def fix(scale, t, halo, x_depth=(), y_depth=(), extra=()):
    t, *faces = kernel(
        functools.partial(fix_body, scale),
        [f32(*t.shape)] + face_shapes(t, *x_depth)[:2] + face_shapes(t, *y_depth)[2:],
        t,
        *halo,
        *extra,
        alias={0: 0},
    )
    return t, faces


def shards(right_side, guess, diagonal):
    devices = lax.axis_size("gx") * lax.axis_size("gy")
    size, block = guess.size, guess.shape
    strip = pltpu.VMEM((block[0], SUB, block[2]), jnp.float32)
    source = pltpu.with_memory_space_constraint(guess, pltpu.HBM)
    shapes = face_shapes(guess)
    faces = kernel(
        x_faces_body,
        shapes[:2],
        source,
        specs=[hbm],
        scratch=[pltpu.SemaphoreType.DMA((2,))],
        flops=100000 * size,
    ) + kernel(
        y_faces_body,
        shapes[2:],
        source,
        specs=[hbm],
        scratch=[strip, strip, pltpu.SemaphoreType.DMA((2,))],
        flops=1000 * size,
    )
    guess, right_side, diagonal = (
        pltpu.with_memory_space_constraint(a, pltpu.VMEM)
        for a in (guess, right_side, diagonal)
    )
    halo = exchange(faces)
    (t,) = kernel(
        first_body, [f32(*block)], guess, right_side, diagonal, flops=20 * size
    )
    t, faces = fix(1.0, t, halo)
    basis, sums, halos, beyond = [t], [], [], []
    for k in range(STEPS - 1):
        halos.append(exchange(faces))
        given = [basis[k], diagonal] if k == 0 else [basis[k], basis[k - 1], diagonal]
        t, s = kernel(
            functools.partial(next_body, k),
            [f32(*block), f32(1 if k == 0 else 2, SUB, LANE)],
            *given,
            *(beyond if k == 1 else ()),
            flops=24 * size,
        )
        sums.append(s)
        basis.append(t)
        if k < STEPS - 2:
            scale = -1.0 / half_range if k == 0 else -2.0 / half_range
            if k == 0:
                edge = kernel(
                    diagonal_x_body, shapes[:2], diagonal, s, *halos[0][2:]
                )
                beyond = exchange(edge, (0, 1))
                depths, extra = ((), (2,)), (diagonal,)
            else:
                depths, extra = ((2,), (2,)), ()
            basis[-1], faces = fix(scale, t, halos[k], *depths, extra=extra)
    corner = kernel(corner_body, [f32(SUB, block[2])] * 2, *halos[-1][2:], s)
    corners = exchange(corner, (0, 1))
    t4, s = kernel(
        ahead_body,
        [f32(*block), f32(4, SUB, LANE)],
        basis[3],
        basis[2],
        diagonal,
        flops=12 * size,
    )
    basis[3], t4, rows = kernel(
        close_body,
        [f32(*block), f32(*block), f32(devices, LANE)],
        basis[3],
        t4,
        basis[2],
        diagonal,
        *halos[-1],
        *faces[2:],
        *corners,
        *halos[-2],
        *beyond,
        *sums,
        s,
        alias={0: 0, 1: 1},
        scratch=[
            pltpu.VMEM((2, block[1], block[2]), jnp.float32),
            pltpu.VMEM((2, block[0], block[2]), jnp.float32),
        ],
    )
    return kernel(
        final_body,
        [f32(*block), f32(*block)],
        all_sum(rows),
        guess,
        *basis,
        t4,
        out_specs=[hbm] * 2,
        scratch=[
            pltpu.VMEM(block, jnp.float32),
            pltpu.VMEM(block, jnp.float32),
            pltpu.SemaphoreType.DMA((2, block[0] // CHUNK)),
        ],
    )


def solution(mesh):
    return jax.shard_map(
        shards,
        mesh=mesh,
        in_specs=(P("gx", "gy", None),) * 3,
        out_specs=(P("gx", "gy", None),) * 2,
        check_vma=False,
    )
```

```python
import functools

import jax
import jax.numpy as jnp
from jax import lax
from jax.experimental import pallas as pl
from jax.experimental.pallas import tpu as pltpu
from jax.sharding import PartitionSpec as P

STEPS = 4
SUB, LANE = 8, 128
center_shift = 6.25
half_range = 6.25
VMEM_LIMIT = 40 * 1024 * 1024

vmem = pl.BlockSpec(memory_space=pltpu.VMEM)
hbm = pl.BlockSpec(memory_space=pltpu.HBM)


def f32(*shape):
    return jax.ShapeDtypeStruct(shape, jnp.float32)


def kernel(body, outs, *args, specs=None, out_specs=None, scratch=(), alias=None, flops=0):
    size = sum(a.size * 4 for a in args) + sum(o.size * 4 for o in outs)
    return pl.pallas_call(
        body,
        out_shape=outs,
        in_specs=specs or [vmem] * len(args),
        out_specs=out_specs or [vmem] * len(outs),
        scratch_shapes=list(scratch),
        input_output_aliases=alias or {},
        compiler_params=pltpu.CompilerParams(vmem_limit_bytes=VMEM_LIMIT),
        cost_estimate=pl.CostEstimate(
            flops=flops, bytes_accessed=size, transcendentals=0
        ),
    )(*args)


def tree(values):
    while len(values) > 1:
        pairs = [a + b for a, b in zip(values[0::2], values[1::2])]
        values = pairs + ([values[-1]] if len(values) % 2 else [])
    return values[0]


def tiles(shape):
    return shape[1] // SUB, shape[2] // LANE


def layer(t_ref, i, below, above, emit, carry):
    rows, cols = tiles(t_ref.shape)
    sub = lax.broadcasted_iota(jnp.int32, (SUB, LANE), 0)
    lane = lax.broadcasted_iota(jnp.int32, (SUB, LANE), 1)
    first_sub, last_sub = sub == 0, sub == SUB - 1
    first_lane, last_lane = lane == 0, lane == LANE - 1

    def load(j, c, di=0):
        return t_ref[i + di, pl.ds(j * SUB, SUB), pl.ds(c * LANE, LANE)]

    zero = jnp.zeros((SUB, LANE), jnp.float32)
    now = [load(0, c) for c in range(cols)]
    fromlow = [zero] * cols
    for j in range(rows):
        after = [load(j + 1, c) for c in range(cols)] if j + 1 < rows else None
        right = [pltpu.roll(v, 1, 1) for v in now]
        left = [pltpu.roll(v, LANE - 1, 1) for v in now]
        down = [pltpu.roll(v, 1, 0) for v in now]
        for c in range(cols):
            up = pltpu.roll(now[c], SUB - 1, 0)
            nextup = pltpu.roll(after[c], SUB - 1, 0) if after is not None else zero
            s = jnp.where(first_sub, fromlow[c], down[c])
            s = s + jnp.where(last_sub, nextup, up)
            s = s + jnp.where(first_lane, right[c - 1] if c > 0 else zero, right[c])
            s = s + jnp.where(last_lane, left[c + 1] if c + 1 < cols else zero, left[c])
            if below:
                s = s + load(j, c, -1)
            if above:
                s = s + load(j, c, 1)
            carry = emit(i, j, c, now[c], s, carry)
        fromlow = down
        now = after
    return carry


def sweep(t_ref, emit, carry):
    nx = t_ref.shape[0]
    carry = layer(t_ref, 0, False, True, emit, carry)
    carry = lax.fori_loop(
        1, nx - 1, lambda i, a: layer(t_ref, i, True, True, emit, a), carry
    )
    return layer(t_ref, nx - 1, True, False, emit, carry)


def at(j, c):
    return pl.ds(j * SUB, SUB), pl.ds(c * LANE, LANE)


def swaps(nx, ny):
    def pairs(partner):
        return [
            (i * ny + j, x * ny + y)
            for i in range(nx)
            for j in range(ny)
            for x, y in [partner(i, j)]
        ]

    def far(i):
        return i + 1 if i % 2 else i - 1

    return (
        pairs(lambda i, j: (far(i), j) if 0 < i < nx - 1 else (i, j ^ 1)),
        pairs(lambda i, j: (i ^ 1, j)),
        pairs(lambda i, j: (i, far(j)) if 0 < j < ny - 1 else (i, ny - 1 - j)),
        pairs(lambda i, j: (i, j ^ 1)),
    )


def side(axis):
    index, count = lax.axis_index(axis), lax.axis_size(axis)
    odd = lax.rem(index, 2) == 1
    ends = jnp.logical_or(index == 0, index == count - 1)
    return odd, jnp.where(ends, 0.0, 1.0).astype(jnp.float32)


def exchange(faces, which=range(4)):
    perms = swaps(lax.axis_size("gx"), lax.axis_size("gy"))
    return [lax.ppermute(f, ("gx", "gy"), perms[n]) for f, n in zip(faces, which)]


def face_shapes(t, *depth):
    nx, ny, nz = t.shape
    return [f32(*depth, ny, nz)] * 2 + [f32(*depth, nx, nz)] * 2


def x_faces_body(field, far_x, near_x, sems):
    nx = field.shape[0]
    odd_x, _ = side("gx")
    near_layer = jnp.where(odd_x, 0, nx - 1)
    copies = [
        pltpu.make_async_copy(field.at[nx - 1 - near_layer], far_x, sems.at[0]),
        pltpu.make_async_copy(field.at[near_layer], near_x, sems.at[1]),
    ]
    for copy in copies:
        copy.start()
    for copy in copies:
        copy.wait()


def y_faces_body(field, far_y, near_y, low, high, sems):
    nx, ny, _ = field.shape
    odd_y, _ = side("gy")
    copies = [
        pltpu.make_async_copy(field.at[:, pl.ds(0, SUB)], low, sems.at[0]),
        pltpu.make_async_copy(field.at[:, pl.ds(ny - SUB, SUB)], high, sems.at[1]),
    ]
    for copy in copies:
        copy.start()
    for copy in copies:
        copy.wait()
    for i in range(nx):
        first, last = low[i, 0:1, :], high[i, SUB - 1 : SUB, :]
        near_y[i : i + 1, :] = jnp.where(odd_y, first, last)
        far_y[i : i + 1, :] = jnp.where(odd_y, last, first)


def first_body(guess, right_side, diagonal, out):
    def emit(i, j, c, mid, beside, carry):
        place = (i, *at(j, c))
        applied = (6.0 + diagonal[place]) * mid - beside
        out[place] = right_side[place] - applied
        return carry

    sweep(guess, emit, 0)


def next_body(index, *refs):
    if index == 0:
        current, diagonal = refs[:2]
    else:
        current, previous, diagonal = refs[:3]
    out, sums = refs[-2:]
    scale = 1.0 / half_range if index == 0 else 2.0 / half_range
    zero = jnp.zeros((SUB, LANE), jnp.float32)
    count = sums.shape[0]

    def emit(i, j, c, mid, beside, carry):
        place = (i, *at(j, c))
        d = diagonal[place]
        value = scale * ((d + (6.0 - center_shift)) * mid - beside)
        added = [mid * mid]
        if index > 0:
            before = previous[place]
            value = value - before
            added.append(mid * before)
        out[place] = value
        return tuple(a + b for a, b in zip(carry, added))

    total = sweep(current, emit, (zero,) * count)
    for n in range(count):
        sums[n] = total[n]


def add_edges(scale, t, halo):
    far_x, near_x, far_y, near_y = halo
    nx, ny, _ = t.shape
    rows, cols = tiles(t.shape)
    sub = lax.broadcasted_iota(jnp.int32, (SUB, LANE), 0)
    odd_x, has_x = side("gx")
    odd_y, has_y = side("gy")
    near_layer = jnp.where(odd_x, 0, nx - 1)
    far_scale_x, far_scale_y = scale * has_x, scale * has_y

    for i, layer, factor, n in (
        (near_layer, near_x, scale, 0),
        (nx - 1 - near_layer, far_x, far_scale_x, 1),
    ):
        for j in range(rows):
            places = [(i, *at(j, c)) for c in range(cols)]
            olds = [t[place] for place in places]
            news = [old + factor * layer[at(j, c)] for c, old in enumerate(olds)]
            for c in range(cols):
                t[places[c]] = news[c]

    low_scale = jnp.where(odd_y, scale, far_scale_y)
    high_scale = jnp.where(odd_y, far_scale_y, scale)
    for i in range(nx):
        places, olds, news = [], [], []
        for c in range(cols):
            lanes = pl.ds(c * LANE, LANE)
            near, far = near_y[pl.ds(i, 1), lanes], far_y[pl.ds(i, 1), lanes]
            low = low_scale * jnp.where(odd_y, near, far)
            high = high_scale * jnp.where(odd_y, far, near)
            for j, row, value in ((0, 0, low), (rows - 1, SUB - 1, high)):
                place = (i, *at(j, c))
                old = t[place]
                places.append(place)
                olds.append(old)
                news.append(old + jnp.where(sub == row, value, 0.0))
        for place, new in zip(places, news):
            t[place] = new


def fix_body(scale, rows_first, t_in, far_x, near_x, far_y, near_y, *refs):
    t, *faces = refs[-5:]
    ffx, nfx, ffy, nfy = faces[2:] + faces[:2] if rows_first else faces
    add_edges(scale, t, (far_x, near_x, first_of(far_y), first_of(near_y)))
    if len(refs) == 6:
        write_faces(t, ffx, nfx, ffy.at[0], nfy.at[0])
        write_rows(refs[0], 0, ffy.at[1], nfy.at[1])
    else:
        write_faces(t, ffx, nfx, ffy, nfy)


def first_of(ref):
    return ref.at[0] if len(ref.shape) == 3 else ref


def write_rows(t, n, far_row, near_row):
    nx, ny, _ = t.shape
    odd_y, _ = side("gy")
    for i in range(nx):
        first, last = t[i, n : n + 1, :], t[i, ny - 1 - n : ny - n, :]
        near_row[i : i + 1, :] = jnp.where(odd_y, first, last)
        far_row[i : i + 1, :] = jnp.where(odd_y, last, first)


def write_faces(t, ffx, nfx, ffy, nfy):
    nx = t.shape[0]
    odd_x, _ = side("gx")
    for n in range(1 if len(ffx.shape) == 2 else ffx.shape[0]):
        views = [r.at[n] if len(r.shape) == 3 else r for r in (ffx, nfx, ffy, nfy)]
        far_layer, near_layer, far_row, near_row = views
        place = jnp.where(odd_x, n, nx - 1 - n)
        near_layer[...] = t[place]
        far_layer[...] = t[nx - 1 - place]
        write_rows(t, n, far_row, near_row)


def diagonal_x_body(diagonal, *refs):
    far, near = refs[-2:]
    nx = diagonal.shape[0]
    odd_x, _ = side("gx")
    place = jnp.where(odd_x, 0, nx - 1)
    near[...] = diagonal[place]
    far[...] = diagonal[nx - 1 - place]


def corner_body(far_y, near_y, far, near):
    nx = far_y.shape[1]
    odd_x, _ = side("gx")
    near[...] = jnp.zeros_like(near)
    far[...] = jnp.zeros_like(far)
    for n, line in enumerate((near_y, far_y)):
        first, last = line[0, 0:1, :], line[0, nx - 1 : nx, :]
        near[n : n + 1, :] = jnp.where(odd_x, first, last)
        far[n : n + 1, :] = jnp.where(odd_x, last, first)


def plane(tile, shape, low, high, others, emit, carry, wanted):
    rows, cols = shape
    sub = lax.broadcasted_iota(jnp.int32, (SUB, LANE), 0)
    lane = lax.broadcasted_iota(jnp.int32, (SUB, LANE), 1)
    zero = jnp.zeros((SUB, LANE), jnp.float32)
    for j in wanted:
        mids = [tile(j, c) for c in range(cols)]
        right = [pltpu.roll(v, 1, 1) for v in mids]
        left = [pltpu.roll(v, LANE - 1, 1) for v in mids]
        for c, mid in enumerate(mids):
            before = pltpu.roll(tile(j - 1, c), 1, 0) if j > 0 else low(c)
            after = pltpu.roll(tile(j + 1, c), SUB - 1, 0) if j + 1 < rows else high(c)
            terms = [
                jnp.where(sub == 0, before, pltpu.roll(mid, 1, 0)),
                jnp.where(sub == SUB - 1, after, pltpu.roll(mid, SUB - 1, 0)),
                jnp.where(lane == 0, right[c - 1] if c > 0 else zero, right[c]),
                jnp.where(
                    lane == LANE - 1, left[c + 1] if c + 1 < cols else zero, left[c]
                ),
            ]
            carry = emit(j, c, mid, tree(terms + others(j, c)), carry)
    return carry


def advance(mid, beside, diagonal, before):
    scale = 2.0 / half_range
    return scale * ((diagonal + (6.0 - center_shift)) * mid - beside) - before


def products(mid, before, value, carry):
    added = (mid * before, mid * mid, mid * value, value * value)
    return tuple(a + b for a, b in zip(carry, added))


def ahead_body(current, previous, diagonal, out, sums):
    nx = current.shape[0]
    rows, cols = tiles(current.shape)

    def one(i, carry):
        def emit(j, c, mid, beside, carry):
            place = (i, *at(j, c))
            before = previous[place]
            value = advance(mid, beside, diagonal[place], before)
            out[place] = value
            return products(mid, before, value, carry)

        return plane(
            lambda j, c: current[(i, *at(j, c))],
            (rows, cols),
            None,
            None,
            lambda j, c: [current[(i - 1, *at(j, c))], current[(i + 1, *at(j, c))]],
            emit,
            carry,
            range(1, rows - 1),
        )

    zero = jnp.zeros((SUB, LANE), jnp.float32)
    total = lax.fori_loop(2, nx - 2, one, (zero,) * 4)
    for n in range(4):
        sums[n] = total[n]


def close_body(*refs):
    (t3_in, t4_in, previous, diagonal), refs = refs[:4], refs[4:]
    (far_y, near_y, far_x, near_x, own_far, own_near), refs = refs[:6], refs[6:]
    (far_c, near_c), older, beyond, refs = refs[:2], refs[2:6], refs[6:8], refs[8:]
    beyond = [*beyond, older[2].at[1], older[3].at[1]]
    older = [*older[:2], older[2].at[0], older[3].at[0]]
    s0, s1, s2, s3, t3, t4, out, hx, hy = refs
    nx, ny, _ = t3.shape
    rows, cols = tiles(t3.shape)
    odd_x, has_x = side("gx")
    odd_y, has_y = side("gy")
    near_layer = jnp.where(odd_x, 0, nx - 1)

    def lanes(c):
        return pl.ds(c * LANE, LANE)

    def spread(line):
        return jnp.broadcast_to(line, (SUB, LANE))

    def outer(target, halo, inner, edges, odd, factor, old, diag):
        near_edge, far_edge = edges

        def low(c):
            return spread(jnp.where(odd, near_edge(c), far_edge(c)))

        def high(c):
            return spread(jnp.where(odd, far_edge(c), near_edge(c)))

        def emit(j, c, mid, beside, carry):
            value = advance(mid, beside, diag[at(j, c)], old[at(j, c)])
            target[at(j, c)] = value if factor is None else factor * value
            return carry

        shape = (halo.shape[1] // SUB, cols)
        plane(
            lambda j, c: halo[(0, *at(j, c))],
            shape,
            low,
            high,
            lambda j, c: [halo[(1, *at(j, c))], inner(j, c)],
            emit,
            0,
            range(shape[0]),
        )

    for n, (halo, corner, layer_index, factor, old, diag) in enumerate(
        (
            (near_x, near_c, near_layer, None, older[1], beyond[1]),
            (far_x, far_c, nx - 1 - near_layer, has_x, older[0], beyond[0]),
        )
    ):
        edges = (
            lambda c, corner=corner: corner[0:1, lanes(c)],
            lambda c, corner=corner: has_y * corner[1:2, lanes(c)],
        )

        def inner(j, c, place=layer_index):
            return previous[(place, *at(j, c))]

        outer(hx.at[n], halo, inner, edges, odd_y, factor, old, diag)
    for n, (halo, own, factor, old, diag) in enumerate(
        (
            (near_y, own_near, None, older[3], beyond[3]),
            (far_y, own_far, has_y, older[2], beyond[2]),
        )
    ):
        edges = (
            lambda c, n=n: near_c[n : n + 1, lanes(c)],
            lambda c, n=n: has_x * far_c[n : n + 1, lanes(c)],
        )

        def inner(j, c, own=own):
            return own[(0, *at(j, c))]

        outer(hy.at[n], halo, inner, edges, odd_x, factor, old, diag)

    scale = -2.0 / half_range
    add_edges(scale, t3, [r.at[0] for r in (far_x, near_x, far_y, near_y)])
    low_x, low_y = jnp.where(odd_x, 0, 1), jnp.where(odd_y, 0, 1)

    def one(i, below, above, wanted, carry):
        def others(j, c):
            return [
                t3[(i - 1, *at(j, c))] if below else hx[(low_x, *at(j, c))],
                t3[(i + 1, *at(j, c))] if above else hx[(1 - low_x, *at(j, c))],
            ]

        def emit(j, c, mid, beside, carry):
            place = (i, *at(j, c))
            before = previous[place]
            value = advance(mid, beside, diagonal[place], before)
            t4[place] = value
            return products(mid, before, value, carry)

        return plane(
            lambda j, c: t3[(i, *at(j, c))],
            (rows, cols),
            lambda c: spread(hy[low_y, pl.ds(i, 1), lanes(c)]),
            lambda c: spread(hy[1 - low_y, pl.ds(i, 1), lanes(c)]),
            others,
            emit,
            carry,
            wanted,
        )

    sums = tuple(s3[n] for n in range(4))
    sums = one(0, False, True, range(rows), sums)
    sums = one(1, True, True, range(rows), sums)
    for i in range(2, nx - 2):
        sums = one(i, True, True, (0, rows - 1), sums)
    sums = one(nx - 2, True, True, range(rows), sums)
    sums = one(nx - 1, True, False, range(rows), sums)
    parts = [s0[0], s1[1], s1[0], s2[1], s2[0], *sums]
    lane = lax.broadcasted_iota(jnp.int32, (SUB, LANE), 1)
    packed = jnp.zeros((SUB, LANE), jnp.float32)
    for n, part in enumerate(parts):
        total = jnp.sum(part, axis=1, keepdims=True)
        packed = jnp.where(lane == n, total, packed)
    packed = jnp.sum(packed, axis=0, keepdims=True)
    out[...] = jnp.broadcast_to(packed, out.shape)


def coefficients(q):
    depth = STEPS
    moment = [None] * (2 * depth + 1)
    moment[0], moment[1] = q[0], q[1]
    for n in range(2, 2 * depth + 1):
        moment[n] = 2.0 * q[n] - moment[n % 2]
    gram = [
        [
            q[i + j] if abs(i - j) < 2 else 0.5 * (moment[i + j] + moment[abs(i - j)])
            for j in range(depth + 1)
        ]
        for i in range(depth + 1)
    ]

    def plus(a, b):
        return b if a is None else a if b is None else a + b

    def times(a, b):
        return None if a is None or b is None else a * b

    def change(v):
        moved = [None] * (depth + 1)
        for k in range(depth):
            if k == 0:
                entries = {0: center_shift, 1: half_range}
            else:
                entries = {
                    k - 1: half_range / 2.0,
                    k: center_shift,
                    k + 1: half_range / 2.0,
                }
            for i, value in entries.items():
                moved[i] = plus(moved[i], times(value, v[k]))
        return moved

    def quad(left, right):
        total = None
        for i in range(depth + 1):
            inner = None
            for j in range(depth + 1):
                inner = plus(inner, times(gram[i][j], right[j]))
            total = plus(total, times(left[i], inner))
        return total

    one = jnp.ones_like(q[0])
    xc = [None] * (depth + 1)
    rc = [one] + [None] * depth
    pc = [one] + [None] * depth
    rr = quad(rc, rc)
    for _ in range(depth):
        moved = change(pc)
        alpha = rr / quad(pc, moved)
        xc = [plus(x, times(alpha, p)) for x, p in zip(xc, pc)]
        rc = [plus(r, times(-alpha, m)) for r, m in zip(rc, moved)]
        following = quad(rc, rc)
        beta = following / rr
        pc = [plus(r, times(beta, p)) for r, p in zip(rc, pc)]
        rr = following
    return xc, rc


CHUNK = 2


def final_body(sums, guess, t0, t1, t2, t3, t4, sol_hbm, res_hbm, sol, res, sems):
    nx = t0.shape[0]
    rows, cols = tiles(t0.shape)
    packed = tree([sums[pl.ds(n * SUB, SUB), :] for n in range(sums.shape[0] // SUB)])
    packed = jnp.sum(packed, axis=0, keepdims=True)
    q = [
        jnp.broadcast_to(packed[:, n : n + 1], (SUB, LANE))
        for n in range(2 * STEPS + 1)
    ]
    xc, rc = coefficients(q)
    basis = [t0, t1, t2, t3, t4]
    steps = nx // CHUNK

    def copies(step):
        block = pl.ds(step * CHUNK, CHUNK)
        return (
            pltpu.make_async_copy(sol.at[block], sol_hbm.at[block], sems.at[0, step]),
            pltpu.make_async_copy(res.at[block], res_hbm.at[block], sems.at[1, step]),
        )

    def step_body(step, carry):
        for u in range(CHUNK):
            i = step * CHUNK + u
            for j in range(rows):
                for c in range(cols):
                    place = (i, *at(j, c))
                    values = [b[place] for b in basis]
                    x, r = guess[place], None
                    for k in range(STEPS + 1):
                        if xc[k] is not None:
                            x = x + xc[k] * values[k]
                        term = rc[k] * values[k]
                        r = term if r is None else r + term
                    sol[place] = x
                    res[place] = r
        for copy in copies(step):
            copy.start()
        return carry

    lax.fori_loop(0, steps, step_body, 0)

    def wait_body(step, carry):
        for copy in copies(step):
            copy.wait()
        return carry

    lax.fori_loop(0, steps, wait_body, 0)


def all_sum(rows):
    parts = lax.all_to_all(rows[:, None, :], ("gx", "gy"), 0, 0)
    return parts[:, 0, :]


def fix(scale, t, halo, x_depth=(), y_depth=(), extra=(), rows_first=False):
    shapes = [face_shapes(t, *x_depth)[:2], face_shapes(t, *y_depth)[2:]]
    if rows_first:
        shapes = shapes[::-1]
    t, *faces = kernel(
        functools.partial(fix_body, scale, rows_first),
        [f32(*t.shape)] + shapes[0] + shapes[1],
        t,
        *halo,
        *extra,
        alias={0: 0},
    )
    return t, faces[2:] + faces[:2] if rows_first else faces


def shards(right_side, guess, diagonal):
    devices = lax.axis_size("gx") * lax.axis_size("gy")
    size, block = guess.size, guess.shape
    strip = pltpu.VMEM((block[0], SUB, block[2]), jnp.float32)
    source = pltpu.with_memory_space_constraint(guess, pltpu.HBM)
    shapes = face_shapes(guess)
    faces = kernel(
        x_faces_body,
        shapes[:2],
        source,
        specs=[hbm],
        scratch=[pltpu.SemaphoreType.DMA((2,))],
        flops=100000 * size,
    ) + kernel(
        y_faces_body,
        shapes[2:],
        source,
        specs=[hbm],
        scratch=[strip, strip, pltpu.SemaphoreType.DMA((2,))],
        flops=1000 * size,
    )
    guess, right_side, diagonal = (
        pltpu.with_memory_space_constraint(a, pltpu.VMEM)
        for a in (guess, right_side, diagonal)
    )
    halo = exchange(faces)
    (t,) = kernel(
        first_body, [f32(*block)], guess, right_side, diagonal, flops=20 * size
    )
    t, faces = fix(1.0, t, halo)
    basis, sums, halos, beyond = [t], [], [], []
    for k in range(STEPS - 1):
        halos.append(exchange(faces))
        given = [basis[k], diagonal] if k == 0 else [basis[k], basis[k - 1], diagonal]
        t, s = kernel(
            functools.partial(next_body, k),
            [f32(*block), f32(1 if k == 0 else 2, SUB, LANE)],
            *given,
            *(beyond if k == 1 else ()),
            flops=24 * size,
        )
        sums.append(s)
        basis.append(t)
        if k < STEPS - 2:
            scale = -1.0 / half_range if k == 0 else -2.0 / half_range
            if k == 0:
                edge = kernel(
                    diagonal_x_body, shapes[:2], diagonal, s, *halos[0][2:]
                )
                beyond = exchange(edge, (0, 1))
                depths, extra = ((), (2,)), (diagonal,)
            else:
                depths, extra = ((2,), (2,)), ()
            basis[-1], faces = fix(
                scale, t, halos[k], *depths, extra=extra, rows_first=k == 1
            )
    corner = kernel(corner_body, [f32(SUB, block[2])] * 2, *halos[-1][2:])
    corners = exchange(corner, (0, 1))
    t4, s = kernel(
        ahead_body,
        [f32(*block), f32(4, SUB, LANE)],
        basis[3],
        basis[2],
        diagonal,
        flops=12 * size,
    )
    basis[3], t4, rows = kernel(
        close_body,
        [f32(*block), f32(*block), f32(devices, LANE)],
        basis[3],
        t4,
        basis[2],
        diagonal,
        *halos[-1][2:],
        *halos[-1][:2],
        *faces[2:],
        *corners,
        *halos[-2],
        *beyond,
        *sums,
        s,
        alias={0: 0, 1: 1},
        scratch=[
            pltpu.VMEM((2, block[1], block[2]), jnp.float32),
            pltpu.VMEM((2, block[0], block[2]), jnp.float32),
        ],
    )
    return kernel(
        final_body,
        [f32(*block), f32(*block)],
        all_sum(rows),
        guess,
        *basis,
        t4,
        out_specs=[hbm] * 2,
        scratch=[
            pltpu.VMEM(block, jnp.float32),
            pltpu.VMEM(block, jnp.float32),
            pltpu.SemaphoreType.DMA((2, block[0] // CHUNK)),
        ],
    )


def solution(mesh):
    return jax.shard_map(
        shards,
        mesh=mesh,
        in_specs=(P("gx", "gy", None),) * 3,
        out_specs=(P("gx", "gy", None),) * 2,
        check_vma=False,
    )
```
